32 devices in a mesh: dp: 4 (over y, x), ctx: 4 (over z), tp: 2 (over core).
Axes of the slice: x: 2, y: 2, z: 4, core: 2. Of those that a mesh axis runs over, the one named last changes fastest.
Arguments:
- block_input: bfloat16 [4, 1536, 2048], P('dp', 'ctx'), may hold values from -6 to 6
- cotangent: bfloat16 [4, 1536, 2048], P('dp', 'ctx'), may hold values from -6 to 6
- segment_ids: int32 [4, 1536], P('dp', 'ctx'), may hold values from 0 to 1535, as said below
- positions: int32 [4, 1536], P('dp', 'ctx'), may hold values from 0 to 1535, as said below
- norm_gain: bfloat16 [2048], replicated, may hold values from 0.099609375 to 1.8984375
- norm_bias: bfloat16 [2048], replicated, may hold values from -1.75 to 1.75
- w_qkv: bfloat16 [3, 2048, 2048], P(None, ('dp', 'ctx'), 'tp'), may hold values from -0.125 to 0.125
- qkv_bias: bfloat16 [3, 2048], P(None, 'tp'), may hold values from -3 to 3
- w_dense: bfloat16 [2048, 2048], P('tp', ('dp', 'ctx')), may hold values from -0.5 to 0.5
- w_fc1: bfloat16 [2048, 8192], P(('dp', 'ctx'), 'tp'), may hold values from -0.125 to 0.125
- fc1_bias: bfloat16 [8192], P('tp'), may hold values from -3 to 3
- w_fc2: bfloat16 [8192, 2048], P('tp', ('dp', 'ctx')), may hold values from -0.0625 to 0.0625
- out_bias: bfloat16 [2048], replicated, may hold values from -3 to 3
Outputs:
- output: bfloat16 [4, 1536, 2048], P('dp', 'ctx')
- grad_input: bfloat16 [4, 1536, 2048], P('dp', 'ctx')
- grad_norm_gain: float32 [2048], replicated
- grad_norm_bias: float32 [2048], replicated
- grad_w_qkv: float32 [3, 2048, 2048], P(None, ('dp', 'ctx'), 'tp')
- grad_qkv_bias: float32 [3, 2048], P(None, 'tp')
- grad_w_dense: float32 [2048, 2048], P('tp', ('dp', 'ctx'))
- grad_w_fc1: float32 [2048, 8192], P(('dp', 'ctx'), 'tp')
- grad_fc1_bias: float32 [8192], P('tp')
- grad_w_fc2: float32 [8192, 2048], P('tp', ('dp', 'ctx'))
- grad_out_bias: float32 [2048], replicated
The draws below stay inside these ranges and needn't reach their ends.
Inputs may be any that keep to these rules, and one draw needn't show every extreme that they name: `segment_ids`: A document's id is the place of its first token in the sequence, so ids never fall along a sequence; the last token of every sequence is a document of its own. Every sequence holds one spanning document that starts within its first 384 tokens and ends within its last 385 tokens; before and after it, documents start at random places with mean spacing 400 and no least length. Within a document positions rise by one from token to token; a document's first position is at least 0, and except in the spanning document at most the place of its first token.
All inputs are finite; a program needn't handle non-finite values.
Results may differ from the reference program's by a relative error of at most 0.014.
Values may be sent and summed in bfloat16 or wider, within the bound.
A program may use at most 320 MiB of HBM per device.

```python
import math
import jax
import jax.numpy as jnp
from jax import lax

D = 2048
HEADS = 32
HD = 64
ROT = 32
FF = 8192
SEQ_DEV = 384
DOC_MEAN = 400
SEQS = 4
LEN = 1536


def document_layout(key):
    first_key, last_key, break_key = jax.random.split(key, 3)
    place_index = jnp.arange(LEN, dtype=jnp.int32)[None, :]
    long_start = jax.random.randint(first_key, (SEQS, 1), 1, SEQ_DEV)
    finish = jax.random.randint(last_key, (SEQS, 1), LEN - SEQ_DEV, LEN - 1)
    breaks = jax.random.randint(break_key, (SEQS, LEN), 0, DOC_MEAN) == 0
    inside = (place_index > long_start) & (place_index <= finish)
    starts = (breaks & ~inside | (place_index == long_start) | (place_index == finish + 1) | (place_index == LEN - 1)) & (place_index > 0)
    opening = lax.cummax(jnp.where(starts | (place_index == 0), place_index, 0), axis=1)
    return (opening, place_index, long_start, finish)


def draw_segment_ids(key, part):
    opening, place_index, long_start, finish = document_layout(key)
    return opening.astype(jnp.int32)


def draw_positions(key, part):
    opening, place_index, long_start, finish = document_layout(key)
    key = jax.random.fold_in(key, 12)
    raw = jax.random.randint(key, (SEQS, LEN), 0, 256)
    offsets = jnp.take_along_axis(raw, opening, axis=1) % (jnp.minimum(opening, 255) + 1)
    offsets = jnp.where(opening == long_start, long_start + LEN - 1 - finish, offsets)
    return (place_index - opening + offsets).astype(jnp.int32)


def levels(key, shape, cuts, low, top_value):
    gain = 1.0
    for dim, shards_of in cuts:
        heights = jax.random.uniform(jax.random.fold_in(jax.random.fold_in(key, 6), dim), (shards_of,), jnp.float32, low / len(cuts), top_value / len(cuts))
        gain = gain * jnp.repeat(jnp.exp(heights), shape[dim] // shards_of).reshape((-1,) + (1,) * (len(shape) - 1 - dim))
    return gain


def scatter_about(key, dims, width, limit, pieces=(), kind=jnp.bfloat16):
    factor_of = levels(key, dims, pieces, -0.22, 0.18) if pieces else 1.0
    values = jax.random.normal(key, dims, jnp.float32) * width * factor_of
    return jnp.minimum(jnp.maximum(values, -limit), limit).astype(kind)


def setup_inputs(seed: int = 0) -> dict:
    splits = jax.random.split(jax.random.key(seed), 14)
    block_input = scatter_about(splits[0], (SEQS, LEN, D), 1.0, 6.0, ((0, 4), (1, 4)))
    cotangent = scatter_about(splits[1], (SEQS, LEN, D), 1.0, 6.0, ((0, 4), (1, 4)))
    segment_ids = draw_segment_ids(jax.random.fold_in(splits[13], 71), 0)
    positions = draw_positions(jax.random.fold_in(splits[13], 71), 0)
    norm_gain = jnp.clip(1.0 + 0.18 * jax.random.normal(splits[4], (D,), jnp.float32), 0.099609375, 1.8984375).astype(jnp.bfloat16)
    norm_bias = scatter_about(splits[5], (D,), 0.3, 1.75)
    w_qkv = scatter_about(splits[6], (3, D, D), D ** -0.5, 0.125, ((1, 16), (2, 2)))
    qkv_bias = scatter_about(splits[7], (3, D), 0.5, 3.0, ((1, 2),))
    w_dense = scatter_about(splits[8], (D, D), (D // 16) ** -0.5, 0.5, ((0, 2), (1, 16)))
    w_fc1 = scatter_about(splits[9], (D, FF), D ** -0.5, 0.125, ((0, 16), (1, 2)))
    fc1_bias = scatter_about(splits[10], (FF,), 0.5, 3.0, ((0, 2),))
    w_fc2 = scatter_about(splits[11], (FF, D), FF ** -0.5, 0.0625, ((0, 2), (1, 16)))
    out_bias = scatter_about(splits[12], (D,), 0.5, 3.0)
    return dict(block_input=block_input, cotangent=cotangent, segment_ids=segment_ids, positions=positions, norm_gain=norm_gain, norm_bias=norm_bias, w_qkv=w_qkv, qkv_bias=qkv_bias, w_dense=w_dense, w_fc1=w_fc1, fc1_bias=fc1_bias, w_fc2=w_fc2, out_bias=out_bias)


epsilon = 1e-05
highest = lax.Precision.HIGHEST

@jax.custom_vjp
def low(v):
    return lax.optimization_barrier(v.astype(jnp.bfloat16)).astype(jnp.float32)

@jax.custom_vjp
def low_back(v):
    return v

def low_keep(v):
    return (low(v), None)

def low_pass(kept, grad):
    return (grad,)

def back_keep(v):
    return (v, None)

def back_low(kept, grad):
    return (low(grad),)
low.defvjp(low_keep, low_pass)
low_back.defvjp(back_keep, back_low)

def rotation(places):
    half_rot = ROT // 2
    frequency = 10000.0 ** (-(jnp.arange(half_rot, dtype=jnp.float32) * 2.0 / ROT))
    angles = places.astype(jnp.float32)[:, None] * frequency[None, :]
    return (jnp.cos(angles)[:, None, :], jnp.sin(angles)[:, None, :])

def rotate(tensor, cosine_table, sine_table):
    half_rot = ROT // 2
    first_half = tensor[..., :half_rot]
    second_half = tensor[..., half_rot:ROT]
    return jnp.concatenate([first_half * cosine_table - second_half * sine_table, second_half * cosine_table + first_half * sine_table, tensor[..., ROT:]], -1)

def attend(queries, keys, values, segments):
    length = queries.shape[0]
    span_rows = min(512, length)
    key_index = jnp.arange(length, dtype=jnp.int32)

    def one_block(number):
        first_row = (number * span_rows).astype(jnp.int32)
        query_rows = lax.dynamic_slice_in_dim(queries, first_row, span_rows, 0)
        row_index = lax.dynamic_slice_in_dim(key_index, first_row, span_rows, 0)
        row_segment = lax.dynamic_slice_in_dim(segments, first_row, span_rows, 0)
        scores = low_back(jnp.einsum('qhd,khd->hqk', query_rows, keys, precision=highest) * (1.0 / math.sqrt(HD)))
        allowed = (key_index[None, :] <= row_index[:, None]) & (segments[None, :] == row_segment[:, None])
        scores = jnp.where(allowed[None], scores, -1e+30)
        running_max = lax.optimization_barrier(jnp.max(scores, -1, keepdims=True))
        expo = jnp.exp(scores - running_max)
        prob_block = low(expo / lax.optimization_barrier(jnp.sum(expo, -1, keepdims=True)))
        return jnp.einsum('hqk,khd->qhd', prob_block, values, precision=highest)
    stacked = lax.map(jax.checkpoint(one_block), jnp.arange(length // span_rows, dtype=jnp.int32))
    return stacked.reshape(length, queries.shape[1], queries.shape[2])

def reference(block_input, cotangent, segment_ids, positions, norm_gain, norm_bias, w_qkv, qkv_bias, w_dense, w_fc1, fc1_bias, w_fc2, out_bias):
    params = tuple((a.astype(jnp.float32) for a in (block_input, norm_gain, norm_bias, w_qkv, qkv_bias, w_dense, w_fc1, fc1_bias, w_fc2, out_bias)))

    def forward(inputs, gain_full, shift_full, weight_qkv, bias_qkv, weight_dense, weight_fc1, bias_fc1, weight_fc2, bias_out):

        def one_sequence(batch_items):
            sequence, segments, places = batch_items
            length = sequence.shape[0]
            mean_in = lax.optimization_barrier(jnp.mean(sequence, -1, keepdims=True))
            centred = sequence - mean_in
            x_hat = centred * lax.rsqrt(lax.optimization_barrier(jnp.mean(centred * centred, -1, keepdims=True)) + epsilon)
            normed = low(x_hat * gain_full + shift_full)
            projected = low_back(jnp.einsum('ld,cde->cle', normed, weight_qkv, precision=highest) + bias_qkv[:, None, :])
            cosine_table, sine_table = rotation(places)
            queries = low(rotate(projected[0].reshape(length, HEADS, HD), cosine_table, sine_table))
            keys = low(rotate(projected[1].reshape(length, HEADS, HD), cosine_table, sine_table))
            values = low(projected[2].reshape(length, HEADS, HD))
            mixture = attend(queries, keys, values, segments).reshape(length, D)
            mixture = low_back(low(mixture))
            attn_out = jnp.dot(mixture, weight_dense, precision=highest)
            hidden_pre = low_back(jnp.dot(normed, weight_fc1, precision=highest) + bias_fc1)
            hidden = low(jax.nn.gelu(hidden_pre, approximate=True))
            mlp_out = jnp.dot(hidden, weight_fc2, precision=highest)
            return sequence + attn_out + mlp_out + bias_out
        return lax.map(one_sequence, (inputs, segment_ids, positions))
    result, pullback = jax.vjp(forward, *params)
    gradients = pullback(cotangent.astype(jnp.float32))
    return (result.astype(jnp.bfloat16), gradients[0].astype(jnp.bfloat16), gradients[1], gradients[2], gradients[3], gradients[4], gradients[5], gradients[6], gradients[7], gradients[8], gradients[9])
```

```python
import functools
import math

import jax
import jax.numpy as jnp
from jax import lax
from jax.experimental import pallas as pl
from jax.experimental.pallas import tpu as pltpu
from jax.sharding import PartitionSpec as P

HD = 64
ROT = 32
EPS = 1e-05
MIB = 1 << 20
F32 = jnp.float32
BF16 = jnp.bfloat16


def dot_nn(a, b):
    return lax.dot_general(a, b, (((1,), (0,)), ((), ())), preferred_element_type=F32)


def dot_nt(a, b):
    return lax.dot_general(a, b, (((1,), (1,)), ((), ())), preferred_element_type=F32)


def dot_tn(a, b):
    return lax.dot_general(a, b, (((0,), (0,)), ((), ())), preferred_element_type=F32)


def rotary_tables(places):
    half = ROT // 2
    frequency = 10000.0 ** (-(jnp.arange(half, dtype=F32) * 2.0 / ROT))
    angles = places.astype(F32)[:, None] * frequency[None, :]
    cos, sin = jnp.cos(angles), jnp.sin(angles)
    rows = places.shape[0]
    zero = jnp.zeros((rows, half), F32)
    rest0 = jnp.zeros((rows, HD - ROT), F32)
    rest1 = jnp.ones((rows, HD - ROT), F32)
    keep = jnp.concatenate([cos, cos, rest1] * 2, 1)
    from_right = jnp.concatenate([-sin, zero, rest0] * 2, 1)
    from_left = jnp.concatenate([zero, sin, rest0] * 2, 1)
    return keep, from_right, from_left


def turn(v, keep, from_right, from_left):
    half = ROT // 2
    return v * keep + pltpu.roll(v, 128 - half, 1) * from_right + pltpu.roll(v, half, 1) * from_left


def attention_body(
    block_rows, pq, pk, pv, mg, keep, fr, fl, seg_row, seg_col, mix, gq, gk, gv, q, k, v, dq, dk, dv
):
    rows = pq.shape[0]
    scale = 1.0 / math.sqrt(HD)
    q[...] = (turn(pq[...], keep[...], fr[...], fl[...]).astype(BF16) * scale).astype(BF16)
    k[...] = turn(pk[...], keep[...], fr[...], fl[...]).astype(BF16)
    v[...] = pv[...].astype(BF16)
    dk[...] = jnp.zeros_like(dk)
    dv[...] = jnp.zeros_like(dv)
    first = lax.broadcasted_iota(jnp.int32, (block_rows, 128), 1) < HD
    for i in range(rows // block_rows):
        here = pl.ds(i * block_rows, block_rows)
        seen = pl.ds(0, (i + 1) * block_rows)
        keys, values = k[seen, :], v[seen, :]
        shape = (block_rows, (i + 1) * block_rows)
        row_index = lax.broadcasted_iota(jnp.int32, shape, 0) + i * block_rows
        col_index = lax.broadcasted_iota(jnp.int32, shape, 1)
        allowed = (col_index <= row_index) & (seg_col[here, :] == seg_row[:, seen])
        parts = []
        for sub in range(2):
            mine = first if sub == 0 else ~first
            qi = jnp.where(mine, q[here, :], 0)
            mi = jnp.where(mine, mg[here, :], 0)
            scores = jnp.where(allowed, dot_nt(qi, keys), -1e30)
            top = jnp.max(scores, 1, keepdims=True)
            expo = jnp.exp(scores - top)
            probs = expo * (1.0 / jnp.sum(expo, 1, keepdims=True))
            low = probs.astype(BF16)
            out = dot_nn(low, values)
            prob_grad = dot_nt(mi, values)
            delta = jnp.sum(probs * prob_grad, 1, keepdims=True)
            score_grad = (probs * (prob_grad - delta)).astype(BF16)
            dqi = dot_nn(score_grad, keys) * scale
            dk[seen, :] += dot_tn(score_grad, qi)
            dv[seen, :] += dot_tn(low, mi)
            parts.append((out, dqi))
        mix[here, :] = jnp.where(first, parts[0][0], parts[1][0]).astype(BF16)
        dq[here, :] = jnp.where(first, parts[0][1], parts[1][1])
    gq[...] = turn(dq[...], keep[...], -fr[...], -fl[...]).astype(BF16)
    gk[...] = turn(dk[...], keep[...], -fr[...], -fl[...]).astype(BF16)
    gv[...] = dv[...].astype(BF16)


def attention(pq, pk, pv, mg, places, segments):
    rows, cols = pq.shape
    keep, fr, fl = rotary_tables(places)
    pair = pl.BlockSpec((rows, 128), lambda h: (0, h))
    whole = pl.BlockSpec((rows, 128), lambda h: (0, 0))
    return pl.pallas_call(
        functools.partial(attention_body, 256),
        grid=(cols // 128,),
        in_specs=[pair] * 4
        + [whole] * 3
        + [
            pl.BlockSpec((1, rows), lambda h: (0, 0)),
            pl.BlockSpec((rows, 1), lambda h: (0, 0)),
        ],
        out_specs=[pair] * 4,
        out_shape=[jax.ShapeDtypeStruct((rows, cols), BF16)] * 4,
        scratch_shapes=[pltpu.VMEM((rows, 128), BF16)] * 3 + [pltpu.VMEM((rows, 128), F32)] * 3,
        compiler_params=pltpu.CompilerParams(vmem_limit_bytes=48 * MIB),
    )(pq, pk, pv, mg, keep, fr, fl, segments[None, :], segments[:, None])


def attention_plain(pq, pk, pv, mg, places, segments):
    rows, cols = pq.shape
    heads = cols // HD
    half = ROT // 2
    scale = 1.0 / math.sqrt(HD)
    frequency = 10000.0 ** (-(jnp.arange(half, dtype=F32) * 2.0 / ROT))
    angles = places.astype(F32)[:, None] * frequency[None, :]
    cos, sin = jnp.cos(angles)[:, None, :], jnp.sin(angles)[:, None, :]

    def rotate(t, s):
        t = t.reshape(rows, heads, HD)
        a, b = t[..., :half], t[..., half:ROT]
        return jnp.concatenate([a * cos - b * s, b * cos + a * s, t[..., ROT:]], -1)

    q = rotate(pq, sin).astype(BF16)
    k = rotate(pk, sin).astype(BF16)
    v = pv.astype(BF16).reshape(rows, heads, HD)
    m = mg.reshape(rows, heads, HD)
    span = 256
    index = jnp.arange(rows, dtype=jnp.int32)

    def step(carry, items):
        dk, dv = carry
        qi, mi, row_index, row_seg = items
        scores = jnp.einsum("qhd,khd->hqk", qi, k, preferred_element_type=F32) * scale
        allowed = (index[None, :] <= row_index[:, None]) & (segments[None, :] == row_seg[:, None])
        scores = jnp.where(allowed[None], scores, -1e30)
        expo = jnp.exp(scores - jnp.max(scores, -1, keepdims=True))
        probs = expo / jnp.sum(expo, -1, keepdims=True)
        low = probs.astype(BF16)
        out = jnp.einsum("hqk,khd->qhd", low, v, preferred_element_type=F32).astype(BF16)
        prob_grad = jnp.einsum("qhd,khd->hqk", mi, v, preferred_element_type=F32)
        delta = jnp.sum(probs * prob_grad, -1, keepdims=True)
        score_grad = (probs * (prob_grad - delta)).astype(BF16)
        dq = jnp.einsum("hqk,khd->qhd", score_grad, k, preferred_element_type=F32) * scale
        dk = dk + jnp.einsum("hqk,qhd->khd", score_grad, qi, preferred_element_type=F32) * scale
        dv = dv + jnp.einsum("hqk,qhd->khd", low, mi, preferred_element_type=F32)
        return (dk, dv), (out, dq)

    zero = jnp.zeros((rows, heads, HD), F32)
    cut = lambda t: t.reshape((rows // span, span) + t.shape[1:])
    (dk, dv), (out, dq) = lax.scan(step, (zero, zero), (cut(q), cut(m), cut(index), cut(segments)))
    flat = lambda t: t.reshape(rows, cols)
    return (
        flat(out),
        flat(rotate(dq.reshape(rows, cols), -sin)).astype(BF16),
        flat(rotate(dk.reshape(rows, cols), -sin)).astype(BF16),
        flat(dv).astype(BF16),
    )


def gather_plain(x, g, wsrc, places, segments):
    pieces = lax.all_to_all(wsrc, "ctx", split_axis=1, concat_axis=1, tiled=True)
    weights = lax.all_gather(pieces, "dp", axis=1, tiled=True)
    along = lambda t: lax.all_gather(t, "ctx", axis=0, tiled=True)
    return along(x), along(g), weights, along(places), along(segments)


def scatter_plain(out_part, normed_part, weight_part):
    summed = lambda t: lax.psum(
        lax.psum_scatter(t, "ctx", scatter_dimension=0, tiled=True), "tp"
    ).astype(F32)
    pieces = lax.psum_scatter(weight_part, "dp", scatter_dimension=1, tiled=True)
    pieces = lax.all_to_all(pieces, "ctx", split_axis=1, concat_axis=1, tiled=True)
    return summed(out_part), summed(normed_part), pieces.astype(F32)


def layer_norm(x):
    xf = x.astype(F32)
    mean = jnp.mean(xf, -1, keepdims=True)
    centred = xf - mean
    inv_std = lax.rsqrt(jnp.mean(centred * centred, -1, keepdims=True) + EPS)
    return centred * inv_std, inv_std


def per_device(
    block_input,
    cotangent,
    segment_ids,
    positions,
    norm_gain,
    norm_bias,
    w_qkv,
    qkv_bias,
    w_dense,
    w_fc1,
    fc1_bias,
    w_fc2,
    out_bias,
):
    ways = lax.axis_size("ctx")
    me = lax.axis_index("ctx")
    x, g = block_input[0], cotangent[0]
    rows, width = x.shape
    depth = w_fc1.shape[0]
    cols = w_fc1.shape[1] // ways
    head_cols = w_qkv.shape[2] // ways

    fc1 = w_fc1.reshape(depth, ways, cols).transpose(1, 0, 2)
    fc2 = w_fc2.reshape(ways, cols, depth).transpose(0, 2, 1)
    qkv = w_qkv.reshape(3, depth, ways, head_cols).transpose(2, 1, 0, 3)
    dense = w_dense.reshape(ways, head_cols, depth).transpose(0, 2, 1)
    att = jnp.concatenate([qkv.reshape(ways, depth, 3 * head_cols), dense], -1)
    wsrc = jnp.stack([fc1, fc2, att])

    x_all, g_all, weights, places, segments = gather_plain(
        x, g, wsrc, positions[0], segment_ids[0]
    )
    weights = weights.reshape(3, width, cols)
    w1, w2, wa = weights[0], weights[1], weights[2]
    wp, wd = wa[:, : 3 * head_cols], wa[:, 3 * head_cols :]

    gain, shift = norm_gain.astype(F32), norm_bias.astype(F32)
    x_hat, unused = layer_norm(x_all)
    normed = (x_hat * gain + shift).astype(BF16)

    qkv_shift = lax.dynamic_slice_in_dim(qkv_bias, me * head_cols, head_cols, 1)
    fc1_shift = lax.dynamic_slice_in_dim(fc1_bias, me * cols, cols, 0)
    projected = dot_nn(normed, wp) + qkv_shift.astype(F32).reshape(1, 3 * head_cols)
    mix_grad = dot_nn(g_all, wd).astype(BF16)
    attend = attention if head_cols % 128 == 0 else attention_plain
    mixture, gq, gk, gv = attend(
        projected[:, :head_cols],
        projected[:, head_cols : 2 * head_cols],
        projected[:, 2 * head_cols :],
        mix_grad,
        places,
        segments,
    )
    proj_grad = jnp.concatenate([gq, gk, gv], 1)

    hidden_pre = dot_nn(normed, w1) + fc1_shift.astype(F32)
    hidden, gelu_back = jax.vjp(lambda t: jax.nn.gelu(t, approximate=True), hidden_pre)
    hidden = hidden.astype(BF16)
    hidden_grad = gelu_back(dot_nn(g_all, w2))[0].astype(BF16)

    out_part = (dot_nt(mixture, wd) + dot_nt(hidden, w2)).astype(BF16)
    normed_part = dot_nt(proj_grad, wp) + dot_nt(hidden_grad, w1)
    weight_part = jnp.stack(
        [
            dot_tn(normed, hidden_grad).astype(BF16),
            dot_tn(g_all, hidden).astype(BF16),
            jnp.concatenate([dot_tn(normed, proj_grad), dot_tn(g_all, mixture)], 1).astype(BF16),
        ]
    )
    gain_part = jnp.sum(normed_part * x_hat, 0)
    shift_part = jnp.sum(normed_part, 0)
    qkv_bias_part = jnp.sum(proj_grad.astype(F32), 0).reshape(3, head_cols)
    fc1_bias_part = jnp.sum(hidden_grad.astype(F32), 0)

    branches, normed_grad, weight_grads = scatter_plain(
        out_part, normed_part.astype(BF16), weight_part.reshape(3, -1, depth, cols)
    )

    gf = g.astype(F32)
    output = (x.astype(F32) + branches + out_bias.astype(F32)).astype(BF16)
    own_hat, inv_std = layer_norm(x)
    scaled = normed_grad * gain
    grad_input = gf + inv_std * (
        scaled
        - jnp.mean(scaled, -1, keepdims=True)
        - own_hat * jnp.mean(scaled * own_hat, -1, keepdims=True)
    )
    place = lambda t, whole, axis: lax.dynamic_update_slice_in_dim(
        jnp.zeros(whole, F32), t, me * t.shape[axis], axis
    )
    small = lax.psum(
        (
            place(qkv_bias_part, (3, head_cols * ways), 1),
            place(fc1_bias_part, (cols * ways,), 0),
            jnp.sum(gf, 0),
        ),
        ("dp", "ctx"),
    )
    norm_small = lax.psum((gain_part, shift_part), ("dp", "ctx", "tp"))

    grad_fc1 = weight_grads[0].transpose(1, 0, 2).reshape(depth, ways * cols)
    grad_fc2 = weight_grads[1].transpose(0, 2, 1).reshape(ways * cols, depth)
    grad_att = weight_grads[2].reshape(ways, depth, 4, head_cols)
    grad_qkv = grad_att[:, :, :3].transpose(2, 1, 0, 3).reshape(3, depth, ways * head_cols)
    grad_dense = grad_att[:, :, 3].transpose(0, 2, 1).reshape(ways * head_cols, depth)
    return (
        output[None],
        grad_input.astype(BF16)[None],
        norm_small[0],
        norm_small[1],
        grad_qkv,
        small[0],
        grad_dense,
        grad_fc1,
        small[1],
        grad_fc2,
        small[2],
    )


def solution(mesh):
    placed = (
        P("dp", "ctx", None),
        P("dp", "ctx", None),
        P("dp", "ctx"),
        P("dp", "ctx"),
        P(),
        P(),
        P(None, ("dp", "ctx"), "tp"),
        P(None, "tp"),
        P("tp", ("dp", "ctx")),
        P(("dp", "ctx"), "tp"),
        P("tp"),
        P("tp", ("dp", "ctx")),
        P(),
    )
    return jax.shard_map(
        per_device,
        mesh=mesh,
        in_specs=placed,
        out_specs=(
            P("dp", "ctx", None),
            P("dp", "ctx", None),
            P(),
            P(),
            P(None, ("dp", "ctx"), "tp"),
            P(None, "tp"),
            P("tp", ("dp", "ctx")),
            P(("dp", "ctx"), "tp"),
            P("tp"),
            P("tp", ("dp", "ctx")),
            P(),
        ),
        check_vma=False,
    )
```

```python
import functools
import math

import jax
import jax.numpy as jnp
from jax import lax
from jax.experimental import pallas as pl
from jax.experimental.pallas import tpu as pltpu
from jax.sharding import PartitionSpec as P

HD = 64
ROT = 32
EPS = 1e-05
MIB = 1 << 20
F32 = jnp.float32
BF16 = jnp.bfloat16
MESH = pl.DeviceIdType.MESH


def dot_nn(a, b):
    return lax.dot_general(a, b, (((1,), (0,)), ((), ())), preferred_element_type=F32)


def dot_nt(a, b):
    return lax.dot_general(a, b, (((1,), (1,)), ((), ())), preferred_element_type=F32)


def dot_tn(a, b):
    return lax.dot_general(a, b, (((0,), (0,)), ((), ())), preferred_element_type=F32)


def rotary_tables(places):
    half = ROT // 2
    frequency = 10000.0 ** (-(jnp.arange(half, dtype=F32) * 2.0 / ROT))
    angles = places.astype(F32)[:, None] * frequency[None, :]
    cos, sin = jnp.cos(angles), jnp.sin(angles)
    rows = places.shape[0]
    zero = jnp.zeros((rows, half), F32)
    rest0 = jnp.zeros((rows, HD - ROT), F32)
    rest1 = jnp.ones((rows, HD - ROT), F32)
    keep = jnp.concatenate([cos, cos, rest1] * 2, 1)
    from_right = jnp.concatenate([-sin, zero, rest0] * 2, 1)
    from_left = jnp.concatenate([zero, sin, rest0] * 2, 1)
    return keep, from_right, from_left


def turn(v, keep, from_right, from_left):
    half = ROT // 2
    return v * keep + pltpu.roll(v, 128 - half, 1) * from_right + pltpu.roll(v, half, 1) * from_left


def attention_body(
    block_rows, pq, pk, pv, mg, keep, fr, fl, seg_row, seg_col, mix, gq, gk, gv, q, k, v, dq, dk, dv
):
    rows = pq.shape[0]
    scale = 1.0 / math.sqrt(HD)
    q[...] = (turn(pq[...], keep[...], fr[...], fl[...]).astype(BF16) * scale).astype(BF16)
    k[...] = turn(pk[...], keep[...], fr[...], fl[...]).astype(BF16)
    v[...] = pv[...].astype(BF16)
    dk[...] = jnp.zeros_like(dk)
    dv[...] = jnp.zeros_like(dv)
    first = lax.broadcasted_iota(jnp.int32, (block_rows, 128), 1) < HD
    for i in range(rows // block_rows):
        here = pl.ds(i * block_rows, block_rows)
        seen = pl.ds(0, (i + 1) * block_rows)
        keys, values = k[seen, :], v[seen, :]
        shape = (block_rows, (i + 1) * block_rows)
        row_index = lax.broadcasted_iota(jnp.int32, shape, 0) + i * block_rows
        col_index = lax.broadcasted_iota(jnp.int32, shape, 1)
        allowed = (col_index <= row_index) & (seg_col[here, :] == seg_row[:, seen])
        parts = []
        for sub in range(2):
            mine = first if sub == 0 else ~first
            qi = jnp.where(mine, q[here, :], 0)
            mi = jnp.where(mine, mg[here, :], 0)
            scores = jnp.where(allowed, dot_nt(qi, keys), -1e30)
            top = jnp.max(scores, 1, keepdims=True)
            expo = jnp.exp(scores - top)
            probs = expo * (1.0 / jnp.sum(expo, 1, keepdims=True))
            low = probs.astype(BF16)
            out = dot_nn(low, values)
            prob_grad = dot_nt(mi, values)
            delta = jnp.sum(probs * prob_grad, 1, keepdims=True)
            score_grad = (probs * (prob_grad - delta)).astype(BF16)
            dqi = dot_nn(score_grad, keys) * scale
            dk[seen, :] += dot_tn(score_grad, qi)
            dv[seen, :] += dot_tn(low, mi)
            parts.append((out, dqi))
        mix[here, :] = jnp.where(first, parts[0][0], parts[1][0]).astype(BF16)
        dq[here, :] = jnp.where(first, parts[0][1], parts[1][1])
    gq[...] = turn(dq[...], keep[...], -fr[...], -fl[...]).astype(BF16)
    gk[...] = turn(dk[...], keep[...], -fr[...], -fl[...]).astype(BF16)
    gv[...] = dv[...].astype(BF16)


def attention(pq, pk, pv, mg, places, segments):
    rows, cols = pq.shape
    keep, fr, fl = rotary_tables(places)
    pair = pl.BlockSpec((rows, 128), lambda h: (0, h))
    whole = pl.BlockSpec((rows, 128), lambda h: (0, 0))
    return pl.pallas_call(
        functools.partial(attention_body, 256),
        grid=(cols // 128,),
        in_specs=[pair] * 4
        + [whole] * 3
        + [
            pl.BlockSpec((1, rows), lambda h: (0, 0)),
            pl.BlockSpec((rows, 1), lambda h: (0, 0)),
        ],
        out_specs=[pair] * 4,
        out_shape=[jax.ShapeDtypeStruct((rows, cols), BF16)] * 4,
        scratch_shapes=[pltpu.VMEM((rows, 128), BF16)] * 3 + [pltpu.VMEM((rows, 128), F32)] * 3,
        compiler_params=pltpu.CompilerParams(vmem_limit_bytes=48 * MIB),
    )(pq, pk, pv, mg, keep, fr, fl, segments[None, :], segments[:, None])


def attention_plain(pq, pk, pv, mg, places, segments):
    rows, cols = pq.shape
    heads = cols // HD
    half = ROT // 2
    scale = 1.0 / math.sqrt(HD)
    frequency = 10000.0 ** (-(jnp.arange(half, dtype=F32) * 2.0 / ROT))
    angles = places.astype(F32)[:, None] * frequency[None, :]
    cos, sin = jnp.cos(angles)[:, None, :], jnp.sin(angles)[:, None, :]

    def rotate(t, s):
        t = t.reshape(rows, heads, HD)
        a, b = t[..., :half], t[..., half:ROT]
        return jnp.concatenate([a * cos - b * s, b * cos + a * s, t[..., ROT:]], -1)

    q = rotate(pq, sin).astype(BF16)
    k = rotate(pk, sin).astype(BF16)
    v = pv.astype(BF16).reshape(rows, heads, HD)
    m = mg.reshape(rows, heads, HD)
    span = 256
    index = jnp.arange(rows, dtype=jnp.int32)

    def step(carry, items):
        dk, dv = carry
        qi, mi, row_index, row_seg = items
        scores = jnp.einsum("qhd,khd->hqk", qi, k, preferred_element_type=F32) * scale
        allowed = (index[None, :] <= row_index[:, None]) & (segments[None, :] == row_seg[:, None])
        scores = jnp.where(allowed[None], scores, -1e30)
        expo = jnp.exp(scores - jnp.max(scores, -1, keepdims=True))
        probs = expo / jnp.sum(expo, -1, keepdims=True)
        low = probs.astype(BF16)
        out = jnp.einsum("hqk,khd->qhd", low, v, preferred_element_type=F32).astype(BF16)
        prob_grad = jnp.einsum("qhd,khd->hqk", mi, v, preferred_element_type=F32)
        delta = jnp.sum(probs * prob_grad, -1, keepdims=True)
        score_grad = (probs * (prob_grad - delta)).astype(BF16)
        dq = jnp.einsum("hqk,khd->qhd", score_grad, k, preferred_element_type=F32) * scale
        dk = dk + jnp.einsum("hqk,qhd->khd", score_grad, qi, preferred_element_type=F32) * scale
        dv = dv + jnp.einsum("hqk,qhd->khd", low, mi, preferred_element_type=F32)
        return (dk, dv), (out, dq)

    zero = jnp.zeros((rows, heads, HD), F32)
    cut = lambda t: t.reshape((rows // span, span) + t.shape[1:])
    (dk, dv), (out, dq) = lax.scan(step, (zero, zero), (cut(q), cut(m), cut(index), cut(segments)))
    flat = lambda t: t.reshape(rows, cols)
    return (
        flat(out),
        flat(rotate(dq.reshape(rows, cols), -sin)).astype(BF16),
        flat(rotate(dk.reshape(rows, cols), -sin)).astype(BF16),
        flat(dv).astype(BF16),
    )


def gather_plain(x, g, wsrc, places, segments):
    pieces = lax.all_to_all(wsrc, "ctx", split_axis=1, concat_axis=1, tiled=True)
    weights = lax.all_gather(pieces, "dp", axis=1, tiled=True)
    along = lambda t: lax.all_gather(t, "ctx", axis=0, tiled=True)
    return along(x), along(g), weights, along(places), along(segments)


def scatter_plain(out_part, normed_part, weight_part):
    summed = lambda t: lax.psum(
        lax.psum_scatter(t, "ctx", scatter_dimension=0, tiled=True), "tp"
    ).astype(F32)
    pieces = lax.psum_scatter(weight_part, "dp", scatter_dimension=1, tiled=True)
    pieces = lax.all_to_all(pieces, "ctx", split_axis=1, concat_axis=1, tiled=True)
    return summed(out_part), summed(normed_part), pieces.astype(F32)


def place_of():
    dp, me, core = lax.axis_index("dp"), lax.axis_index("ctx"), lax.axis_index("tp")
    return dp, me, core, dp + 1 - 2 * (dp % 2), dp + 2 - 4 * (dp // 2)


def greet(ways):
    dp, me, core, dpx, dpy = place_of()
    barrier = pltpu.get_barrier_semaphore()
    for device in [(dp, me, 1 - core), (dpx, me, core), (dpy, me, core)] + [
        (dp, (me + k) % ways, core) for k in range(1, ways)
    ]:
        pl.semaphore_signal(barrier, inc=1, device_id=device, device_id_type=MESH)
    pl.semaphore_wait(barrier, ways + 2)


def remote(src, dst, send, recv, device):
    return pltpu.make_async_remote_copy(
        src_ref=src, dst_ref=dst, send_sem=send, recv_sem=recv, device_id=device, device_id_type=MESH
    )


PIECES = 2


def gather_body(
    ways, x, g, w, ids, xo, go, wo, ido, zs, zr, ts, tr, ws, wr, ls, lr, ds, dr, ids_s, ids_r, own
):
    dp, me, core, dpx, dpy = place_of()
    rows = x.shape[0]
    piece = rows // 2 // PIECES
    groups = w.shape[0]
    srcs, outs = (x, g), (xo, go)

    def part(which, s):
        return pl.ds(pl.multiple_of(which * (rows // 2) + s * piece, 16), piece)

    def along(a, owner, s, side, mine=False):
        at = part(core, s)
        src = srcs[a].at[at, :] if mine else outs[a].at[owner, at, :]
        return remote(
            src,
            outs[a].at[owner, at, :],
            zs.at[side, a, owner, s],
            zr.at[a, owner, s],
            (dp, me - 1 + 2 * side, core),
        )

    def across(a, owner, s, which):
        at = part(which, s)
        ref = outs[a].at[owner, at, :]
        return remote(ref, ref, ts.at[a, owner, s], tr.at[a, owner, s], (dp, me, 1 - core))

    def share(grp, k):
        return remote(
            w.at[grp, (me + k) % ways],
            wo.at[grp, dp, me],
            ws.at[grp, k],
            wr.at[grp, k],
            (dp, (me + k) % ways, core),
        )

    def source(k):
        return (me - k + ways) % ways

    def spread(grp, k, axis):
        src = w.at[grp, me] if k == 0 else wo.at[grp, dp, source(k)]
        return remote(
            src,
            wo.at[grp, dp, source(k)],
            ls.at[axis, grp, k],
            lr.at[axis, grp, k],
            ((dpx, dpy)[axis], me, core),
        )

    def corner(grp, k):
        axis = (grp + k) % 2
        ref = wo.at[grp, (dpx, dpy)[axis], source(k)]
        return remote(ref, ref, ds.at[grp, k], dr.at[grp, k], ((dpy, dpx)[axis], me, core))

    def labels(k):
        return remote(
            ids, ido.at[me], ids_s.at[k], ids_r.at[k], (dp, (me + k) % ways, core)
        )

    greet(ways)
    local = [
        pltpu.make_async_copy(x, xo.at[me], own.at[0]),
        pltpu.make_async_copy(g, go.at[me], own.at[1]),
        pltpu.make_async_copy(ids, ido.at[me], own.at[2]),
    ] + [pltpu.make_async_copy(w.at[i], wo.at[i, dp, me], own.at[3 + i]) for i in range(0)]

    def send_own(a):
        for s in range(PIECES):
            pl.when(me > 0)(lambda: along(a, me, s, 0, True).start())
            pl.when(me < ways - 1)(lambda: along(a, me, s, 1, True).start())

    def send_shares(grp):
        for k in range(1, ways):
            share(grp, k).start()
        for axis in range(2):
            spread(grp, 0, axis).start()

    def pass_on(a, k):
        for s in range(PIECES):

            @pl.when(me + k < ways)
            def _():
                along(a, me + k, s, 0).wait_recv()
                pl.when(me > 0)(lambda: along(a, me + k, s, 0).start())
                across(a, me + k, s, core).start()

            @pl.when(me - k >= 0)
            def _():
                along(a, me - k, s, 1).wait_recv()
                pl.when(me < ways - 1)(lambda: along(a, me - k, s, 1).start())
                across(a, me - k, s, core).start()

    def spread_on(grp, k):
        share(grp, k).wait_recv()
        for axis in range(2):
            spread(grp, k, axis).start()

    def corner_on(grp, k):
        axis = (grp + k) % 2
        spread(grp, k, axis).wait_recv()
        corner(grp, k).start()

    for k in range(1, ways):
        labels(k).start()
    send_own(0)
    send_shares(0)
    for copy in local:
        copy.start()
    mine = [pltpu.make_async_copy(w.at[i, me], wo.at[i, dp, me], own.at[3 + i]) for i in range(groups)]
    for copy in mine:
        copy.start()
    send_shares(1)
    send_own(1)
    send_shares(2)
    for k in range(1, ways):
        pass_on(0, k)
        for grp in range(groups):
            spread_on(grp, k)
            corner_on(grp, k - 1)
        pass_on(1, k)
    for grp in range(groups):
        corner_on(grp, ways - 1)

    for k in range(1, ways):
        labels(k).wait()
    for copy in local + mine:
        copy.wait()
    for a in range(2):
        for owner in range(ways):
            for s in range(PIECES):

                @pl.when(owner != me)
                def _():
                    across(a, owner, s, core).wait_send()
                    across(a, owner, s, 1 - core).wait_recv()

                @pl.when((me > 0) & (owner >= me))
                def _():
                    along(a, owner, s, 0).wait_send()

                @pl.when((me < ways - 1) & (owner <= me))
                def _():
                    along(a, owner, s, 1).wait_send()

    for grp in range(groups):
        for k in range(ways):
            axis = (grp + k) % 2
            if k:
                share(grp, k).wait_send()
            for ax in range(2):
                spread(grp, k, ax).wait_send()
            spread(grp, k, 1 - axis).wait_recv()
            corner(grp, k).wait()


def gather(x, g, wsrc, places, segments):
    ways = lax.axis_size("ctx")
    chips = lax.axis_size("dp")
    rows, width = x.shape
    groups, unused, depth, cols = wsrc.shape
    ids = jnp.zeros((8, rows), jnp.int32).at[0].set(places).at[1].set(segments)
    dma = pltpu.SemaphoreType.DMA
    anywhere = pl.BlockSpec(memory_space=pl.ANY)
    xo, go, wo, ido = pl.pallas_call(
        functools.partial(gather_body, ways),
        in_specs=[anywhere] * 4,
        out_specs=[anywhere] * 4,
        out_shape=[
            jax.ShapeDtypeStruct((ways, rows, width), BF16),
            jax.ShapeDtypeStruct((ways, rows, width), BF16),
            jax.ShapeDtypeStruct((groups, chips, ways, depth, cols), BF16),
            jax.ShapeDtypeStruct((ways, 8, rows), jnp.int32),
        ],
        scratch_shapes=[
            dma((2, 2, ways, PIECES)),
            dma((2, ways, PIECES)),
            dma((2, ways, PIECES)),
            dma((2, ways, PIECES)),
            dma((groups, ways)),
            dma((groups, ways)),
            dma((2, groups, ways)),
            dma((2, groups, ways)),
            dma((groups, ways)),
            dma((groups, ways)),
            dma((ways,)),
            dma((ways,)),
            dma((3 + groups,)),
        ],
        compiler_params=pltpu.CompilerParams(
            collective_id=0, has_side_effects=True, vmem_limit_bytes=32 * MIB
        ),
    )(x, g, wsrc, ids)
    ids_all = ido[:, :2].transpose(1, 0, 2).reshape(2, ways * rows)
    flat = lambda t: t.reshape(ways * rows, width)
    return flat(xo), flat(go), wo, ids_all[0], ids_all[1]


def scatter_body(
    ways, p0, p1, gw, out, gwo,
    acc, tin, lin, rin, gown, first_in, second_in,
    tps, tpr, zs, zr, fs, fr, ss, sr, ws, wr, os, orr, loc, gloc,
):
    dp, me, core, dpx, dpy = place_of()
    rows, width = out.shape[1:]
    half = rows // 2
    piece = half // PIECES
    groups = gw.shape[0]
    span = gw.shape[2]
    lanes = gw.shape[3] // 2
    depth = span // ways
    parts = (p0, p1)
    nxt = (dpx, dpy)
    far = dpx + dpy - dp

    def part(which, s):
        return pl.ds(pl.multiple_of(which * half + s * piece, 16), piece)

    def swap(a, d, s):
        return remote(
            parts[a].at[d, part(1 - core, s), :],
            tin.at[a, d, s],
            tps.at[a, d, s],
            tpr.at[a, d, s],
            (dp, me, 1 - core),
        )

    def load(a, d, s):
        return pltpu.make_async_copy(parts[a].at[d, part(core, s), :], acc.at[a, d, s], loc.at[a, d, s])

    def stream(a, d, s, side):
        return remote(
            acc.at[a, d, s],
            (rin, lin)[side].at[a, d, s],
            zs.at[side, a, d, s],
            zr.at[side, a, d, s],
            (dp, me - 1 + 2 * side, core),
        )

    def finish(a, s):
        ref = out.at[a, part(core, s), :]
        return remote(ref, ref, os.at[a, s], orr.at[a, s], (dp, me, 1 - core))

    def quarter(path, which):
        return ((nxt[path], far), (nxt[1 - path], dp))[which]

    def lanes_of(path):
        return pl.ds(path * lanes, lanes)

    def first(grp, path, i):
        q = quarter(path, 0)[1 - i]
        return remote(
            gw.at[grp, q, :, lanes_of(path)],
            first_in.at[grp, path, i],
            fs.at[grp, path, i],
            fr.at[grp, path, i],
            (nxt[path], me, core),
        )

    def gload(grp, path, i):
        q = quarter(path, 1)[i]
        return pltpu.make_async_copy(
            gw.at[grp, q, :, lanes_of(path)], gown.at[grp, path, i], gloc.at[grp, path, i]
        )

    def second(grp, path):
        return remote(
            gown.at[grp, path, 0],
            second_in.at[grp, path],
            ss.at[grp, path],
            sr.at[grp, path],
            (nxt[1 - path], me, core),
        )

    def share(grp, path, k):
        d = (me + k) % ways
        return remote(
            gown.at[grp, path, 1, pl.ds(pl.multiple_of(d * depth, 16), depth), :],
            gwo.at[grp, me, :, lanes_of(path)],
            ws.at[grp, path, k],
            wr.at[grp, path, k],
            (dp, d, core),
        )

    def keep(grp, path):
        return pltpu.make_async_copy(
            gown.at[grp, path, 1, pl.ds(pl.multiple_of(me * depth, 16), depth), :],
            gwo.at[grp, me, :, lanes_of(path)],
            ws.at[grp, path, 0],
        )

    def add(dst, src, height):
        step = 32

        def body(i, carry):
            at = pl.ds(pl.multiple_of(i * step, step), step)
            dst[at, :] = dst[at, :] + src[at, :]
            return carry

        lax.fori_loop(0, height // step, body, 0)

    greet(ways)
    order = [0, 3, 1, 2] if ways == 4 else list(range(ways))
    for a in range(2):
        for d in order:
            for s in range(PIECES):
                swap(a, d, s).start()
                load(a, d, s).start()
    for grp in range(groups):
        for i in range(2):
            for path in range(2):
                first(grp, path, i).start()
                gload(grp, path, i).start()

    def merge(a):
        for d in order:
            for s in range(PIECES):
                swap(a, d, s).wait_recv()
                load(a, d, s).wait()
                add(acc.at[a, d, s], tin.at[a, d, s], piece)
                pl.when((me == 0) & (d > 0))(lambda: stream(a, d, s, 1).start())
                pl.when((me == ways - 1) & (d < ways - 1))(lambda: stream(a, d, s, 0).start())

    def hop(a, k):
        for s in range(PIECES):
            for d in range(ways - 1, -1, -1):

                @pl.when((me == k) & (d >= me))
                def _():
                    stream(a, d, s, 1).wait_recv()
                    add(acc.at[a, d, s], lin.at[a, d, s], piece)
                    pl.when(d > me)(lambda: stream(a, d, s, 1).start())

            for d in range(ways):

                @pl.when((me == ways - 1 - k) & (d <= me))
                def _():
                    stream(a, d, s, 0).wait_recv()
                    add(acc.at[a, d, s], rin.at[a, d, s], piece)
                    pl.when(d < me)(lambda: stream(a, d, s, 0).start())

    def grads_first(grp):
        for path in range(2):
            first(grp, path, 0).wait_recv()
            gload(grp, path, 0).wait()
            add(gown.at[grp, path, 0], first_in.at[grp, path, 0], span)
            second(grp, path).start()
            first(grp, path, 1).wait_recv()
            gload(grp, path, 1).wait()
            add(gown.at[grp, path, 1], first_in.at[grp, path, 1], span)

    def grads_second(grp):
        for path in range(2):
            second(grp, path).wait_recv()
            add(gown.at[grp, path, 1], second_in.at[grp, path], span)
            for k in range(1, ways):
                share(grp, path, k).start()
            keep(grp, path).start()

    def last(a):
        for s in range(PIECES):
            out[a, part(core, s), :] = acc[a, me, s]
            finish(a, s).start()

    merge(0)
    merge(1)
    for k in range(1, ways):
        hop(0, k)
        if k - 1 < groups:
            grads_first(k - 1)
        hop(1, k)
        if 0 <= k - 2 < groups:
            grads_second(k - 2)
    last(0)
    last(1)
    grads_second(groups - 1)

    for a in range(2):
        for s in range(PIECES):
            finish(a, s).wait_send()
            remote(
                out.at[a, part(1 - core, s), :],
                out.at[a, part(1 - core, s), :],
                os.at[a, s],
                orr.at[a, s],
                (dp, me, 1 - core),
            ).wait_recv()
            for d in range(ways):
                swap(a, d, s).wait_send()
                pl.when(d > me)(lambda: stream(a, d, s, 1).wait_send())
                pl.when(d < me)(lambda: stream(a, d, s, 0).wait_send())
    for grp in range(groups):
        for path in range(2):
            for i in range(2):
                first(grp, path, i).wait_send()
            second(grp, path).wait_send()
            keep(grp, path).wait()
            for k in range(1, ways):
                share(grp, path, k).wait()


def scatter(out_part, normed_part, weight_part):
    ways = lax.axis_size("ctx")
    chips = lax.axis_size("dp")
    width = out_part.shape[1]
    rows = out_part.shape[0] // ways
    groups, cols = weight_part.shape[0], weight_part.shape[-1]
    span = width // chips
    depth = span // ways
    piece = rows // 2 // PIECES
    lanes = cols // 2
    dma = pltpu.SemaphoreType.DMA
    anywhere = pl.BlockSpec(memory_space=pl.ANY)
    inside = pl.BlockSpec(memory_space=pltpu.VMEM)
    stack = pltpu.VMEM((2, ways, PIECES, piece, width), BF16)
    out, gwo = pl.pallas_call(
        functools.partial(scatter_body, ways),
        in_specs=[anywhere] * 3,
        out_specs=[inside, anywhere],
        out_shape=[
            jax.ShapeDtypeStruct((2, rows, width), BF16),
            jax.ShapeDtypeStruct((groups, ways, depth, cols), BF16),
        ],
        scratch_shapes=[
            stack,
            stack,
            stack,
            stack,
            pltpu.VMEM((groups, 2, 2, span, lanes), BF16),
            pltpu.VMEM((groups, 2, 2, span, lanes), BF16),
            pltpu.VMEM((groups, 2, span, lanes), BF16),
            dma((2, ways, PIECES)),
            dma((2, ways, PIECES)),
            dma((2, 2, ways, PIECES)),
            dma((2, 2, ways, PIECES)),
            dma((groups, 2, 2)),
            dma((groups, 2, 2)),
            dma((groups, 2)),
            dma((groups, 2)),
            dma((groups, 2, ways)),
            dma((groups, 2, ways)),
            dma((2, PIECES)),
            dma((2, PIECES)),
            dma((2, ways, PIECES)),
            dma((groups, 2, 2)),
        ],
        compiler_params=pltpu.CompilerParams(
            collective_id=1, has_side_effects=True, vmem_limit_bytes=56 * MIB
        ),
    )(
        out_part.reshape(ways, rows, width),
        normed_part.reshape(ways, rows, width),
        weight_part.reshape(groups, chips, span, cols),
    )
    return out[0].astype(F32), out[1].astype(F32), gwo.astype(F32)


def layer_norm(x):
    xf = x.astype(F32)
    mean = jnp.mean(xf, -1, keepdims=True)
    centred = xf - mean
    inv_std = lax.rsqrt(jnp.mean(centred * centred, -1, keepdims=True) + EPS)
    return centred * inv_std, inv_std


def per_device(
    block_input,
    cotangent,
    segment_ids,
    positions,
    norm_gain,
    norm_bias,
    w_qkv,
    qkv_bias,
    w_dense,
    w_fc1,
    fc1_bias,
    w_fc2,
    out_bias,
):
    ways = lax.axis_size("ctx")
    me = lax.axis_index("ctx")
    x, g = block_input[0], cotangent[0]
    rows, width = x.shape
    depth = w_fc1.shape[0]
    cols = w_fc1.shape[1] // ways
    head_cols = w_qkv.shape[2] // ways

    fc1 = w_fc1.reshape(depth, ways, cols).transpose(1, 0, 2)
    fc2 = w_fc2.reshape(ways, cols, depth).transpose(0, 2, 1)
    qkv = w_qkv.reshape(3, depth, ways, head_cols).transpose(2, 1, 0, 3)
    dense = w_dense.reshape(ways, head_cols, depth).transpose(0, 2, 1)
    att = jnp.concatenate([qkv.reshape(ways, depth, 3 * head_cols), dense], -1)
    wsrc = jnp.stack([fc1, fc2, att])

    fast = ways == 4 and lax.axis_size("dp") == 4 and rows % 64 == 0 and head_cols % 128 == 0
    exchange_in, exchange_out = (gather, scatter) if fast else (gather_plain, scatter_plain)
    x_all, g_all, weights, places, segments = exchange_in(
        x, g, wsrc, positions[0], segment_ids[0]
    )
    weights = weights.reshape(3, width, cols)
    w1, w2, wa = weights[0], weights[1], weights[2]
    wp, wd = wa[:, : 3 * head_cols], wa[:, 3 * head_cols :]

    gain, shift = norm_gain.astype(F32), norm_bias.astype(F32)
    x_hat, unused = layer_norm(x_all)
    normed = (x_hat * gain + shift).astype(BF16)

    qkv_shift = lax.dynamic_slice_in_dim(qkv_bias, me * head_cols, head_cols, 1)
    fc1_shift = lax.dynamic_slice_in_dim(fc1_bias, me * cols, cols, 0)
    projected = dot_nn(normed, wp) + qkv_shift.astype(F32).reshape(1, 3 * head_cols)
    mix_grad = dot_nn(g_all, wd).astype(BF16)
    attend = attention if head_cols % 128 == 0 else attention_plain
    mixture, gq, gk, gv = attend(
        projected[:, :head_cols],
        projected[:, head_cols : 2 * head_cols],
        projected[:, 2 * head_cols :],
        mix_grad,
        places,
        segments,
    )
    proj_grad = jnp.concatenate([gq, gk, gv], 1)

    hidden_pre = dot_nn(normed, w1) + fc1_shift.astype(F32)
    hidden, gelu_back = jax.vjp(lambda t: jax.nn.gelu(t, approximate=True), hidden_pre)
    hidden = hidden.astype(BF16)
    hidden_grad = gelu_back(dot_nn(g_all, w2))[0].astype(BF16)

    out_part = (dot_nt(mixture, wd) + dot_nt(hidden, w2)).astype(BF16)
    normed_part = dot_nt(proj_grad, wp) + dot_nt(hidden_grad, w1)
    weight_part = jnp.stack(
        [
            dot_tn(normed, hidden_grad).astype(BF16),
            dot_tn(g_all, hidden).astype(BF16),
            jnp.concatenate([dot_tn(normed, proj_grad), dot_tn(g_all, mixture)], 1).astype(BF16),
        ]
    )
    gain_part = jnp.sum(normed_part * x_hat, 0)
    shift_part = jnp.sum(normed_part, 0)
    qkv_bias_part = jnp.sum(proj_grad.astype(F32), 0).reshape(3, head_cols)
    fc1_bias_part = jnp.sum(hidden_grad.astype(F32), 0)

    branches, normed_grad, weight_grads = exchange_out(
        out_part, normed_part.astype(BF16), weight_part.reshape(3, -1, depth, cols)
    )

    gf = g.astype(F32)
    output = (x.astype(F32) + branches + out_bias.astype(F32)).astype(BF16)
    own_hat, inv_std = layer_norm(x)
    scaled = normed_grad * gain
    grad_input = gf + inv_std * (
        scaled
        - jnp.mean(scaled, -1, keepdims=True)
        - own_hat * jnp.mean(scaled * own_hat, -1, keepdims=True)
    )
    place = lambda t, whole, axis: lax.dynamic_update_slice_in_dim(
        jnp.zeros(whole, F32), t, me * t.shape[axis], axis
    )
    small = lax.psum(
        (
            place(qkv_bias_part, (3, head_cols * ways), 1),
            place(fc1_bias_part, (cols * ways,), 0),
            jnp.sum(gf, 0),
        ),
        ("dp", "ctx"),
    )
    norm_small = lax.psum((gain_part, shift_part), ("dp", "ctx", "tp"))

    grad_fc1 = weight_grads[0].transpose(1, 0, 2).reshape(depth, ways * cols)
    grad_fc2 = weight_grads[1].transpose(0, 2, 1).reshape(ways * cols, depth)
    grad_att = weight_grads[2].reshape(ways, depth, 4, head_cols)
    grad_qkv = grad_att[:, :, :3].transpose(2, 1, 0, 3).reshape(3, depth, ways * head_cols)
    grad_dense = grad_att[:, :, 3].transpose(0, 2, 1).reshape(ways * head_cols, depth)
    return (
        output[None],
        grad_input.astype(BF16)[None],
        norm_small[0],
        norm_small[1],
        grad_qkv,
        small[0],
        grad_dense,
        grad_fc1,
        small[1],
        grad_fc2,
        small[2],
    )


def solution(mesh):
    placed = (
        P("dp", "ctx", None),
        P("dp", "ctx", None),
        P("dp", "ctx"),
        P("dp", "ctx"),
        P(),
        P(),
        P(None, ("dp", "ctx"), "tp"),
        P(None, "tp"),
        P("tp", ("dp", "ctx")),
        P(("dp", "ctx"), "tp"),
        P("tp"),
        P("tp", ("dp", "ctx")),
        P(),
    )
    return jax.shard_map(
        per_device,
        mesh=mesh,
        in_specs=placed,
        out_specs=(
            P("dp", "ctx", None),
            P("dp", "ctx", None),
            P(),
            P(),
            P(None, ("dp", "ctx"), "tp"),
            P(None, "tp"),
            P("tp", ("dp", "ctx")),
            P(("dp", "ctx"), "tp"),
            P("tp"),
            P("tp", ("dp", "ctx")),
            P(),
        ),
        check_vma=False,
    )
```

```python
import functools
import math

import jax
import jax.numpy as jnp
from jax import lax
from jax.experimental import pallas as pl
from jax.experimental.pallas import tpu as pltpu
from jax.sharding import PartitionSpec as P

HD = 64
ROT = 32
EPS = 1e-05
MIB = 1 << 20
F32 = jnp.float32
BF16 = jnp.bfloat16
MESH = pl.DeviceIdType.MESH


def dot_nn(a, b):
    return lax.dot_general(a, b, (((1,), (0,)), ((), ())), preferred_element_type=F32)


def dot_nt(a, b):
    return lax.dot_general(a, b, (((1,), (1,)), ((), ())), preferred_element_type=F32)


def dot_tn(a, b):
    return lax.dot_general(a, b, (((0,), (0,)), ((), ())), preferred_element_type=F32)


def rotary_tables(places):
    half = ROT // 2
    frequency = 10000.0 ** (-(jnp.arange(half, dtype=F32) * 2.0 / ROT))
    angles = places.astype(F32)[:, None] * frequency[None, :]
    cos, sin = jnp.cos(angles), jnp.sin(angles)
    rows = places.shape[0]
    zero = jnp.zeros((rows, half), F32)
    rest0 = jnp.zeros((rows, HD - ROT), F32)
    rest1 = jnp.ones((rows, HD - ROT), F32)
    keep = jnp.concatenate([cos, cos, rest1] * 2, 1)
    from_right = jnp.concatenate([-sin, zero, rest0] * 2, 1)
    from_left = jnp.concatenate([zero, sin, rest0] * 2, 1)
    return keep, from_right, from_left


def turn(v, keep, from_right, from_left):
    half = ROT // 2
    return v * keep + pltpu.roll(v, 128 - half, 1) * from_right + pltpu.roll(v, half, 1) * from_left


def attention_body(
    block_rows, pq, pk, pv, mg, keep, fr, fl, seg_row, seg_col, mix, gq, gk, gv, q, k, v, dq, dk, dv
):
    rows = pq.shape[0]
    scale = 1.0 / math.sqrt(HD)
    q[...] = (turn(pq[...], keep[...], fr[...], fl[...]).astype(BF16) * scale).astype(BF16)
    k[...] = turn(pk[...], keep[...], fr[...], fl[...]).astype(BF16)
    v[...] = pv[...].astype(BF16)
    dk[...] = jnp.zeros_like(dk)
    dv[...] = jnp.zeros_like(dv)
    first = lax.broadcasted_iota(jnp.int32, (block_rows, 128), 1) < HD
    for i in range(rows // block_rows):
        here = pl.ds(i * block_rows, block_rows)
        seen = pl.ds(0, (i + 1) * block_rows)
        keys, values = k[seen, :], v[seen, :]
        shape = (block_rows, (i + 1) * block_rows)
        row_index = lax.broadcasted_iota(jnp.int32, shape, 0) + i * block_rows
        col_index = lax.broadcasted_iota(jnp.int32, shape, 1)
        allowed = (col_index <= row_index) & (seg_col[here, :] == seg_row[:, seen])
        parts = []
        for sub in range(2):
            mine = first if sub == 0 else ~first
            qi = jnp.where(mine, q[here, :], 0)
            mi = jnp.where(mine, mg[here, :], 0)
            scores = jnp.where(allowed, dot_nt(qi, keys), -1e30)
            top = jnp.max(scores, 1, keepdims=True)
            expo = jnp.exp(scores - top)
            probs = expo * (1.0 / jnp.sum(expo, 1, keepdims=True))
            low = probs.astype(BF16)
            out = dot_nn(low, values)
            prob_grad = dot_nt(mi, values)
            delta = jnp.sum(probs * prob_grad, 1, keepdims=True)
            score_grad = (probs * (prob_grad - delta)).astype(BF16)
            dqi = dot_nn(score_grad, keys) * scale
            dk[seen, :] += dot_tn(score_grad, qi)
            dv[seen, :] += dot_tn(low, mi)
            parts.append((out, dqi))
        mix[here, :] = jnp.where(first, parts[0][0], parts[1][0]).astype(BF16)
        dq[here, :] = jnp.where(first, parts[0][1], parts[1][1])
    gq[...] = turn(dq[...], keep[...], -fr[...], -fl[...]).astype(BF16)
    gk[...] = turn(dk[...], keep[...], -fr[...], -fl[...]).astype(BF16)
    gv[...] = dv[...].astype(BF16)


def attention(pq, pk, pv, mg, places, segments):
    rows, cols = pq.shape
    keep, fr, fl = rotary_tables(places)
    pair = pl.BlockSpec((rows, 128), lambda h: (0, h))
    whole = pl.BlockSpec((rows, 128), lambda h: (0, 0))
    return pl.pallas_call(
        functools.partial(attention_body, 256),
        grid=(cols // 128,),
        in_specs=[pair] * 4
        + [whole] * 3
        + [
            pl.BlockSpec((1, rows), lambda h: (0, 0)),
            pl.BlockSpec((rows, 1), lambda h: (0, 0)),
        ],
        out_specs=[pair] * 4,
        out_shape=[jax.ShapeDtypeStruct((rows, cols), BF16)] * 4,
        scratch_shapes=[pltpu.VMEM((rows, 128), BF16)] * 3 + [pltpu.VMEM((rows, 128), F32)] * 3,
        compiler_params=pltpu.CompilerParams(vmem_limit_bytes=48 * MIB),
    )(pq, pk, pv, mg, keep, fr, fl, segments[None, :], segments[:, None])


def attention_plain(pq, pk, pv, mg, places, segments):
    rows, cols = pq.shape
    heads = cols // HD
    half = ROT // 2
    scale = 1.0 / math.sqrt(HD)
    frequency = 10000.0 ** (-(jnp.arange(half, dtype=F32) * 2.0 / ROT))
    angles = places.astype(F32)[:, None] * frequency[None, :]
    cos, sin = jnp.cos(angles)[:, None, :], jnp.sin(angles)[:, None, :]

    def rotate(t, s):
        t = t.reshape(rows, heads, HD)
        a, b = t[..., :half], t[..., half:ROT]
        return jnp.concatenate([a * cos - b * s, b * cos + a * s, t[..., ROT:]], -1)

    q = rotate(pq, sin).astype(BF16)
    k = rotate(pk, sin).astype(BF16)
    v = pv.astype(BF16).reshape(rows, heads, HD)
    m = mg.reshape(rows, heads, HD)
    span = 256
    index = jnp.arange(rows, dtype=jnp.int32)

    def step(carry, items):
        dk, dv = carry
        qi, mi, row_index, row_seg = items
        scores = jnp.einsum("qhd,khd->hqk", qi, k, preferred_element_type=F32) * scale
        allowed = (index[None, :] <= row_index[:, None]) & (segments[None, :] == row_seg[:, None])
        scores = jnp.where(allowed[None], scores, -1e30)
        expo = jnp.exp(scores - jnp.max(scores, -1, keepdims=True))
        probs = expo / jnp.sum(expo, -1, keepdims=True)
        low = probs.astype(BF16)
        out = jnp.einsum("hqk,khd->qhd", low, v, preferred_element_type=F32).astype(BF16)
        prob_grad = jnp.einsum("qhd,khd->hqk", mi, v, preferred_element_type=F32)
        delta = jnp.sum(probs * prob_grad, -1, keepdims=True)
        score_grad = (probs * (prob_grad - delta)).astype(BF16)
        dq = jnp.einsum("hqk,khd->qhd", score_grad, k, preferred_element_type=F32) * scale
        dk = dk + jnp.einsum("hqk,qhd->khd", score_grad, qi, preferred_element_type=F32) * scale
        dv = dv + jnp.einsum("hqk,qhd->khd", low, mi, preferred_element_type=F32)
        return (dk, dv), (out, dq)

    zero = jnp.zeros((rows, heads, HD), F32)
    cut = lambda t: t.reshape((rows // span, span) + t.shape[1:])
    (dk, dv), (out, dq) = lax.scan(step, (zero, zero), (cut(q), cut(m), cut(index), cut(segments)))
    flat = lambda t: t.reshape(rows, cols)
    return (
        flat(out),
        flat(rotate(dq.reshape(rows, cols), -sin)).astype(BF16),
        flat(rotate(dk.reshape(rows, cols), -sin)).astype(BF16),
        flat(dv).astype(BF16),
    )


def gather_plain(x, g, wsrc, places, segments):
    pieces = lax.all_to_all(wsrc, "ctx", split_axis=1, concat_axis=1, tiled=True)
    weights = lax.all_gather(pieces, "dp", axis=1, tiled=True)
    along = lambda t: lax.all_gather(t, "ctx", axis=0, tiled=True)
    return along(x), along(g), weights, along(places), along(segments)


def scatter_plain(out_part, normed_part, weight_part):
    summed = lambda t: lax.psum(
        lax.psum_scatter(t, "ctx", scatter_dimension=0, tiled=True), "tp"
    ).astype(F32)
    pieces = lax.psum_scatter(weight_part, "dp", scatter_dimension=1, tiled=True)
    pieces = lax.all_to_all(pieces, "ctx", split_axis=1, concat_axis=1, tiled=True)
    return summed(out_part), summed(normed_part), pieces.astype(F32)


def place_of():
    dp, me, core = lax.axis_index("dp"), lax.axis_index("ctx"), lax.axis_index("tp")
    return dp, me, core, dp + 1 - 2 * (dp % 2), dp + 2 - 4 * (dp // 2)


def greet(ways):
    dp, me, core, dpx, dpy = place_of()
    barrier = pltpu.get_barrier_semaphore()
    for device in [(dp, me, 1 - core), (dpx, me, core), (dpy, me, core)] + [
        (dp, (me + k) % ways, core) for k in range(1, ways)
    ]:
        pl.semaphore_signal(barrier, inc=1, device_id=device, device_id_type=MESH)
    pl.semaphore_wait(barrier, ways + 2)


def remote(src, dst, send, recv, device):
    return pltpu.make_async_remote_copy(
        src_ref=src, dst_ref=dst, send_sem=send, recv_sem=recv, device_id=device, device_id_type=MESH
    )


PIECES = 2


def gelu_and_slope(v):
    c = math.sqrt(2.0 / math.pi)
    square = v * v
    tanh = jnp.tanh(c * v * (1.0 + 0.044715 * square))
    half = 0.5 * (1.0 + tanh)
    slope = half + 0.5 * c * v * (1.0 - tanh * tanh) * (1.0 + 3.0 * 0.044715 * square)
    return v * half, slope


def forward_body(
    ways, x, g, w, ids, gain, shift, fc1_shift, qkv_shift,
    go, ido, no, xho, ho, hgo, outo, ngo, pro, mgo, wao, biaso,
    xo, wv, norm, xb, gb, pre, hid, slope, hgb, ob, nb, pb, mb,
    zs, zr, ts, tr, ws, wr, ls, lr, ds, dr, ids_s, ids_r, own, ls_in, ls_out,
):
    dp, me, core, dpx, dpy = place_of()
    rows, width = x.shape
    piece = rows // 2 // PIECES
    groups, unused, depth, cols = w.shape
    head_cols = cols // 4
    srcs, outs = (x, g), (xo, go)
    blocks = [me, 1 + me % 2, None, 3 * (1 - me // 2)]
    blocks[2] = 6 - me - blocks[1] - blocks[3]

    def part(which, s):
        return pl.ds(pl.multiple_of(which * (rows // 2) + s * piece, 16), piece)

    def along(a, owner, s, side, mine=False):
        at = part(core, s)
        src = srcs[a].at[at, :] if mine else outs[a].at[owner, at, :]
        return remote(
            src,
            outs[a].at[owner, at, :],
            zs.at[side, a, owner, s],
            zr.at[a, owner, s],
            (dp, me - 1 + 2 * side, core),
        )

    def across(a, owner, s, which):
        at = part(which, s)
        ref = outs[a].at[owner, at, :]
        return remote(ref, ref, ts.at[a, owner, s], tr.at[a, owner, s], (dp, me, 1 - core))

    def rows_of(chip, j):
        return pl.ds(pl.multiple_of((chip * ways + j) * depth, 16), depth)

    def share(grp, k):
        return remote(
            w.at[grp, (me + k) % ways],
            wv.at[grp, rows_of(dp, me), :],
            ws.at[grp, k],
            wr.at[grp, k],
            (dp, (me + k) % ways, core),
        )

    def source(k):
        return (me - k + ways) % ways

    def spread(grp, k, axis):
        at = rows_of(dp, source(k))
        return remote(
            w.at[grp, me] if k == 0 else wv.at[grp, at, :],
            wv.at[grp, at, :],
            ls.at[axis, grp, k],
            lr.at[axis, grp, k],
            ((dpx, dpy)[axis], me, core),
        )

    def corner(grp, k):
        axis = (grp + k) % 2
        ref = wv.at[grp, rows_of((dpx, dpy)[axis], source(k)), :]
        return remote(ref, ref, ds.at[grp, k], dr.at[grp, k], ((dpy, dpx)[axis], me, core))

    def labels(k):
        return remote(ids, ido.at[me], ids_s.at[k], ids_r.at[k], (dp, (me + k) % ways, core))

    def send_own(a):
        for s in range(PIECES):
            pl.when(me > 0)(lambda: along(a, me, s, 0, True).start())
            pl.when(me < ways - 1)(lambda: along(a, me, s, 1, True).start())

    def send_shares(grp):
        for k in range(1, ways):
            share(grp, k).start()
        for axis in range(2):
            spread(grp, 0, axis).start()

    def pass_on(a, k):
        for s in range(PIECES):

            @pl.when(me + k < ways)
            def _():
                along(a, me + k, s, 0).wait_recv()
                pl.when(me > 0)(lambda: along(a, me + k, s, 0).start())
                across(a, me + k, s, core).start()

            @pl.when(me - k >= 0)
            def _():
                along(a, me - k, s, 1).wait_recv()
                pl.when(me < ways - 1)(lambda: along(a, me - k, s, 1).start())
                across(a, me - k, s, core).start()

    def spread_on(grp, k):
        share(grp, k).wait_recv()
        for axis in range(2):
            spread(grp, k, axis).start()

    def corner_on(grp, k):
        axis = (grp + k) % 2
        spread(grp, k, axis).wait_recv()
        corner(grp, k).start()

    def settle(grp):
        keeps[grp].wait()
        for k in range(ways):
            spread(grp, k, 1 - (grp + k) % 2).wait_recv()
            corner(grp, k).wait_recv()

    def arrive(a, t):
        if t:
            for s in range(PIECES):
                across(a, blocks[t], s, 1 - core).wait_recv()

    def loop(count, body):
        lax.fori_loop(0, count, lambda i, c: (body(i), c)[1], 0)

    def load_x(t):
        src = x if t == 0 else xo.at[blocks[t]]
        return pltpu.make_async_copy(src, xb.at[t % 2], ls_in.at[0, t])

    def load_g(t):
        src = g if t == 0 else go.at[blocks[t]]
        return pltpu.make_async_copy(src, gb.at[t % 2], ls_in.at[1, t])

    def store(which, t):
        o = blocks[t]
        src, dst = (
            (xb.at[t % 2], xho.at[o]),
            (norm.at[o], no.at[o]),
            (hid.at[o], ho.at[o]),
            (ob.at[t % 2], outo.at[o]),
            (nb.at[t % 2], ngo.at[o]),
            (hgb.at[t % 2], hgo.at[o]),
            (pb.at[t % 2], pro.at[o]),
            (mb.at[t], mgo.at[o]),
        )[which]
        return pltpu.make_async_copy(src, dst, ls_out.at[which, t])

    def normalise(t):
        arrive(0, t)
        if t >= 2:
            store(0, t - 2).wait()
        load_x(t).start()
        load_x(t).wait()
        step = 32

        def body(i):
            at = pl.ds(pl.multiple_of(i * step, step), step)
            xf = xb[t % 2, at, :].astype(F32)
            centred = xf - jnp.mean(xf, -1, keepdims=True)
            inv_std = lax.rsqrt(jnp.mean(centred * centred, -1, keepdims=True) + EPS)
            x_hat = centred * inv_std
            norm[blocks[t], at, :] = (x_hat * gain[...] + shift[...]).astype(BF16)
            xb[t % 2, at, :] = x_hat.astype(BF16)

        loop(rows // step, body)
        store(0, t).start()
        store(1, t).start()

    wide = 512

    def span(i):
        return pl.ds(pl.multiple_of(i * wide, wide), wide)

    def up(t):
        o = blocks[t]

        def mul(i):
            pre[:, span(i)] = dot_nn(norm[o], wv[0, :, span(i)]) + fc1_shift[:, span(i)]

        loop(cols // wide, mul)

        def act(i):
            at = pl.ds(pl.multiple_of(i * 16, 16), 16)
            value, grad = gelu_and_slope(pre[at, :])
            hid[o, at, :] = value.astype(BF16)
            slope[o, at, :] = grad

        loop(rows // 16, act)
        store(2, t).start()

    def project(t):
        if t >= 2:
            store(6, t - 2).wait()
        o = blocks[t]
        pb[t % 2] = dot_nn(norm[o], wv[2, :, : 3 * head_cols]) + qkv_shift[...]
        store(6, t).start()

    def down(t):
        if t >= 2:
            store(3, t - 2).wait()
        o = blocks[t]

        def mul(i):
            ob[t % 2, :, span(i)] = dot_nt(hid[o], wv[1, span(i), :]).astype(BF16)

        loop(width // wide, mul)
        store(3, t).start()

    def back(t):
        arrive(1, t)
        load_g(t).start()
        if t >= 2:
            store(4, t - 2).wait()
            store(5, t - 2).wait()
        load_g(t).wait()
        o = blocks[t]

        def mul(i):
            act = dot_nn(gb[t % 2], wv[1, :, span(i)])
            grad = (act * slope[o, :, span(i)]).astype(BF16)
            hgb[t % 2, :, span(i)] = grad
            total = jnp.sum(grad.astype(F32), 0, keepdims=True)
            biaso[:, span(i)] = total if t == 0 else biaso[:, span(i)] + total

        loop(cols // wide, mul)
        store(5, t).start()

        def mul_back(i):
            nb[t % 2, :, span(i)] = dot_nt(hgb[t % 2], wv[0, span(i), :]).astype(BF16)

        loop(width // wide, mul_back)
        store(4, t).start()
        mb[t] = dot_nn(gb[t % 2], wv[2, :, 3 * head_cols :]).astype(BF16)
        store(7, t).start()

    greet(ways)
    send_own(0)
    send_shares(0)
    send_shares(1)
    for k in range(1, ways):
        labels(k).start()
    keeps = [
        pltpu.make_async_copy(w.at[i, me], wv.at[i, rows_of(dp, me), :], own.at[i])
        for i in range(groups)
    ] + [
        pltpu.make_async_copy(g, go.at[me], own.at[groups]),
        pltpu.make_async_copy(ids, ido.at[me], own.at[groups + 1]),
    ]
    for copy in keeps:
        copy.start()
    wa_out = pltpu.make_async_copy(wv.at[2], wao, own.at[groups + 2])
    steps = dict(
        S=send_shares,
        G=lambda: send_own(1),
        W=wa_out.start,
        x=lambda k: pass_on(0, k),
        g=lambda k: pass_on(1, k),
        s=spread_on,
        c=corner_on,
        e=settle,
        n=normalise,
        u=up,
        p=project,
        d=down,
        b=back,
    )
    plan = (
        "n0", "s01", "c00", "x1", "S2", "n1", "s02", "c01", "s03", "c02", "x2", "G", "n2", "c03",
        "s11", "c10", "s12", "c11", "s13", "c12", "x3", "n3", "e0", "u0", "c13", "s21", "c20",
        "u1", "s22", "c21", "g1", "u2", "s23", "c22", "u3", "c23", "e1", "d0", "d1", "g2", "e2",
        "W", "p0", "b0", "p1", "b1", "d2", "p2", "g3", "b2", "d3", "p3", "b3",
    )
    for word in plan:
        steps[word[0]](*(int(digit) for digit in word[1:]))
    for copy in keeps[groups:]:
        copy.wait()

    for k in range(1, ways):
        labels(k).wait()
    wa_out.wait()
    for t in range(4):
        for which in (1, 2, 7):
            store(which, t).wait()
        if t >= 2:
            for which in (0, 3, 4, 5, 6):
                store(which, t).wait()
    for a in range(2):
        for owner in range(ways):
            for s in range(PIECES):

                @pl.when(owner != me)
                def _():
                    across(a, owner, s, core).wait_send()

                @pl.when((me > 0) & (owner >= me))
                def _():
                    along(a, owner, s, 0).wait_send()

                @pl.when((me < ways - 1) & (owner <= me))
                def _():
                    along(a, owner, s, 1).wait_send()

    for grp in range(groups):
        for k in range(ways):
            if k:
                share(grp, k).wait_send()
            for axis in range(2):
                spread(grp, k, axis).wait_send()
            corner(grp, k).wait_send()


def forward(x, g, wsrc, places, segments, gain, shift, fc1_shift, qkv_shift):
    ways = lax.axis_size("ctx")
    rows, width = x.shape
    groups, unused, depth, cols = wsrc.shape
    head_cols = cols // 4
    ids = jnp.zeros((8, rows), jnp.int32).at[0].set(places).at[1].set(segments)
    dma = pltpu.SemaphoreType.DMA
    vmem = pltpu.VMEM
    anywhere = pl.BlockSpec(memory_space=pl.ANY)
    inside = pl.BlockSpec(memory_space=pltpu.VMEM)
    seq = lambda n, dtype=BF16: jax.ShapeDtypeStruct((ways, rows, n), dtype)
    outs = pl.pallas_call(
        functools.partial(forward_body, ways),
        in_specs=[anywhere] * 4 + [inside] * 4,
        out_specs=[anywhere] * 11 + [inside, anywhere],
        out_shape=[
            seq(width),
            jax.ShapeDtypeStruct((ways, 8, rows), jnp.int32),
            seq(width),
            seq(width),
            seq(cols),
            seq(cols),
            seq(width),
            seq(width),
            seq(3 * head_cols, F32),
            seq(head_cols),
            jax.ShapeDtypeStruct((width, cols), BF16),
            jax.ShapeDtypeStruct((1, cols), F32),
            seq(width),
        ],
        scratch_shapes=[
            vmem((groups, width, cols), BF16),
            vmem((ways, rows, width), BF16),
            vmem((2, rows, width), BF16),
            vmem((2, rows, width), BF16),
            vmem((rows, cols), F32),
            vmem((ways, rows, cols), BF16),
            vmem((ways, rows, cols), F32),
            vmem((2, rows, cols), BF16),
            vmem((2, rows, width), BF16),
            vmem((2, rows, width), BF16),
            vmem((2, rows, 3 * head_cols), F32),
            vmem((ways, rows, head_cols), BF16),
            dma((2, 2, ways, PIECES)),
            dma((2, ways, PIECES)),
            dma((2, ways, PIECES)),
            dma((2, ways, PIECES)),
            dma((groups, ways)),
            dma((groups, ways)),
            dma((2, groups, ways)),
            dma((2, groups, ways)),
            dma((groups, ways)),
            dma((groups, ways)),
            dma((ways,)),
            dma((ways,)),
            dma((3 + groups,)),
            dma((2, ways)),
            dma((8, ways)),
        ],
        compiler_params=pltpu.CompilerParams(
            collective_id=0, has_side_effects=True, vmem_limit_bytes=60 * MIB
        ),
    )(
        x, g, wsrc, ids,
        gain.reshape(1, width), shift.reshape(1, width), fc1_shift.reshape(1, cols),
        qkv_shift.reshape(1, 3 * head_cols),
    )
    return outs


def scatter_body(
    ways, p0, p1, gw, small, out, gwo, smallo,
    acc, tin, lin, rin, gown, first_in, second_in,
    tps, tpr, zs, zr, fs, fr, ss, sr, ws, wr, os, orr, loc, gloc,
    sum_in, sum_out, sms, smr,
):
    dp, me, core, dpx, dpy = place_of()
    rows, width = out.shape[1:]
    half = rows // 2
    piece = half // PIECES
    groups = gw.shape[0]
    span = gw.shape[2]
    lanes = gw.shape[3] // 2
    depth = span // ways
    parts = (p0, p1)
    nxt = (dpx, dpy)
    far = dpx + dpy - dp

    def part(which, s):
        return pl.ds(pl.multiple_of(which * half + s * piece, 16), piece)

    def swap(a, d, s):
        return remote(
            parts[a].at[d, part(1 - core, s), :],
            tin.at[a, d, s],
            tps.at[a, d, s],
            tpr.at[a, d, s],
            (dp, me, 1 - core),
        )

    def load(a, d, s):
        return pltpu.make_async_copy(parts[a].at[d, part(core, s), :], acc.at[a, d, s], loc.at[a, d, s])

    def stream(a, d, s, side):
        return remote(
            acc.at[a, d, s],
            (rin, lin)[side].at[a, d, s],
            zs.at[side, a, d, s],
            zr.at[side, a, d, s],
            (dp, me - 1 + 2 * side, core),
        )

    def finish(a, s):
        ref = out.at[a, part(core, s), :]
        return remote(ref, ref, os.at[a, s], orr.at[a, s], (dp, me, 1 - core))

    def quarter(path, which):
        return ((nxt[path], far), (nxt[1 - path], dp))[which]

    def lanes_of(path):
        return pl.ds(path * lanes, lanes)

    def first(grp, path, i):
        q = quarter(path, 0)[1 - i]
        return remote(
            gw.at[grp, q, :, lanes_of(path)],
            first_in.at[grp, path, i],
            fs.at[grp, path, i],
            fr.at[grp, path, i],
            (nxt[path], me, core),
        )

    def gload(grp, path, i):
        q = quarter(path, 1)[i]
        return pltpu.make_async_copy(
            gw.at[grp, q, :, lanes_of(path)], gown.at[grp, path, i], gloc.at[grp, path, i]
        )

    def second(grp, path):
        return remote(
            gown.at[grp, path, 0],
            second_in.at[grp, path],
            ss.at[grp, path],
            sr.at[grp, path],
            (nxt[1 - path], me, core),
        )

    def share(grp, path, k):
        d = (me + k) % ways
        return remote(
            gown.at[grp, path, 1, pl.ds(pl.multiple_of(d * depth, 16), depth), :],
            gwo.at[grp, me, :, lanes_of(path)],
            ws.at[grp, path, k],
            wr.at[grp, path, k],
            (dp, d, core),
        )

    def keep(grp, path):
        return pltpu.make_async_copy(
            gown.at[grp, path, 1, pl.ds(pl.multiple_of(me * depth, 16), depth), :],
            gwo.at[grp, me, :, lanes_of(path)],
            ws.at[grp, path, 0],
        )

    def add(dst, src, height):
        step = 32

        def body(i, carry):
            at = pl.ds(pl.multiple_of(i * step, step), step)
            dst[at, :] = dst[at, :] + src[at, :]
            return carry

        lax.fori_loop(0, height // step, body, 0)

    def small_send(i):
        src = small if i == 0 else sum_out.at[i - 1]
        device = ((dp, me, 1 - core), (dpx, me, core), (dpy, me, core))[i]
        return remote(src, sum_in.at[i], sms.at[i], smr.at[i], device)

    def small_all(k):
        device = (dp, (me + k) % ways, core)
        return remote(sum_out.at[2], smallo.at[me], sms.at[2 + k], smr.at[2 + k], device)

    def small_step(i):
        small_send(i).wait_recv()
        before = small[...] if i == 0 else sum_out[i - 1]
        after = before + sum_in[i]
        if i == 0:
            row = lax.broadcasted_iota(jnp.int32, after.shape, 0)
            after = jnp.where(row < 2, after, before)
        sum_out[i] = after
        if i < 2:
            small_send(i + 1).start()
        else:
            for k in range(1, ways):
                small_all(k).start()
            smallo[me] = after

    greet(ways)
    small_send(0).start()
    order = [0, 3, 1, 2] if ways == 4 else list(range(ways))
    for a in range(2):
        for d in order:
            for s in range(PIECES):
                swap(a, d, s).start()
                load(a, d, s).start()
    for grp in range(groups):
        for i in range(2):
            for path in range(2):
                first(grp, path, i).start()
                gload(grp, path, i).start()

    def merge(a):
        for d in order:
            for s in range(PIECES):
                swap(a, d, s).wait_recv()
                load(a, d, s).wait()
                add(acc.at[a, d, s], tin.at[a, d, s], piece)
                pl.when((me == 0) & (d > 0))(lambda: stream(a, d, s, 1).start())
                pl.when((me == ways - 1) & (d < ways - 1))(lambda: stream(a, d, s, 0).start())

    def hop(a, k):
        for s in range(PIECES):
            for d in range(ways - 1, -1, -1):

                @pl.when((me == k) & (d >= me))
                def _():
                    stream(a, d, s, 1).wait_recv()
                    add(acc.at[a, d, s], lin.at[a, d, s], piece)
                    pl.when(d > me)(lambda: stream(a, d, s, 1).start())

            for d in range(ways):

                @pl.when((me == ways - 1 - k) & (d <= me))
                def _():
                    stream(a, d, s, 0).wait_recv()
                    add(acc.at[a, d, s], rin.at[a, d, s], piece)
                    pl.when(d < me)(lambda: stream(a, d, s, 0).start())

    def grads_first(grp):
        for path in range(2):
            first(grp, path, 0).wait_recv()
            gload(grp, path, 0).wait()
            add(gown.at[grp, path, 0], first_in.at[grp, path, 0], span)
            second(grp, path).start()
            first(grp, path, 1).wait_recv()
            gload(grp, path, 1).wait()
            add(gown.at[grp, path, 1], first_in.at[grp, path, 1], span)

    def grads_second(grp):
        for path in range(2):
            second(grp, path).wait_recv()
            add(gown.at[grp, path, 1], second_in.at[grp, path], span)
            for k in range(1, ways):
                share(grp, path, k).start()
            keep(grp, path).start()

    def last(a):
        for s in range(PIECES):
            out[a, part(core, s), :] = acc[a, me, s]
            finish(a, s).start()

    merge(0)
    small_step(0)
    merge(1)
    small_step(1)
    for k in range(1, ways):
        hop(0, k)
        if k == 1:
            small_step(2)
        if k - 1 < groups:
            grads_first(k - 1)
        hop(1, k)
        if 0 <= k - 2 < groups:
            grads_second(k - 2)
    last(0)
    last(1)
    grads_second(groups - 1)

    for i in range(3):
        small_send(i).wait_send()
    for k in range(1, ways):
        small_all(k).wait()
    for a in range(2):
        for s in range(PIECES):
            finish(a, s).wait_send()
            remote(
                out.at[a, part(1 - core, s), :],
                out.at[a, part(1 - core, s), :],
                os.at[a, s],
                orr.at[a, s],
                (dp, me, 1 - core),
            ).wait_recv()
            for d in range(ways):
                swap(a, d, s).wait_send()
                pl.when(d > me)(lambda: stream(a, d, s, 1).wait_send())
                pl.when(d < me)(lambda: stream(a, d, s, 0).wait_send())
    for grp in range(groups):
        for path in range(2):
            for i in range(2):
                first(grp, path, i).wait_send()
            second(grp, path).wait_send()
            keep(grp, path).wait()
            for k in range(1, ways):
                share(grp, path, k).wait()


def scatter(out_part, normed_part, weight_part, small):
    ways = lax.axis_size("ctx")
    chips = lax.axis_size("dp")
    width = out_part.shape[1]
    rows = out_part.shape[0] // ways
    groups, cols = weight_part.shape[0], weight_part.shape[-1]
    span = width // chips
    depth = span // ways
    piece = rows // 2 // PIECES
    lanes = cols // 2
    dma = pltpu.SemaphoreType.DMA
    anywhere = pl.BlockSpec(memory_space=pl.ANY)
    inside = pl.BlockSpec(memory_space=pltpu.VMEM)
    stack = pltpu.VMEM((2, ways, PIECES, piece, width), BF16)
    out, gwo, smallo = pl.pallas_call(
        functools.partial(scatter_body, ways),
        in_specs=[anywhere] * 3 + [inside],
        out_specs=[inside, anywhere, inside],
        out_shape=[
            jax.ShapeDtypeStruct((2, rows, width), BF16),
            jax.ShapeDtypeStruct((groups, ways, depth, cols), BF16),
            jax.ShapeDtypeStruct((ways,) + small.shape, F32),
        ],
        scratch_shapes=[
            stack,
            stack,
            stack,
            stack,
            pltpu.VMEM((groups, 2, 2, span, lanes), BF16),
            pltpu.VMEM((groups, 2, 2, span, lanes), BF16),
            pltpu.VMEM((groups, 2, span, lanes), BF16),
            dma((2, ways, PIECES)),
            dma((2, ways, PIECES)),
            dma((2, 2, ways, PIECES)),
            dma((2, 2, ways, PIECES)),
            dma((groups, 2, 2)),
            dma((groups, 2, 2)),
            dma((groups, 2)),
            dma((groups, 2)),
            dma((groups, 2, ways)),
            dma((groups, 2, ways)),
            dma((2, PIECES)),
            dma((2, PIECES)),
            dma((2, ways, PIECES)),
            dma((groups, 2, 2)),
            pltpu.VMEM((3,) + small.shape, F32),
            pltpu.VMEM((3,) + small.shape, F32),
            dma((2 + ways,)),
            dma((2 + ways,)),
        ],
        compiler_params=pltpu.CompilerParams(
            collective_id=1, has_side_effects=True, vmem_limit_bytes=56 * MIB
        ),
    )(
        out_part.reshape(ways, rows, width),
        normed_part.reshape(ways, rows, width),
        weight_part.reshape(groups, chips, span, cols),
        small,
    )
    return out[0].astype(F32), out[1].astype(F32), gwo.astype(F32), smallo


def layer_norm(x):
    xf = x.astype(F32)
    mean = jnp.mean(xf, -1, keepdims=True)
    centred = xf - mean
    inv_std = lax.rsqrt(jnp.mean(centred * centred, -1, keepdims=True) + EPS)
    return centred * inv_std, inv_std


def plain_work(x, g, wsrc, places, segments, gain, shift, fc1_shift, qkv_shift):
    me, ways = lax.axis_index("ctx"), lax.axis_size("ctx")
    width = x.shape[1]
    unused, unused, depth, cols = wsrc.shape
    head_cols = cols // 4
    x_all, g_all, weights, places, segments = gather_plain(x, g, wsrc, places, segments)
    weights = weights.reshape(3, width, cols)
    w1, w2, wa = weights[0], weights[1], weights[2]
    wp, wd = wa[:, : 3 * head_cols], wa[:, 3 * head_cols :]
    x_hat, unused = layer_norm(x_all)
    normed = (x_hat * gain + shift).astype(BF16)
    projected = dot_nn(normed, wp) + qkv_shift.reshape(1, 3 * head_cols)
    mix_grad = dot_nn(g_all, wd).astype(BF16)
    attend = attention if head_cols % 128 == 0 else attention_plain
    mixture, gq, gk, gv = attend(
        projected[:, :head_cols],
        projected[:, head_cols : 2 * head_cols],
        projected[:, 2 * head_cols :],
        mix_grad,
        places,
        segments,
    )
    proj_grad = jnp.concatenate([gq, gk, gv], 1)

    hidden_pre = dot_nn(normed, w1) + fc1_shift
    hidden, slope = gelu_and_slope(hidden_pre)
    hidden = hidden.astype(BF16)
    hidden_grad = (dot_nn(g_all, w2) * slope).astype(BF16)

    out_part = (dot_nt(mixture, wd) + dot_nt(hidden, w2)).astype(BF16)
    normed_part = dot_nt(proj_grad, wp) + dot_nt(hidden_grad, w1)
    weight_part = jnp.stack(
        [
            dot_tn(normed, hidden_grad).astype(BF16),
            dot_tn(g_all, hidden).astype(BF16),
            jnp.concatenate([dot_tn(normed, proj_grad), dot_tn(g_all, mixture)], 1).astype(BF16),
        ]
    )
    qkv_bias_part = jnp.sum(proj_grad.astype(F32), 0).reshape(3, head_cols)
    fc1_bias_part = jnp.sum(hidden_grad.astype(F32), 0)
    branches, normed_grad, weight_grads = scatter_plain(
        out_part, normed_part.astype(BF16), weight_part.reshape(3, -1, depth, cols)
    )
    place = lambda t, whole, axis: lax.dynamic_update_slice_in_dim(
        jnp.zeros(whole, F32), t, me * t.shape[axis], axis
    )
    small = lax.psum(
        (
            place(qkv_bias_part, (3, head_cols * ways), 1),
            place(fc1_bias_part, (cols * ways,), 0),
            jnp.sum(g.astype(F32), 0),
        ),
        ("dp", "ctx"),
    )
    norms = lax.psum(
        (jnp.sum(normed_part * x_hat, 0), jnp.sum(normed_part, 0)), ("dp", "ctx", "tp")
    )
    return branches, normed_grad, weight_grads, norms + small


def fast_work(x, g, wsrc, places, segments, gain, shift, fc1_shift, qkv_shift):
    ways = lax.axis_size("ctx")
    rows, width = x.shape
    unused, unused, depth, cols = wsrc.shape
    head_cols = cols // 4
    g_all, ids, normed, x_hat, hidden, hidden_grad, out_mlp, back_mlp, projected, mix_grad, wa, fc1_sum, unused = forward(
        x, g, wsrc, places, segments, gain, shift, fc1_shift, qkv_shift
    )
    flat = lambda t: t.reshape(ways * rows, t.shape[-1])
    g_all, normed, x_hat, hidden, hidden_grad = map(flat, (g_all, normed, x_hat, hidden, hidden_grad))
    out_mlp, back_mlp, projected, mix_grad = map(flat, (out_mlp, back_mlp, projected, mix_grad))
    ids = ids[:, :2].transpose(1, 0, 2).reshape(2, ways * rows)
    wp, wd = wa[:, : 3 * head_cols], wa[:, 3 * head_cols :]
    mixture, gq, gk, gv = attention(
        projected[:, :head_cols],
        projected[:, head_cols : 2 * head_cols],
        projected[:, 2 * head_cols :],
        mix_grad,
        ids[0],
        ids[1],
    )
    proj_grad = jnp.concatenate([gq, gk, gv], 1)
    out_part = (dot_nt(mixture, wd) + out_mlp.astype(F32)).astype(BF16)
    normed_part = dot_nt(proj_grad, wp) + back_mlp.astype(F32)
    weight_part = jnp.stack(
        [
            dot_tn(normed, hidden_grad).astype(BF16),
            dot_tn(g_all, hidden).astype(BF16),
            jnp.concatenate([dot_tn(normed, proj_grad), dot_tn(g_all, mixture)], 1).astype(BF16),
        ]
    )
    qkv_sum = jnp.sum(proj_grad.astype(F32), 0)
    line = lambda t: jnp.pad(t.reshape(-1), (0, width - t.size))
    small = jnp.stack(
        [
            jnp.sum(normed_part * x_hat.astype(F32), 0),
            jnp.sum(normed_part, 0),
            jnp.sum(g.astype(F32), 0),
            line(fc1_sum),
            line(qkv_sum),
        ]
        + [jnp.zeros((width,), F32)] * 3
    )
    branches, normed_grad, weight_grads, sums = scatter(
        out_part, normed_part.astype(BF16), weight_part, small
    )
    total = jnp.sum(sums[:, :3], 0)
    fc1_bias_sum = sums[:, 3, :cols].reshape(ways * cols)
    qkv_bias_sum = sums[:, 4, : 3 * head_cols].reshape(ways, 3, head_cols).transpose(1, 0, 2)
    return (
        branches,
        normed_grad,
        weight_grads,
        (total[0], total[1], qkv_bias_sum.reshape(3, ways * head_cols), fc1_bias_sum, total[2]),
    )


def per_device(
    block_input,
    cotangent,
    segment_ids,
    positions,
    norm_gain,
    norm_bias,
    w_qkv,
    qkv_bias,
    w_dense,
    w_fc1,
    fc1_bias,
    w_fc2,
    out_bias,
):
    ways = lax.axis_size("ctx")
    me = lax.axis_index("ctx")
    x, g = block_input[0], cotangent[0]
    rows, width = x.shape
    depth = w_fc1.shape[0]
    cols = w_fc1.shape[1] // ways
    head_cols = w_qkv.shape[2] // ways

    fc1 = w_fc1.reshape(depth, ways, cols).transpose(1, 0, 2)
    fc2 = w_fc2.reshape(ways, cols, depth).transpose(0, 2, 1)
    qkv = w_qkv.reshape(3, depth, ways, head_cols).transpose(2, 1, 0, 3)
    dense = w_dense.reshape(ways, head_cols, depth).transpose(0, 2, 1)
    att = jnp.concatenate([qkv.reshape(ways, depth, 3 * head_cols), dense], -1)
    wsrc = jnp.stack([fc1, fc2, att])

    gain, shift = norm_gain.astype(F32), norm_bias.astype(F32)
    qkv_shift = lax.dynamic_slice_in_dim(qkv_bias, me * head_cols, head_cols, 1).astype(F32)
    fc1_shift = lax.dynamic_slice_in_dim(fc1_bias, me * cols, cols, 0).astype(F32)
    fast = ways == 4 and lax.axis_size("dp") == 4 and rows % 64 == 0 and head_cols % 128 == 0
    work = fast_work if fast else plain_work
    branches, normed_grad, weight_grads, sums = work(
        x, g, wsrc, positions[0], segment_ids[0], gain, shift, fc1_shift, qkv_shift
    )

    gf = g.astype(F32)
    output = (x.astype(F32) + branches + out_bias.astype(F32)).astype(BF16)
    own_hat, inv_std = layer_norm(x)
    scaled = normed_grad * gain
    grad_input = gf + inv_std * (
        scaled
        - jnp.mean(scaled, -1, keepdims=True)
        - own_hat * jnp.mean(scaled * own_hat, -1, keepdims=True)
    )
    gain_sum, shift_sum, qkv_bias_sum, fc1_bias_sum, out_bias_sum = sums

    grad_fc1 = weight_grads[0].transpose(1, 0, 2).reshape(depth, ways * cols)
    grad_fc2 = weight_grads[1].transpose(0, 2, 1).reshape(ways * cols, depth)
    grad_att = weight_grads[2].reshape(ways, depth, 4, head_cols)
    grad_qkv = grad_att[:, :, :3].transpose(2, 1, 0, 3).reshape(3, depth, ways * head_cols)
    grad_dense = grad_att[:, :, 3].transpose(0, 2, 1).reshape(ways * head_cols, depth)
    return (
        output[None],
        grad_input.astype(BF16)[None],
        gain_sum,
        shift_sum,
        grad_qkv,
        qkv_bias_sum,
        grad_dense,
        grad_fc1,
        fc1_bias_sum,
        grad_fc2,
        out_bias_sum,
    )


def solution(mesh):
    placed = (
        P("dp", "ctx", None),
        P("dp", "ctx", None),
        P("dp", "ctx"),
        P("dp", "ctx"),
        P(),
        P(),
        P(None, ("dp", "ctx"), "tp"),
        P(None, "tp"),
        P("tp", ("dp", "ctx")),
        P(("dp", "ctx"), "tp"),
        P("tp"),
        P("tp", ("dp", "ctx")),
        P(),
    )
    return jax.shard_map(
        per_device,
        mesh=mesh,
        in_specs=placed,
        out_specs=(
            P("dp", "ctx", None),
            P("dp", "ctx", None),
            P(),
            P(),
            P(None, ("dp", "ctx"), "tp"),
            P(None, "tp"),
            P("tp", ("dp", "ctx")),
            P(("dp", "ctx"), "tp"),
            P("tp"),
            P("tp", ("dp", "ctx")),
            P(),
        ),
        check_vma=False,
    )
```

```python
import functools
import math

import jax
import jax.numpy as jnp
from jax import lax
from jax.experimental import pallas as pl
from jax.experimental.pallas import tpu as pltpu
from jax.sharding import PartitionSpec as P

HD = 64
ROT = 32
EPS = 1e-05
MIB = 1 << 20
F32 = jnp.float32
BF16 = jnp.bfloat16
MESH = pl.DeviceIdType.MESH


def dot_nn(a, b):
    return lax.dot_general(a, b, (((1,), (0,)), ((), ())), preferred_element_type=F32)


def dot_nt(a, b):
    return lax.dot_general(a, b, (((1,), (1,)), ((), ())), preferred_element_type=F32)


def dot_tn(a, b):
    return lax.dot_general(a, b, (((0,), (0,)), ((), ())), preferred_element_type=F32)


QUERIES = 256


def frequencies():
    half = ROT // 2
    one = jnp.concatenate(
        [10000.0 ** (-(jnp.arange(half, dtype=F32) * 2.0 / ROT))] * 2 + [jnp.zeros(HD - ROT, F32)]
    )
    return jnp.concatenate([one, one])[None, :]


def turn(v, cos, sin):
    half = ROT // 2
    lane = lax.broadcasted_iota(jnp.int32, v.shape, 1) % HD
    left, right = pltpu.roll(v, 128 - half, 1), pltpu.roll(v, half, 1)
    return v * cos + jnp.where(lane < half, -left, right) * sin


def allowed_keys(labr, labc, i):
    shape = (QUERIES, (i + 1) * QUERIES)
    row = lax.broadcasted_iota(jnp.int32, shape, 0) + i * QUERIES
    col = lax.broadcasted_iota(jnp.int32, shape, 1)
    here = pl.ds(i * QUERIES, QUERIES)
    return (col <= row) & (labc[here, 1:2] == labr[1:2, 0 : (i + 1) * QUERIES])


def attention_plain(pq, pk, pv, mg, places, segments):
    rows, cols = pq.shape
    heads = cols // HD
    half = ROT // 2
    scale = 1.0 / math.sqrt(HD)
    frequency = 10000.0 ** (-(jnp.arange(half, dtype=F32) * 2.0 / ROT))
    angles = places.astype(F32)[:, None] * frequency[None, :]
    cos, sin = jnp.cos(angles)[:, None, :], jnp.sin(angles)[:, None, :]

    def rotate(t, s):
        t = t.reshape(rows, heads, HD)
        a, b = t[..., :half], t[..., half:ROT]
        return jnp.concatenate([a * cos - b * s, b * cos + a * s, t[..., ROT:]], -1)

    q = rotate(pq, sin).astype(BF16)
    k = rotate(pk, sin).astype(BF16)
    v = pv.astype(BF16).reshape(rows, heads, HD)
    m = mg.reshape(rows, heads, HD)
    span = 256
    index = jnp.arange(rows, dtype=jnp.int32)

    def step(carry, items):
        dk, dv = carry
        qi, mi, row_index, row_seg = items
        scores = jnp.einsum("qhd,khd->hqk", qi, k, preferred_element_type=F32) * scale
        allowed = (index[None, :] <= row_index[:, None]) & (segments[None, :] == row_seg[:, None])
        scores = jnp.where(allowed[None], scores, -1e30)
        expo = jnp.exp(scores - jnp.max(scores, -1, keepdims=True))
        probs = expo / jnp.sum(expo, -1, keepdims=True)
        low = probs.astype(BF16)
        out = jnp.einsum("hqk,khd->qhd", low, v, preferred_element_type=F32).astype(BF16)
        prob_grad = jnp.einsum("qhd,khd->hqk", mi, v, preferred_element_type=F32)
        delta = jnp.sum(probs * prob_grad, -1, keepdims=True)
        score_grad = (probs * (prob_grad - delta)).astype(BF16)
        dq = jnp.einsum("hqk,khd->qhd", score_grad, k, preferred_element_type=F32) * scale
        dk = dk + jnp.einsum("hqk,qhd->khd", score_grad, qi, preferred_element_type=F32) * scale
        dv = dv + jnp.einsum("hqk,qhd->khd", low, mi, preferred_element_type=F32)
        return (dk, dv), (out, dq)

    zero = jnp.zeros((rows, heads, HD), F32)
    cut = lambda t: t.reshape((rows // span, span) + t.shape[1:])
    (dk, dv), (out, dq) = lax.scan(step, (zero, zero), (cut(q), cut(m), cut(index), cut(segments)))
    flat = lambda t: t.reshape(rows, cols)
    return (
        flat(out),
        flat(rotate(dq.reshape(rows, cols), -sin)).astype(BF16),
        flat(rotate(dk.reshape(rows, cols), -sin)).astype(BF16),
        flat(dv).astype(BF16),
    )


def gather_plain(x, g, wsrc, places, segments):
    pieces = lax.all_to_all(wsrc, "ctx", split_axis=1, concat_axis=1, tiled=True)
    weights = lax.all_gather(pieces, "dp", axis=1, tiled=True)
    along = lambda t: lax.all_gather(t, "ctx", axis=0, tiled=True)
    return along(x), along(g), weights, along(places), along(segments)


def scatter_plain(out_part, normed_part, weight_part):
    summed = lambda t: lax.psum(
        lax.psum_scatter(t, "ctx", scatter_dimension=0, tiled=True), "tp"
    ).astype(F32)
    pieces = lax.psum_scatter(weight_part, "dp", scatter_dimension=1, tiled=True)
    pieces = lax.all_to_all(pieces, "ctx", split_axis=1, concat_axis=1, tiled=True)
    return summed(out_part), summed(normed_part), pieces.astype(F32)


def place_of():
    dp, me, core = lax.axis_index("dp"), lax.axis_index("ctx"), lax.axis_index("tp")
    return dp, me, core, dp + 1 - 2 * (dp % 2), dp + 2 - 4 * (dp // 2)


def greet(ways):
    dp, me, core, dpx, dpy = place_of()
    barrier = pltpu.get_barrier_semaphore()
    for device in [(dp, me, 1 - core), (dpx, me, core), (dpy, me, core)] + [
        (dp, (me + k) % ways, core) for k in range(1, ways)
    ]:
        pl.semaphore_signal(barrier, inc=1, device_id=device, device_id_type=MESH)
    pl.semaphore_wait(barrier, ways + 2)


def remote(src, dst, send, recv, device):
    return pltpu.make_async_remote_copy(
        src_ref=src, dst_ref=dst, send_sem=send, recv_sem=recv, device_id=device, device_id_type=MESH
    )


PIECES = 2


def gelu_and_slope(v):
    c = math.sqrt(2.0 / math.pi)
    square = v * v
    tanh = jnp.tanh(c * v * (1.0 + 0.044715 * square))
    half = 0.5 * (1.0 + tanh)
    slope = half + 0.5 * c * v * (1.0 - tanh * tanh) * (1.0 + 3.0 * 0.044715 * square)
    return v * half, slope


def forward_body(
    ways, x, g, w, ids, gain, shift, fc1_shift, qkv_shift, freq,
    go, no, xho, ho, hgo, outo, ngo, mgo, wao, qo, ko, vo, mixo, lseo, coso, sino, ido, biaso,
    xo, wv, norm, xb, gb, pre, hid, slope, hgb, ob, nb, mb, qb, kb, vb, mixb, lse, cosb, sinb, labr, labc,
    zs, zr, ts, tr, ws, wr, ls, lr, ds, dr, ids_s, ids_r, own, ls_in, ls_out, keep_out,
):
    dp, me, core, dpx, dpy = place_of()
    rows, width = x.shape
    piece = rows // 2 // PIECES
    groups, unused, depth, cols = w.shape
    head_cols = cols // 4
    srcs, outs = (x, g), (xo, go)
    blocks = [me, 1 + me % 2, None, 3 * (1 - me // 2)]
    blocks[2] = 6 - me - blocks[1] - blocks[3]

    def part(which, s):
        return pl.ds(pl.multiple_of(which * (rows // 2) + s * piece, 16), piece)

    def along(a, owner, s, side, mine=False):
        at = part(core, s)
        src = srcs[a].at[at, :] if mine else outs[a].at[owner, at, :]
        return remote(
            src,
            outs[a].at[owner, at, :],
            zs.at[side, a, owner, s],
            zr.at[a, owner, s],
            (dp, me - 1 + 2 * side, core),
        )

    def across(a, owner, s, which):
        at = part(which, s)
        ref = outs[a].at[owner, at, :]
        return remote(ref, ref, ts.at[a, owner, s], tr.at[a, owner, s], (dp, me, 1 - core))

    def rows_of(chip, j):
        return pl.ds(pl.multiple_of((chip * ways + j) * depth, 16), depth)

    def share(grp, k):
        return remote(
            w.at[grp, (me + k) % ways],
            wv.at[grp, rows_of(dp, me), :],
            ws.at[grp, k],
            wr.at[grp, k],
            (dp, (me + k) % ways, core),
        )

    def source(k):
        return (me - k + ways) % ways

    def spread(grp, k, axis):
        at = rows_of(dp, source(k))
        return remote(
            w.at[grp, me] if k == 0 else wv.at[grp, at, :],
            wv.at[grp, at, :],
            ls.at[axis, grp, k],
            lr.at[axis, grp, k],
            ((dpx, dpy)[axis], me, core),
        )

    def corner(grp, k):
        axis = (grp + k) % 2
        ref = wv.at[grp, rows_of((dpx, dpy)[axis], source(k)), :]
        return remote(ref, ref, ds.at[grp, k], dr.at[grp, k], ((dpy, dpx)[axis], me, core))

    def labels(k):
        return remote(ids, ido.at[me], ids_s.at[k], ids_r.at[k], (dp, (me + k) % ways, core))

    def send_own(a):
        for s in range(PIECES):
            pl.when(me > 0)(lambda: along(a, me, s, 0, True).start())
            pl.when(me < ways - 1)(lambda: along(a, me, s, 1, True).start())

    def send_shares(grp):
        for k in range(1, ways):
            share(grp, k).start()
        for axis in range(2):
            spread(grp, 0, axis).start()

    def pass_on(a, k):
        for s in range(PIECES):

            @pl.when(me + k < ways)
            def _():
                along(a, me + k, s, 0).wait_recv()
                pl.when(me > 0)(lambda: along(a, me + k, s, 0).start())
                across(a, me + k, s, core).start()

            @pl.when(me - k >= 0)
            def _():
                along(a, me - k, s, 1).wait_recv()
                pl.when(me < ways - 1)(lambda: along(a, me - k, s, 1).start())
                across(a, me - k, s, core).start()

    def spread_on(grp, k):
        share(grp, k).wait_recv()
        for axis in range(2):
            spread(grp, k, axis).start()

    def corner_on(grp, k):
        axis = (grp + k) % 2
        spread(grp, k, axis).wait_recv()
        corner(grp, k).start()

    def settle(grp):
        keeps[grp].wait()
        for k in range(ways):
            spread(grp, k, 1 - (grp + k) % 2).wait_recv()
            corner(grp, k).wait_recv()

    def arrive(a, t):
        if t:
            for s in range(PIECES):
                across(a, blocks[t], s, 1 - core).wait_recv()

    def loop(count, body):
        lax.fori_loop(0, count, lambda i, c: (body(i), c)[1], 0)

    def load_x(t):
        src = x if t == 0 else xo.at[blocks[t]]
        return pltpu.make_async_copy(src, xb.at[t % 2], ls_in.at[0, t])

    def load_g(t):
        src = g if t == 0 else go.at[blocks[t]]
        return pltpu.make_async_copy(src, gb.at[t % 2], ls_in.at[1, t])

    def store(which, t):
        o = blocks[t]
        src, dst = (
            (xb.at[t % 2], xho.at[o]),
            (norm.at[o], no.at[o]),
            (hid.at[o], ho.at[o]),
            (ob.at[t % 2], outo.at[o]),
            (nb.at[t % 2], ngo.at[o]),
            (hgb.at[t % 2], hgo.at[o]),
            (mb.at[t], mgo.at[o]),
        )[which]
        return pltpu.make_async_copy(src, dst, ls_out.at[which, t])

    def normalise(t):
        arrive(0, t)
        if t >= 2:
            store(0, t - 2).wait()
        load_x(t).start()
        load_x(t).wait()
        step = 32

        def body(i):
            at = pl.ds(pl.multiple_of(i * step, step), step)
            xf = xb[t % 2, at, :].astype(F32)
            centred = xf - jnp.mean(xf, -1, keepdims=True)
            inv_std = lax.rsqrt(jnp.mean(centred * centred, -1, keepdims=True) + EPS)
            x_hat = centred * inv_std
            norm[blocks[t], at, :] = (x_hat * gain[...] + shift[...]).astype(BF16)
            xb[t % 2, at, :] = x_hat.astype(BF16)

        loop(rows // step, body)
        store(0, t).start()
        store(1, t).start()

    wide = 512

    def span(i):
        return pl.ds(pl.multiple_of(i * wide, wide), wide)

    def up(t):
        o = blocks[t]

        def mul(i):
            pre[:, span(i)] = dot_nn(norm[o], wv[0, :, span(i)]) + fc1_shift[:, span(i)]

        loop(cols // wide, mul)

        def act(i):
            at = pl.ds(pl.multiple_of(i * 16, 16), 16)
            value, grad = gelu_and_slope(pre[at, :])
            hid[o, at, :] = value.astype(BF16)
            slope[o, at, :] = grad

        loop(rows // 16, act)
        store(2, t).start()

    def tables():
        for k in range(1, ways):
            labels(k).wait_recv()
        keeps[groups + 1].wait()
        lse[...] = jnp.zeros_like(lse)
        for o in range(ways):
            at = slice(o * rows, (o + 1) * rows)
            rows_here = ido[o].astype(F32)
            labr[:, at] = rows_here
            columns = jnp.transpose(rows_here)
            labc[at, :] = columns
            angles = columns[:, 0:1] * freq[...]
            cosb[at, :] = jnp.cos(angles)
            sinb[at, :] = jnp.sin(angles)
        for copy in table_stores:
            copy.start()

    def project(t):
        o = blocks[t]
        at = pl.ds(pl.multiple_of(o * rows, 16), rows)
        cos, sin = cosb[at, :], sinb[at, :]
        for pair in range(head_cols // 128):
            lanes = pl.ds(pair * 128, 128)
            for which, ref in enumerate((qb, kb, vb)):
                wide_lanes = pl.ds(which * head_cols + pair * 128, 128)
                v = dot_nn(norm[o], wv[2, :, wide_lanes]) + qkv_shift[:, wide_lanes]
                if which < 2:
                    v = turn(v, cos, sin)
                v = v.astype(BF16)
                ref[at, lanes] = v * BF16(1.0 / math.sqrt(HD)) if which == 0 else v

    def attend(pair, i):
        lanes = pl.ds(pair * 128, 128)
        here, seen = pl.ds(i * QUERIES, QUERIES), pl.ds(0, (i + 1) * QUERIES)
        allowed = allowed_keys(labr, labc, i)
        first = lax.broadcasted_iota(jnp.int32, (QUERIES, 128), 1) < HD
        lane = lax.broadcasted_iota(jnp.int32, (QUERIES, 128), 1)
        keys, values = kb[seen, lanes], vb[seen, lanes]
        outs_of, logs = [], lse[here, :]
        for sub in range(2):
            mine = first if sub == 0 else ~first
            scores = dot_nt(jnp.where(mine, qb[here, lanes], 0), keys)
            scores = jnp.where(allowed, scores, -1e30)
            top = jnp.max(scores, 1, keepdims=True)
            expo = jnp.exp(scores - top)
            total = jnp.sum(expo, 1, keepdims=True)
            outs_of.append(dot_nn((expo * (1.0 / total)).astype(BF16), values))
            logs = jnp.where(lane == pair * 2 + sub, top + jnp.log(total), logs)
        lse[here, :] = logs
        mixb[here, lanes] = jnp.where(first, outs_of[0], outs_of[1]).astype(BF16)

    def down(t):
        if t >= 2:
            store(3, t - 2).wait()
        o = blocks[t]
        at = pl.ds(pl.multiple_of(o * rows, 16), rows)

        def mul(i):
            total = dot_nt(hid[o], wv[1, span(i), :])
            total = total + dot_nt(mixb[at, :], wv[2, span(i), 3 * head_cols :])
            ob[t % 2, :, span(i)] = total.astype(BF16)

        loop(width // wide, mul)
        store(3, t).start()

    def back(t):
        arrive(1, t)
        load_g(t).start()
        if t >= 2:
            store(4, t - 2).wait()
            store(5, t - 2).wait()
        load_g(t).wait()
        o = blocks[t]

        def mul(i):
            act = dot_nn(gb[t % 2], wv[1, :, span(i)])
            grad = (act * slope[o, :, span(i)]).astype(BF16)
            hgb[t % 2, :, span(i)] = grad
            total = jnp.sum(grad.astype(F32), 0, keepdims=True)
            biaso[:, span(i)] = total if t == 0 else biaso[:, span(i)] + total

        loop(cols // wide, mul)
        store(5, t).start()

        def mul_back(i):
            nb[t % 2, :, span(i)] = dot_nt(hgb[t % 2], wv[0, span(i), :]).astype(BF16)

        loop(width // wide, mul_back)
        store(4, t).start()
        mb[t] = dot_nn(gb[t % 2], wv[2, :, 3 * head_cols :]).astype(BF16)
        store(6, t).start()

    greet(ways)
    send_own(0)
    send_shares(0)
    send_shares(1)
    for k in range(1, ways):
        labels(k).start()
    keeps = [
        pltpu.make_async_copy(w.at[i, me], wv.at[i, rows_of(dp, me), :], own.at[i])
        for i in range(groups)
    ] + [
        pltpu.make_async_copy(g, go.at[me], own.at[groups]),
        pltpu.make_async_copy(ids, ido.at[me], own.at[groups + 1]),
    ]
    for copy in keeps:
        copy.start()
    wa_out = pltpu.make_async_copy(wv.at[2], wao, own.at[groups + 2])
    stores = [
        pltpu.make_async_copy(src, dst, keep_out.at[i])
        for i, (src, dst) in enumerate(
            ((cosb, coso), (sinb, sino), (qb, qo), (kb, ko), (vb, vo), (mixb, mixo), (lse, lseo))
        )
    ]
    table_stores, state_stores = stores[:2], stores[2:]
    steps = dict(
        S=send_shares,
        G=lambda: send_own(1),
        W=wa_out.start,
        Z=lambda: [copy.start() for copy in state_stores],
        x=lambda k: pass_on(0, k),
        g=lambda k: pass_on(1, k),
        s=spread_on,
        c=corner_on,
        e=settle,
        l=tables,
        n=normalise,
        u=up,
        p=project,
        a=attend,
        d=down,
        b=back,
    )
    plan = (
        "n0", "s01", "c00", "x1", "S2", "n1", "s02", "c01", "s03", "c02", "x2", "G", "n2", "c03",
        "l", "s11", "c10", "s12", "c11", "s13", "c12", "x3", "n3", "e0", "u0", "c13", "s21", "c20",
        "u1", "s22", "c21", "u2", "g1", "s23", "c22", "u3", "c23", "e2", "W", "p0", "p1", "p2",
        "p3", "a00", "a01", "a02", "a03", "g2", "a04", "a05", "a10", "a11", "a12", "a13", "a14",
        "a15", "Z", "e1", "d0", "b0", "d1", "b1", "g3", "d2", "d3", "b2", "b3",
    )
    for word in plan:
        steps[word[0]](*(int(digit) for digit in word[1:]))
    keeps[groups].wait()

    for k in range(1, ways):
        labels(k).wait_send()
    for copy in table_stores + state_stores:
        copy.wait()
    wa_out.wait()
    for t in range(4):
        for which in (1, 2, 6):
            store(which, t).wait()
        if t >= 2:
            for which in (0, 3, 4, 5):
                store(which, t).wait()
    for a in range(2):
        for owner in range(ways):
            for s in range(PIECES):

                @pl.when(owner != me)
                def _():
                    across(a, owner, s, core).wait_send()

                @pl.when((me > 0) & (owner >= me))
                def _():
                    along(a, owner, s, 0).wait_send()

                @pl.when((me < ways - 1) & (owner <= me))
                def _():
                    along(a, owner, s, 1).wait_send()

    for grp in range(groups):
        for k in range(ways):
            if k:
                share(grp, k).wait_send()
            for axis in range(2):
                spread(grp, k, axis).wait_send()
            corner(grp, k).wait_send()


def forward(x, g, wsrc, ids, gain, shift, fc1_shift, qkv_shift):
    ways = lax.axis_size("ctx")
    rows, width = x.shape
    groups, unused, depth, cols = wsrc.shape
    head_cols = cols // 4
    dma = pltpu.SemaphoreType.DMA
    vmem = pltpu.VMEM
    anywhere = pl.BlockSpec(memory_space=pl.ANY)
    inside = pl.BlockSpec(memory_space=pltpu.VMEM)
    seq = lambda n, dtype=BF16: jax.ShapeDtypeStruct((ways, rows, n), dtype)
    tokens = ways * rows
    line = lambda n, dtype: jax.ShapeDtypeStruct((tokens, n), dtype)
    outs = pl.pallas_call(
        functools.partial(forward_body, ways),
        in_specs=[anywhere] * 4 + [inside] * 5,
        out_specs=[anywhere] * 16 + [inside] * 2 + [anywhere],
        out_shape=[
            seq(width),
            seq(width),
            seq(width),
            seq(cols),
            seq(cols),
            seq(width),
            seq(width),
            seq(head_cols),
            jax.ShapeDtypeStruct((width, cols), BF16),
            line(head_cols, BF16),
            line(head_cols, BF16),
            line(head_cols, BF16),
            line(head_cols, BF16),
            line(128, F32),
            line(128, F32),
            line(128, F32),
            jax.ShapeDtypeStruct((ways, 8, rows), jnp.int32),
            jax.ShapeDtypeStruct((1, cols), F32),
            seq(width),
        ],
        scratch_shapes=[
            vmem((groups, width, cols), BF16),
            vmem((ways, rows, width), BF16),
            vmem((2, rows, width), BF16),
            vmem((2, rows, width), BF16),
            vmem((rows, cols), F32),
            vmem((ways, rows, cols), BF16),
            vmem((ways, rows, cols), F32),
            vmem((2, rows, cols), BF16),
            vmem((2, rows, width), BF16),
            vmem((2, rows, width), BF16),
            vmem((ways, rows, head_cols), BF16),
            vmem((tokens, head_cols), BF16),
            vmem((tokens, head_cols), BF16),
            vmem((tokens, head_cols), BF16),
            vmem((tokens, head_cols), BF16),
            vmem((tokens, 128), F32),
            vmem((tokens, 128), F32),
            vmem((tokens, 128), F32),
            vmem((8, tokens), F32),
            vmem((tokens, 8), F32),
            dma((2, 2, ways, PIECES)),
            dma((2, ways, PIECES)),
            dma((2, ways, PIECES)),
            dma((2, ways, PIECES)),
            dma((groups, ways)),
            dma((groups, ways)),
            dma((2, groups, ways)),
            dma((2, groups, ways)),
            dma((groups, ways)),
            dma((groups, ways)),
            dma((ways,)),
            dma((ways,)),
            dma((3 + groups,)),
            dma((2, ways)),
            dma((7, ways)),
            dma((7,)),
        ],
        compiler_params=pltpu.CompilerParams(
            collective_id=0, has_side_effects=True, vmem_limit_bytes=62 * MIB
        ),
    )(
        x, g, wsrc, ids,
        gain.reshape(1, width), shift.reshape(1, width), fc1_shift.reshape(1, cols),
        qkv_shift.reshape(1, 3 * head_cols), frequencies(),
    )
    return outs


def backward_body(
    ways,
    p0, ngm, normed, xh, g, hg, hidden, q, k, v, mg, mix, lse, cos, sin, wa, labels, small,
    out, gwo, tin, smallo,
    lt, ra, rb, wp, qv, kv, vv, mgv, lsev, cosv, sinv, dkv, dvv, labr, labc,
    acc, zin, tst, ngi, xhi, ngs, gown, gsend, first_in, second_in, sums, sum_in, sum_out,
    tps, tpr, zs, zr, fs, fr, ss, sr, ws, wr, os, orr, loc, tloc, sms, smr, ins, lts, ngl,
):
    dp, me, core, dpx, dpy = place_of()
    rows, width = out.shape[1:]
    half = rows // 2
    piece = half // PIECES
    groups = first_in.shape[0]
    span_rows = gown.shape[3]
    lanes = gown.shape[4]
    depth = span_rows // ways
    head_cols = q.shape[1]
    nxt = (dpx, dpy)
    far = dpx + dpy - dp
    scale = 1.0 / math.sqrt(HD)

    order = (0, 3, 1, 2)

    def part(which, s):
        return pl.ds(pl.multiple_of(which * half + s * piece, 16), piece)

    def loop(count, body):
        lax.fori_loop(0, count, lambda i, c: (body(i), c)[1], 0)

    def add(dst, src, height):
        step = 32

        def body(i):
            at = pl.ds(pl.multiple_of(i * step, step), step)
            dst[at, :] = dst[at, :] + src[at, :]

        loop(height // step, body)

    def swap(a, d, s):
        at = pl.ds(s * piece, piece)
        src = p0.at[d, part(1 - core, s), :] if a == 0 else ngs.at[order.index(d) % 2, at, :]
        return remote(
            src, tin.at[a, d, s], tps.at[a, d, s], tpr.at[a, d, s], (dp, me, 1 - core)
        )

    def load(d, s):
        return pltpu.make_async_copy(p0.at[d, part(core, s), :], acc.at[0, d, s], loc.at[d, s])

    def load_swapped(a, d, s):
        return pltpu.make_async_copy(tin.at[a, d, s], tst.at[s], tloc.at[a, d, s])

    def slot(d, side):
        if side:
            return d
        here = 1 - jnp.minimum(jnp.abs(me - 1 - d), 1)
        return d + here * (ways - d)

    def came(d, side):
        if side:
            return d
        here = 1 - jnp.minimum(jnp.abs(me - d), 1)
        return d + here * (ways - d)

    def stream(a, d, s, side):
        return remote(
            acc.at[a, d, s],
            zin.at[a, slot(d, side), s],
            zs.at[a, d, s],
            zr.at[a, slot(d, side), s],
            (dp, me - 1 + 2 * side, core),
        )

    def arrived(a, d, s, side):
        ref = zin.at[a, came(d, side), s]
        return remote(
            ref, ref, zs.at[a, d, s], zr.at[a, came(d, side), s], (dp, me - 1 + 2 * side, core)
        )

    def finish(a, s, which):
        ref = out.at[a, part(which, s), :]
        return remote(acc.at[a, me, s], ref, os.at[0, a, s], orr.at[a, s], (dp, me, 1 - core))

    def finish_here(a, s):
        return pltpu.make_async_copy(acc.at[a, me, s], out.at[a, part(core, s), :], os.at[1, a, s])

    def merge(a, d):
        for s in range(PIECES):
            swap(a, d, s).wait_recv()
            load_swapped(a, d, s).start()
        for s in range(PIECES):
            load_swapped(a, d, s).wait()
            if a == 0:
                load(d, s).wait()
            add(acc.at[a, d, s], tst.at[s], piece)
            pl.when((me == 0) & (d > 0))(lambda: stream(a, d, s, 1).start())
            pl.when((me == ways - 1) & (d < ways - 1))(lambda: stream(a, d, s, 0).start())

    def hop(a, far_by, j):
        for s in range(PIECES):
            d = ways - 1 - j

            @pl.when(me == far_by)
            def _():
                arrived(a, d, s, 1).wait_recv()
                add(acc.at[a, d, s], zin.at[a, came(d, 1), s], piece)
                if d > far_by:
                    stream(a, d, s, 1).start()

            @pl.when(me == ways - 1 - far_by)
            def _():
                arrived(a, j, s, 0).wait_recv()
                add(acc.at[a, j, s], zin.at[a, came(j, 0), s], piece)
                if j < ways - 1 - far_by:
                    stream(a, j, s, 0).start()

    def last(a):
        for s in range(PIECES):
            finish(a, s, core).start()
            finish_here(a, s).start()

    def lanes_of(path):
        return pl.ds(path * lanes, lanes)

    def first(grp, path, i):
        return remote(
            gsend.at[2 * i + path],
            first_in.at[grp, path, i],
            fs.at[grp, path, i],
            fr.at[grp, path, i],
            (nxt[path], me, core),
        )

    def second(grp, path):
        return remote(
            gown.at[grp % 2, path, 0],
            second_in.at[grp, path],
            ss.at[grp, path],
            sr.at[grp, path],
            (nxt[1 - path], me, core),
        )

    def share(grp, path, i):
        d = (me + i) % ways
        return remote(
            gown.at[grp % 2, path, 1, pl.ds(pl.multiple_of(d * depth, 16), depth), :],
            gwo.at[grp, me, :, lanes_of(path)],
            ws.at[grp, path, i],
            wr.at[grp, path, i],
            (dp, d, core),
        )

    def keep(grp, path):
        return pltpu.make_async_copy(
            gown.at[grp % 2, path, 1, pl.ds(pl.multiple_of(me * depth, 16), depth), :],
            gwo.at[grp, me, :, lanes_of(path)],
            ws.at[grp, path, 0],
        )

    quarters = (far, dpx, dpy, dp)

    def load_left(grp, r, which=0):
        at = pl.ds(pl.multiple_of(quarters[r] * span_rows, 128), span_rows)
        src = (normed, g, normed)[grp] if which == 0 else g
        into = (4 * grp + r) % 2 if grp < 2 else which
        return pltpu.make_async_copy(src.at[:, at], lt.at[into], lts.at[grp, r, which])

    def products(grp, r):
        load_left(grp, r).wait()
        if grp == 2:
            load_left(grp, r, 1).wait()
        elif 4 * grp + r < 7:
            after = 4 * grp + r + 1
            load_left(after // 4, after % 4).start()
        left = (4 * grp + r) % 2 if grp < 2 else 0
        for path in range(2):
            if r == 0:
                dst = gsend.at[path]
                i = 0
            elif r == 1 + path:
                dst = gsend.at[2 + path]
                i = 1
            else:
                dst = gown.at[grp % 2, path, 1 if r == 3 else 0]
                i = None
            if i is not None and grp:
                first(grp - 1, path, i).wait_send()
            if i is None and grp == 2:
                if r == 3:
                    keep(0, path).wait()
                    for n in range(1, ways):
                        share(0, path, n).wait_send()
                else:
                    second(0, path).wait_send()
            right = (ra, rb, ra)[grp]
            if grp == 2 and path == 1:
                dst[:, :head_cols] = dot_tn(lt[0], right[:, 2 * head_cols : 3 * head_cols]).astype(BF16)
                dst[:, head_cols:] = dot_tn(lt[1], right[:, 3 * head_cols :]).astype(BF16)
            else:
                dst[...] = dot_tn(lt[left], right[:, lanes_of(path)]).astype(BF16)
            if i is not None:
                first(grp, path, i).start()
        if grp == 2 and r < 3:
            load_left(grp, r + 1).start()
            load_left(grp, r + 1, 1).start()

    def first_sum(grp, path):
        first(grp, path, 0).wait_recv()
        add(gown.at[grp % 2, path, 0], first_in.at[grp, path, 0], span_rows)
        second(grp, path).start()
        first(grp, path, 1).wait_recv()
        add(gown.at[grp % 2, path, 1], first_in.at[grp, path, 1], span_rows)

    def second_sum(grp, path):
        second(grp, path).wait_recv()
        add(gown.at[grp % 2, path, 1], second_in.at[grp, path], span_rows)
        for i in range(1, ways):
            share(grp, path, i).start()
        keep(grp, path).start()

    pairs = (
        (hg, ra), (hidden, rb), (wa.at[:, pl.ds(0, 3 * head_cols)], wp),
        (q, qv), (k, kv), (v, vv), (mg, mgv), (lse, lsev), (cos, cosv), (sin, sinv),
    )

    def copy_in(i):
        return pltpu.make_async_copy(*pairs[i], ins.at[i])

    mix_in = pltpu.make_async_copy(mix, ra.at[:, pl.ds(3 * head_cols, head_cols)], ins.at[10])

    def begin():
        for i in range(3, 10):
            copy_in(i).wait()
        mix_in.start()
        for o in range(ways):
            at = slice(o * rows, (o + 1) * rows)
            rows_here = labels[o].astype(F32)
            labr[:, at] = rows_here
            labc[at, :] = jnp.transpose(rows_here)

    def turned_back(value, at):
        return turn(value, cosv[at, :], -sinv[at, :]).astype(BF16)

    def attend_back(pair, i):
        at = pl.ds(pair * 128, 128)
        here, seen = pl.ds(i * QUERIES, QUERIES), pl.ds(0, (i + 1) * QUERIES)
        allowed = allowed_keys(labr, labc, i)
        head = lax.broadcasted_iota(jnp.int32, (QUERIES, 128), 1) < HD
        if i == 0:
            dkv[...] = jnp.zeros_like(dkv)
            dvv[...] = jnp.zeros_like(dvv)
        keys, values = kv[seen, at], vv[seen, at]
        parts = []
        for sub in range(2):
            mine = head if sub == 0 else ~head
            qi = jnp.where(mine, qv[here, at], 0)
            mi = jnp.where(mine, mgv[here, at], 0)
            log = lsev[here, pair * 2 + sub : pair * 2 + sub + 1]
            probs = jnp.where(allowed, jnp.exp(dot_nt(qi, keys) - log), 0.0)
            prob_grad = dot_nt(mi, values)
            delta = jnp.sum(probs * prob_grad, 1, keepdims=True)
            score_grad = (probs * (prob_grad - delta)).astype(BF16)
            parts.append(dot_nn(score_grad, keys))
            dkv[seen, :] += dot_tn(score_grad, qi)
            dvv[seen, :] += dot_tn(probs.astype(BF16), mi)
        ra[here, at] = turned_back(jnp.where(head, parts[0], parts[1]) * scale, here)
        if i == rows * ways // QUERIES - 1:
            ra[:, pl.ds(head_cols + pair * 128, 128)] = turned_back(dkv[...], slice(None))
            ra[:, pl.ds(2 * head_cols + pair * 128, 128)] = dvv[...].astype(BF16)

    def load_back(d, own):
        at = pl.ds(pl.multiple_of((core if own else 1 - core) * half, 16), half)
        return [
            pltpu.make_async_copy(ngm.at[d, at, :], ngi.at[own], ngl.at[0, d, own]),
            pltpu.make_async_copy(xh.at[d, at, :], xhi.at[own], ngl.at[1, d, own]),
        ]

    def normed_back(n):
        d = order[n]
        if n == 0:
            copy_in(2).wait()
            sums[...] = small[...]
        if n >= 2:
            for s in range(PIECES):
                swap(1, order[n - 2], s).wait_send()
        wide = 512
        for own in range(2):
            for copy in load_back(d, own):
                copy.wait()
            at = pl.ds(pl.multiple_of(d * rows + (core if own else 1 - core) * half, 16), half)

            def mul(i):
                cols = pl.ds(pl.multiple_of(i * wide, wide), wide)
                tile = dot_nt(ra[at, : 3 * head_cols], wp[cols, :]) + ngi[own, :, cols].astype(F32)
                sums[0:1, cols] += jnp.sum(tile * xhi[own, :, cols].astype(F32), 0, keepdims=True)
                sums[1:2, cols] += jnp.sum(tile, 0, keepdims=True)
                tile = tile.astype(BF16)
                for s in range(PIECES):
                    if own:
                        acc[1, d, s, :, cols] = tile[s * piece : (s + 1) * piece]
                    else:
                        ngs[n % 2, s * piece : (s + 1) * piece, cols] = tile[s * piece : (s + 1) * piece]

            loop(width // wide, mul)
            if not own:
                for s in range(PIECES):
                    swap(1, d, s).start()
            if n < ways - 1:
                for copy in load_back(order[n + 1], own):
                    copy.start()

    def small_send(i):
        src = sums if i == 0 else sum_out.at[i - 1]
        device = ((dp, me, 1 - core), (dpx, me, core), (dpy, me, core))[i]
        return remote(src, sum_in.at[i], sms.at[i], smr.at[i], device)

    def small_all(i):
        device = (dp, (me + i) % ways, core)
        return remote(sum_out.at[2], smallo.at[me], sms.at[2 + i], smr.at[2 + i], device)

    def small_begin():
        sums[4:5, : 3 * head_cols] = jnp.sum(ra[:, : 3 * head_cols].astype(F32), 0, keepdims=True)
        small_send(0).start()

    def small_step(i):
        small_send(i).wait_recv()
        before = sums[...] if i == 0 else sum_out[i - 1]
        after = before + sum_in[i]
        if i == 0:
            row = lax.broadcasted_iota(jnp.int32, after.shape, 0)
            after = jnp.where(row < 2, after, before)
        sum_out[i] = after
        if i < 2:
            small_send(i + 1).start()
        else:
            for n in range(1, ways):
                small_all(n).start()
            smallo[me] = after

    greet(ways)
    for d in order:
        for s in range(PIECES):
            swap(0, d, s).start()
            load(d, s).start()
    load_left(0, 0).start()
    for i in range(len(pairs)):
        copy_in(i).start()
    for own in range(2):
        for copy in load_back(order[0], own):
            copy.start()
    copy_in(0).wait()
    copy_in(1).wait()

    def last_left():
        mix_in.wait()
        load_left(2, 0).start()
        load_left(2, 0, 1).start()

    steps = dict(
        t=products,
        f=first_sum,
        h=second_sum,
        m=merge,
        z=hop,
        o=last,
        B=begin,
        a=attend_back,
        L=last_left,
        n=normed_back,
        Y=small_begin,
        y=small_step,
    )
    plan = (
        "t00", "m00", "m03", "m01", "m02", "t01", "t02", "t03", "t10", "z010", "t11", "t12", "t13",
        "B", "f00", "f01", "z011", "z020", "a00", "a01", "a02", "h00", "h01", "a03", "z012",
        "z021", "a04", "z030", "a05", "o0", "f10", "f11", "a10", "a11", "h10", "h11", "a12", "a13",
        "a14", "a15", "L", "n0", "n1", "m10", "m13", "n2", "n3", "m11", "m12", "Y", "t20", "y0",
        "t21", "y1", "z110", "t22", "y2", "t23", "z111", "z120", "f20", "f21", "h20", "h21",
        "z112", "z121", "z130", "o1",
    )
    for word in plan:
        steps[word[0]](*(int(digit) for digit in word[1:]))

    for i in range(3):
        small_send(i).wait_send()
    for i in range(1, ways):
        small_all(i).wait()
    for a in range(2):
        for s in range(PIECES):
            finish(a, s, core).wait_send()
            finish_here(a, s).wait()
            finish(a, s, 1 - core).wait_recv()
            for n, d in enumerate(order):
                if a == 0 or n >= 2:
                    swap(a, d, s).wait_send()
                pl.when(d > me)(lambda: stream(a, d, s, 1).wait_send())
                pl.when(d < me)(lambda: stream(a, d, s, 0).wait_send())
    for grp in range(groups):
        for path in range(2):
            if grp == 2:
                for i in range(2):
                    first(grp, path, i).wait_send()
            if grp:
                second(grp, path).wait_send()
                keep(grp, path).wait()
            for i in range(1, ways):
                share(grp, path, i).wait_recv()
                if grp:
                    share(grp, path, i).wait_send()


def backward(p0, ngm, normed, xh, g, hg, hidden, q, k, v, mg, mix, lse, cos, sin, wa, labels, small):
    ways, rows, width = p0.shape
    chips = lax.axis_size("dp")
    tokens = ways * rows
    groups, cols, head_cols = 3, hg.shape[-1], q.shape[-1]
    span = width // chips
    lanes = cols // 2
    piece = rows // 2 // PIECES
    half = rows // 2
    dma = pltpu.SemaphoreType.DMA
    vmem = pltpu.VMEM
    anywhere = pl.BlockSpec(memory_space=pl.ANY)
    inside = pl.BlockSpec(memory_space=pltpu.VMEM)
    flat = lambda t: t.reshape(tokens, t.shape[-1])
    out, gwo, unused, smallo = pl.pallas_call(
        functools.partial(backward_body, ways),
        in_specs=[anywhere] * 16 + [inside] * 2,
        out_specs=[anywhere] * 3 + [inside],
        out_shape=[
            jax.ShapeDtypeStruct((2, rows, width), BF16),
            jax.ShapeDtypeStruct((groups, ways, span // ways, cols), BF16),
            jax.ShapeDtypeStruct((2, ways, PIECES, piece, width), BF16),
            jax.ShapeDtypeStruct((ways,) + small.shape, F32),
        ],
        scratch_shapes=[
            vmem((2, tokens, span), BF16),
            vmem((tokens, cols), BF16),
            vmem((tokens, cols), BF16),
            vmem((width, 3 * head_cols), BF16),
            vmem((tokens, head_cols), BF16),
            vmem((tokens, head_cols), BF16),
            vmem((tokens, head_cols), BF16),
            vmem((tokens, head_cols), BF16),
            vmem((tokens, 128), F32),
            vmem((tokens, 128), F32),
            vmem((tokens, 128), F32),
            vmem((tokens, 128), F32),
            vmem((tokens, 128), F32),
            vmem((8, tokens), F32),
            vmem((tokens, 8), F32),
            vmem((2, ways, PIECES, piece, width), BF16),
            vmem((2, ways + 1, PIECES, piece, width), BF16),
            vmem((PIECES, piece, width), BF16),
            vmem((2, half, width), BF16),
            vmem((2, half, width), BF16),
            vmem((2, half, width), BF16),
            vmem((2, 2, 2, span, lanes), BF16),
            vmem((4, span, lanes), BF16),
            vmem((groups, 2, 2, span, lanes), BF16),
            vmem((groups, 2, span, lanes), BF16),
            vmem(small.shape, F32),
            vmem((3,) + small.shape, F32),
            vmem((3,) + small.shape, F32),
            dma((2, ways, PIECES)),
            dma((2, ways, PIECES)),
            dma((2, ways, PIECES)),
            dma((2, ways + 1, PIECES)),
            dma((groups, 2, 2)),
            dma((groups, 2, 2)),
            dma((groups, 2)),
            dma((groups, 2)),
            dma((groups, 2, ways)),
            dma((groups, 2, ways)),
            dma((2, 2, PIECES)),
            dma((2, PIECES)),
            dma((ways, PIECES)),
            dma((2, ways, PIECES)),
            dma((2 + ways,)),
            dma((2 + ways,)),
            dma((11,)),
            dma((groups, 4, 2)),
            dma((2, ways, 2)),
        ],
        compiler_params=pltpu.CompilerParams(
            collective_id=1, has_side_effects=True, vmem_limit_bytes=63 * MIB
        ),
    )(
        p0, ngm, flat(normed), xh, flat(g), flat(hg), flat(hidden), q, k, v, flat(mg), mix,
        lse, cos, sin, wa, labels, small,
    )
    return out[0].astype(F32), out[1].astype(F32), gwo.astype(F32), smallo


def layer_norm(x):
    xf = x.astype(F32)
    mean = jnp.mean(xf, -1, keepdims=True)
    centred = xf - mean
    inv_std = lax.rsqrt(jnp.mean(centred * centred, -1, keepdims=True) + EPS)
    return centred * inv_std, inv_std


def plain_work(x, g, wsrc, places, segments, gain, shift, fc1_shift, qkv_shift):
    me, ways = lax.axis_index("ctx"), lax.axis_size("ctx")
    width = x.shape[1]
    unused, unused, depth, cols = wsrc.shape
    head_cols = cols // 4
    x_all, g_all, weights, places, segments = gather_plain(x, g, wsrc, places, segments)
    weights = weights.reshape(3, width, cols)
    w1, w2, wa = weights[0], weights[1], weights[2]
    wp, wd = wa[:, : 3 * head_cols], wa[:, 3 * head_cols :]
    x_hat, unused = layer_norm(x_all)
    normed = (x_hat * gain + shift).astype(BF16)
    projected = dot_nn(normed, wp) + qkv_shift.reshape(1, 3 * head_cols)
    mix_grad = dot_nn(g_all, wd).astype(BF16)
    mixture, gq, gk, gv = attention_plain(
        projected[:, :head_cols],
        projected[:, head_cols : 2 * head_cols],
        projected[:, 2 * head_cols :],
        mix_grad,
        places,
        segments,
    )
    proj_grad = jnp.concatenate([gq, gk, gv], 1)

    hidden_pre = dot_nn(normed, w1) + fc1_shift
    hidden, slope = gelu_and_slope(hidden_pre)
    hidden = hidden.astype(BF16)
    hidden_grad = (dot_nn(g_all, w2) * slope).astype(BF16)

    out_part = (dot_nt(mixture, wd) + dot_nt(hidden, w2)).astype(BF16)
    normed_part = dot_nt(proj_grad, wp) + dot_nt(hidden_grad, w1)
    weight_part = jnp.stack(
        [
            dot_tn(normed, hidden_grad).astype(BF16),
            dot_tn(g_all, hidden).astype(BF16),
            jnp.concatenate([dot_tn(normed, proj_grad), dot_tn(g_all, mixture)], 1).astype(BF16),
        ]
    )
    qkv_bias_part = jnp.sum(proj_grad.astype(F32), 0).reshape(3, head_cols)
    fc1_bias_part = jnp.sum(hidden_grad.astype(F32), 0)
    branches, normed_grad, weight_grads = scatter_plain(
        out_part, normed_part.astype(BF16), weight_part.reshape(3, -1, depth, cols)
    )
    place = lambda t, whole, axis: lax.dynamic_update_slice_in_dim(
        jnp.zeros(whole, F32), t, me * t.shape[axis], axis
    )
    small = lax.psum(
        (
            place(qkv_bias_part, (3, head_cols * ways), 1),
            place(fc1_bias_part, (cols * ways,), 0),
            jnp.sum(g.astype(F32), 0),
        ),
        ("dp", "ctx"),
    )
    norms = lax.psum(
        (jnp.sum(normed_part * x_hat, 0), jnp.sum(normed_part, 0)), ("dp", "ctx", "tp")
    )
    return branches, normed_grad, weight_grads, norms + small


def fast_work(x, g, wsrc, places, segments, gain, shift, fc1_shift, qkv_shift):
    ways = lax.axis_size("ctx")
    rows, width = x.shape
    cols = wsrc.shape[-1]
    head_cols = cols // 4
    ids = jnp.zeros((8, rows), jnp.int32).at[0].set(places).at[1].set(segments)
    (
        g_all, normed, x_hat, hidden, hidden_grad, out_part, back_mlp, mix_grad, wa,
        q, k, v, mixture, lse, cos, sin, labels, fc1_sum, unused,
    ) = forward(x, g, wsrc, ids, gain, shift, fc1_shift, qkv_shift)
    line = lambda t: jnp.pad(t.reshape(1, -1), ((0, 0), (0, width - t.size)))
    none = jnp.zeros((1, width), F32)
    small = jnp.concatenate(
        [none, none, jnp.sum(g.astype(F32), 0, keepdims=True), line(fc1_sum)] + [none] * 4
    )
    branches, normed_grad, weight_grads, sums = backward(
        out_part, back_mlp, normed, x_hat, g_all, hidden_grad, hidden,
        q, k, v, mix_grad, mixture, lse, cos, sin, wa, labels, small,
    )
    total = jnp.sum(sums[:, :3], 0)
    fc1_bias_sum = sums[:, 3, :cols].reshape(ways * cols)
    qkv_bias_sum = sums[:, 4, : 3 * head_cols].reshape(ways, 3, head_cols).transpose(1, 0, 2)
    return (
        branches,
        normed_grad,
        weight_grads,
        (total[0], total[1], qkv_bias_sum.reshape(3, ways * head_cols), fc1_bias_sum, total[2]),
    )


def per_device(
    block_input,
    cotangent,
    segment_ids,
    positions,
    norm_gain,
    norm_bias,
    w_qkv,
    qkv_bias,
    w_dense,
    w_fc1,
    fc1_bias,
    w_fc2,
    out_bias,
):
    ways = lax.axis_size("ctx")
    me = lax.axis_index("ctx")
    x, g = block_input[0], cotangent[0]
    rows, width = x.shape
    depth = w_fc1.shape[0]
    cols = w_fc1.shape[1] // ways
    head_cols = w_qkv.shape[2] // ways

    fc1 = w_fc1.reshape(depth, ways, cols).transpose(1, 0, 2)
    fc2 = w_fc2.reshape(ways, cols, depth).transpose(0, 2, 1)
    qkv = w_qkv.reshape(3, depth, ways, head_cols).transpose(2, 1, 0, 3)
    dense = w_dense.reshape(ways, head_cols, depth).transpose(0, 2, 1)
    att = jnp.concatenate([qkv.reshape(ways, depth, 3 * head_cols), dense], -1)
    wsrc = jnp.stack([fc1, fc2, att])

    gain, shift = norm_gain.astype(F32), norm_bias.astype(F32)
    qkv_shift = lax.dynamic_slice_in_dim(qkv_bias, me * head_cols, head_cols, 1).astype(F32)
    fc1_shift = lax.dynamic_slice_in_dim(fc1_bias, me * cols, cols, 0).astype(F32)
    fast = ways == 4 and lax.axis_size("dp") == 4 and rows % 64 == 0 and head_cols % 128 == 0
    work = fast_work if fast else plain_work
    branches, normed_grad, weight_grads, sums = work(
        x, g, wsrc, positions[0], segment_ids[0], gain, shift, fc1_shift, qkv_shift
    )

    gf = g.astype(F32)
    output = (x.astype(F32) + branches + out_bias.astype(F32)).astype(BF16)
    own_hat, inv_std = layer_norm(x)
    scaled = normed_grad * gain
    grad_input = gf + inv_std * (
        scaled
        - jnp.mean(scaled, -1, keepdims=True)
        - own_hat * jnp.mean(scaled * own_hat, -1, keepdims=True)
    )
    gain_sum, shift_sum, qkv_bias_sum, fc1_bias_sum, out_bias_sum = sums

    grad_fc1 = weight_grads[0].transpose(1, 0, 2).reshape(depth, ways * cols)
    grad_fc2 = weight_grads[1].transpose(0, 2, 1).reshape(ways * cols, depth)
    grad_att = weight_grads[2].reshape(ways, depth, 4, head_cols)
    grad_qkv = grad_att[:, :, :3].transpose(2, 1, 0, 3).reshape(3, depth, ways * head_cols)
    grad_dense = grad_att[:, :, 3].transpose(0, 2, 1).reshape(ways * head_cols, depth)
    return (
        output[None],
        grad_input.astype(BF16)[None],
        gain_sum,
        shift_sum,
        grad_qkv,
        qkv_bias_sum,
        grad_dense,
        grad_fc1,
        fc1_bias_sum,
        grad_fc2,
        out_bias_sum,
    )


def solution(mesh):
    placed = (
        P("dp", "ctx", None),
        P("dp", "ctx", None),
        P("dp", "ctx"),
        P("dp", "ctx"),
        P(),
        P(),
        P(None, ("dp", "ctx"), "tp"),
        P(None, "tp"),
        P("tp", ("dp", "ctx")),
        P(("dp", "ctx"), "tp"),
        P("tp"),
        P("tp", ("dp", "ctx")),
        P(),
    )
    return jax.shard_map(
        per_device,
        mesh=mesh,
        in_specs=placed,
        out_specs=(
            P("dp", "ctx", None),
            P("dp", "ctx", None),
            P(),
            P(),
            P(None, ("dp", "ctx"), "tp"),
            P(None, "tp"),
            P("tp", ("dp", "ctx")),
            P(("dp", "ctx"), "tp"),
            P("tp"),
            P("tp", ("dp", "ctx")),
            P(),
        ),
        check_vma=False,
    )
```

```python
import functools
import math

import jax
import jax.numpy as jnp
from jax import lax
from jax.experimental import pallas as pl
from jax.experimental.pallas import tpu as pltpu
from jax.sharding import PartitionSpec as P

HD = 64
ROT = 32
EPS = 1e-05
MIB = 1 << 20
F32 = jnp.float32
BF16 = jnp.bfloat16
MESH = pl.DeviceIdType.MESH


def dot_nn(a, b):
    return lax.dot_general(a, b, (((1,), (0,)), ((), ())), preferred_element_type=F32)


def dot_nt(a, b):
    return lax.dot_general(a, b, (((1,), (1,)), ((), ())), preferred_element_type=F32)


def dot_tn(a, b):
    return lax.dot_general(a, b, (((0,), (0,)), ((), ())), preferred_element_type=F32)


QUERIES = 256


def frequencies():
    half = ROT // 2
    one = jnp.concatenate(
        [10000.0 ** (-(jnp.arange(half, dtype=F32) * 2.0 / ROT))] * 2 + [jnp.zeros(HD - ROT, F32)]
    )
    return jnp.concatenate([one, one])[None, :]


def turn(v, cos, sin):
    half = ROT // 2
    lane = lax.broadcasted_iota(jnp.int32, v.shape, 1) % HD
    left, right = pltpu.roll(v, 128 - half, 1), pltpu.roll(v, half, 1)
    return v * cos + jnp.where(lane < half, -left, right) * sin


def allowed_keys(labr, labc, i):
    shape = (QUERIES, (i + 1) * QUERIES)
    row = lax.broadcasted_iota(jnp.int32, shape, 0) + i * QUERIES
    col = lax.broadcasted_iota(jnp.int32, shape, 1)
    here = pl.ds(i * QUERIES, QUERIES)
    return (col <= row) & (labc[here, 1:2] == labr[1:2, 0 : (i + 1) * QUERIES])


def attention_plain(pq, pk, pv, mg, places, segments):
    rows, cols = pq.shape
    heads = cols // HD
    half = ROT // 2
    scale = 1.0 / math.sqrt(HD)
    frequency = 10000.0 ** (-(jnp.arange(half, dtype=F32) * 2.0 / ROT))
    angles = places.astype(F32)[:, None] * frequency[None, :]
    cos, sin = jnp.cos(angles)[:, None, :], jnp.sin(angles)[:, None, :]

    def rotate(t, s):
        t = t.reshape(rows, heads, HD)
        a, b = t[..., :half], t[..., half:ROT]
        return jnp.concatenate([a * cos - b * s, b * cos + a * s, t[..., ROT:]], -1)

    q = rotate(pq, sin).astype(BF16)
    k = rotate(pk, sin).astype(BF16)
    v = pv.astype(BF16).reshape(rows, heads, HD)
    m = mg.reshape(rows, heads, HD)
    span = 256
    index = jnp.arange(rows, dtype=jnp.int32)

    def step(carry, items):
        dk, dv = carry
        qi, mi, row_index, row_seg = items
        scores = jnp.einsum("qhd,khd->hqk", qi, k, preferred_element_type=F32) * scale
        allowed = (index[None, :] <= row_index[:, None]) & (segments[None, :] == row_seg[:, None])
        scores = jnp.where(allowed[None], scores, -1e30)
        expo = jnp.exp(scores - jnp.max(scores, -1, keepdims=True))
        probs = expo / jnp.sum(expo, -1, keepdims=True)
        low = probs.astype(BF16)
        out = jnp.einsum("hqk,khd->qhd", low, v, preferred_element_type=F32).astype(BF16)
        prob_grad = jnp.einsum("qhd,khd->hqk", mi, v, preferred_element_type=F32)
        delta = jnp.sum(probs * prob_grad, -1, keepdims=True)
        score_grad = (probs * (prob_grad - delta)).astype(BF16)
        dq = jnp.einsum("hqk,khd->qhd", score_grad, k, preferred_element_type=F32) * scale
        dk = dk + jnp.einsum("hqk,qhd->khd", score_grad, qi, preferred_element_type=F32) * scale
        dv = dv + jnp.einsum("hqk,qhd->khd", low, mi, preferred_element_type=F32)
        return (dk, dv), (out, dq)

    zero = jnp.zeros((rows, heads, HD), F32)
    cut = lambda t: t.reshape((rows // span, span) + t.shape[1:])
    (dk, dv), (out, dq) = lax.scan(step, (zero, zero), (cut(q), cut(m), cut(index), cut(segments)))
    flat = lambda t: t.reshape(rows, cols)
    return (
        flat(out),
        flat(rotate(dq.reshape(rows, cols), -sin)).astype(BF16),
        flat(rotate(dk.reshape(rows, cols), -sin)).astype(BF16),
        flat(dv).astype(BF16),
    )


def gather_plain(x, g, wsrc, places, segments):
    pieces = lax.all_to_all(wsrc, "ctx", split_axis=1, concat_axis=1, tiled=True)
    weights = lax.all_gather(pieces, "dp", axis=1, tiled=True)
    along = lambda t: lax.all_gather(t, "ctx", axis=0, tiled=True)
    return along(x), along(g), weights, along(places), along(segments)


def scatter_plain(out_part, normed_part, weight_part):
    summed = lambda t: lax.psum(
        lax.psum_scatter(t, "ctx", scatter_dimension=0, tiled=True), "tp"
    ).astype(F32)
    pieces = lax.psum_scatter(weight_part, "dp", scatter_dimension=1, tiled=True)
    pieces = lax.all_to_all(pieces, "ctx", split_axis=1, concat_axis=1, tiled=True)
    return summed(out_part), summed(normed_part), pieces.astype(F32)


def place_of():
    dp, me, core = lax.axis_index("dp"), lax.axis_index("ctx"), lax.axis_index("tp")
    return dp, me, core, dp + 1 - 2 * (dp % 2), dp + 2 - 4 * (dp // 2)


def greet(ways):
    dp, me, core, dpx, dpy = place_of()
    barrier = pltpu.get_barrier_semaphore()
    for device in [(dp, me, 1 - core), (dpx, me, core), (dpy, me, core)] + [
        (dp, (me + k) % ways, core) for k in range(1, ways)
    ]:
        pl.semaphore_signal(barrier, inc=1, device_id=device, device_id_type=MESH)
    pl.semaphore_wait(barrier, ways + 2)


def remote(src, dst, send, recv, device):
    return pltpu.make_async_remote_copy(
        src_ref=src, dst_ref=dst, send_sem=send, recv_sem=recv, device_id=device, device_id_type=MESH
    )


PIECES = 2


def gelu_and_slope(v):
    c = math.sqrt(2.0 / math.pi)
    square = v * v
    tanh = jnp.tanh(c * v * (1.0 + 0.044715 * square))
    half = 0.5 * (1.0 + tanh)
    slope = half + 0.5 * c * v * (1.0 - tanh * tanh) * (1.0 + 3.0 * 0.044715 * square)
    return v * half, slope


def forward_body(
    ways, x, g, w1, w2, wq, wd, ids, gain, shift, fc1_shift, qkv_shift, freq,
    go, no, xho, ho, hgo, outo, ngo, mgo, wao, qo, ko, vo, mixo, lseo, coso, sino, ido, biaso,
    xo, w1v, w2v, wqv, wdv, norm, xb, gb, pre, hid, slope, hgb, ob, nb, mb, qb, kb, vb, mixb, lse, cosb, sinb, labr, labc,
    zs, zr, ts, tr, ws, wr, ls, lr, ds, dr, ids_s, ids_r, own, ls_in, ls_out, keep_out,
):
    dp, me, core, dpx, dpy = place_of()
    rows, width = x.shape
    piece = rows // 2 // PIECES
    groups, depth = ws.shape[0], w1.shape[0]
    cols, head_cols = w1v.shape[1], wdv.shape[0]
    srcs, outs = (x, g), (xo, go)
    blocks = [me, 1 + me % 2, None, 3 * (1 - me // 2)]
    blocks[2] = 6 - me - blocks[1] - blocks[3]

    def part(which, s):
        return pl.ds(pl.multiple_of(which * (rows // 2) + s * piece, 16), piece)

    def along(a, owner, s, side, mine=False):
        at = part(core, s)
        src = srcs[a].at[at, :] if mine else outs[a].at[owner, at, :]
        return remote(
            src,
            outs[a].at[owner, at, :],
            zs.at[side, a, owner, s],
            zr.at[a, owner, s],
            (dp, me - 1 + 2 * side, core),
        )

    def across(a, owner, s, which):
        at = part(which, s)
        ref = outs[a].at[owner, at, :]
        return remote(ref, ref, ts.at[a, owner, s], tr.at[a, owner, s], (dp, me, 1 - core))

    def here(chip, j, height=None):
        return pl.ds(pl.multiple_of((chip * ways + j) * depth, depth), depth)

    def held(grp, chip, j):
        at = here(chip, j)
        return ([w1v.at[at, :]], [w2v.at[:, at]], [wqv.at[at, :], wdv.at[:, at]])[grp]

    def given(grp, d):
        at = here(dp, me)
        mine = pl.ds(pl.multiple_of(d * cols, 128), cols)
        if grp == 0:
            return [(w1.at[:, mine], w1v.at[at, :])]
        if grp == 1:
            return [(w2.at[mine, :], w2v.at[:, at])]
        mine = pl.ds(pl.multiple_of(d * head_cols, 128), head_cols)
        return [
            (wq.at[c, :, mine], wqv.at[at, pl.ds(c * head_cols, head_cols)]) for c in range(3)
        ] + [(wd.at[mine, :], wdv.at[:, at])]

    def share(grp, k):
        d = (me + k) % ways
        return [
            remote(src, dst, ws.at[grp, k, i], wr.at[grp, k, i], (dp, d, core))
            for i, (src, dst) in enumerate(given(grp, d))
        ]

    def keep(grp):
        return [
            pltpu.make_async_copy(src, dst, ws.at[grp, 0, i])
            for i, (src, dst) in enumerate(given(grp, me))
        ]

    def source(k):
        return (me - k + ways) % ways

    def spread(grp, k, axis):
        return [
            remote(ref, ref, ls.at[axis, grp, k, i], lr.at[axis, grp, k, i], ((dpx, dpy)[axis], me, core))
            for i, ref in enumerate(held(grp, dp, source(k)))
        ]

    def corner(grp, k):
        axis = (grp + k) % 2
        return [
            remote(ref, ref, ds.at[grp, k, i], dr.at[grp, k, i], ((dpy, dpx)[axis], me, core))
            for i, ref in enumerate(held(grp, (dpx, dpy)[axis], source(k)))
        ]

    def start(copies):
        for copy in copies:
            copy.start()

    def wait_recv(copies):
        for copy in copies:
            copy.wait_recv()

    def wait_send(copies):
        for copy in copies:
            copy.wait_send()

    def labels(k):
        return remote(ids, ido.at[me], ids_s.at[k], ids_r.at[k], (dp, (me + k) % ways, core))

    def send_own(a, s):
        pl.when(me > 0)(lambda: along(a, me, s, 0, True).start())
        pl.when(me < ways - 1)(lambda: along(a, me, s, 1, True).start())

    def send_share(grp, k):
        if k:
            start(share(grp, k))
            return
        start(keep(grp))
        for copy in keep(grp):
            copy.wait()
        for axis in range(2):
            start(spread(grp, 0, axis))

    def pass_on(a, k, s):
        @pl.when(me + k < ways)
        def _():
            along(a, me + k, s, 0).wait_recv()
            pl.when(me > 0)(lambda: along(a, me + k, s, 0).start())
            across(a, me + k, s, core).start()

        @pl.when(me - k >= 0)
        def _():
            along(a, me - k, s, 1).wait_recv()
            pl.when(me < ways - 1)(lambda: along(a, me - k, s, 1).start())
            across(a, me - k, s, core).start()

    def spread_on(grp, k):
        wait_recv(share(grp, k))
        for axis in range(2):
            start(spread(grp, k, axis))

    def corner_on(grp, k):
        wait_recv(spread(grp, k, (grp + k) % 2))
        start(corner(grp, k))

    def settle(grp):
        for k in range(ways):
            wait_recv(spread(grp, k, 1 - (grp + k) % 2))
            wait_recv(corner(grp, k))

    def arrive(a, t):
        if t:
            for s in range(PIECES):
                across(a, blocks[t], s, 1 - core).wait_recv()

    def loop(count, body):
        lax.fori_loop(0, count, lambda i, c: (body(i), c)[1], 0)

    def load_x(t):
        src = x if t == 0 else xo.at[blocks[t]]
        return pltpu.make_async_copy(src, xb.at[t % 2], ls_in.at[0, t])

    def load_g(t):
        src = g if t == 0 else go.at[blocks[t]]
        return pltpu.make_async_copy(src, gb.at[t % 2], ls_in.at[1, t])

    def store(which, t):
        o = blocks[t]
        src, dst = (
            (xb.at[t % 2], xho.at[o]),
            (norm.at[o], no.at[o]),
            (hid.at[o], ho.at[o]),
            (ob.at[t % 2], outo.at[o]),
            (nb.at[t % 2], ngo.at[o]),
            (hgb.at[t % 2], hgo.at[o]),
            (mb.at[t], mgo.at[o]),
        )[which]
        return pltpu.make_async_copy(src, dst, ls_out.at[which, t])

    def normalise(t):
        arrive(0, t)
        if t >= 2:
            store(0, t - 2).wait()
        load_x(t).start()
        load_x(t).wait()
        step = 32

        def body(i):
            at = pl.ds(pl.multiple_of(i * step, step), step)
            xf = xb[t % 2, at, :].astype(F32)
            centred = xf - jnp.mean(xf, -1, keepdims=True)
            inv_std = lax.rsqrt(jnp.mean(centred * centred, -1, keepdims=True) + EPS)
            x_hat = centred * inv_std
            norm[blocks[t], at, :] = (x_hat * gain[...] + shift[...]).astype(BF16)
            xb[t % 2, at, :] = x_hat.astype(BF16)

        loop(rows // step, body)
        store(0, t).start()
        store(1, t).start()

    wide = 512

    def span(i):
        return pl.ds(pl.multiple_of(i * wide, wide), wide)

    def up(t):
        o = blocks[t]

        def mul(i):
            pre[:, span(i)] = dot_nn(norm[o], w1v[:, span(i)]) + fc1_shift[:, span(i)]

        loop(cols // wide, mul)

        def act(i):
            at = pl.ds(pl.multiple_of(i * 16, 16), 16)
            value, grad = gelu_and_slope(pre[at, :])
            hid[o, at, :] = value.astype(BF16)
            slope[o, at, :] = grad

        loop(rows // 16, act)
        store(2, t).start()

    def tables():
        for k in range(1, ways):
            labels(k).wait_recv()
        keeps[1].wait()
        lse[...] = jnp.zeros_like(lse)
        for o in range(ways):
            at = slice(o * rows, (o + 1) * rows)
            rows_here = ido[o].astype(F32)
            labr[:, at] = rows_here
            columns = jnp.transpose(rows_here)
            labc[at, :] = columns
            angles = columns[:, 0:1] * freq[...]
            cosb[at, :] = jnp.cos(angles)
            sinb[at, :] = jnp.sin(angles)
        for copy in table_stores:
            copy.start()

    def project(t):
        o = blocks[t]
        at = pl.ds(pl.multiple_of(o * rows, 16), rows)
        cos, sin = cosb[at, :], sinb[at, :]
        for pair in range(head_cols // 128):
            lanes = pl.ds(pair * 128, 128)
            for which, ref in enumerate((qb, kb, vb)):
                wide_lanes = pl.ds(which * head_cols + pair * 128, 128)
                v = dot_nn(norm[o], wqv[:, wide_lanes]) + qkv_shift[:, wide_lanes]
                if which < 2:
                    v = turn(v, cos, sin)
                v = v.astype(BF16)
                ref[at, lanes] = v * BF16(1.0 / math.sqrt(HD)) if which == 0 else v

    def attend(pair, i):
        lanes = pl.ds(pair * 128, 128)
        here, seen = pl.ds(i * QUERIES, QUERIES), pl.ds(0, (i + 1) * QUERIES)
        allowed = allowed_keys(labr, labc, i)
        first = lax.broadcasted_iota(jnp.int32, (QUERIES, 128), 1) < HD
        lane = lax.broadcasted_iota(jnp.int32, (QUERIES, 128), 1)
        keys, values = kb[seen, lanes], vb[seen, lanes]
        outs_of, logs = [], lse[here, :]
        for sub in range(2):
            mine = first if sub == 0 else ~first
            scores = dot_nt(jnp.where(mine, qb[here, lanes], 0), keys)
            scores = jnp.where(allowed, scores, -1e30)
            top = jnp.max(scores, 1, keepdims=True)
            expo = jnp.exp(scores - top)
            total = jnp.sum(expo, 1, keepdims=True)
            outs_of.append(dot_nn((expo * (1.0 / total)).astype(BF16), values))
            logs = jnp.where(lane == pair * 2 + sub, top + jnp.log(total), logs)
        lse[here, :] = logs
        mixb[here, lanes] = jnp.where(first, outs_of[0], outs_of[1]).astype(BF16)

    def down(t):
        if t >= 2:
            store(3, t - 2).wait()
        o = blocks[t]
        at = pl.ds(pl.multiple_of(o * rows, 16), rows)

        def mul(i):
            total = dot_nn(hid[o], w2v[:, span(i)])
            total = total + dot_nn(mixb[at, :], wdv[:, span(i)])
            ob[t % 2, :, span(i)] = total.astype(BF16)

        loop(width // wide, mul)
        store(3, t).start()

    def back(t):
        arrive(1, t)
        load_g(t).start()
        if t >= 2:
            store(5, t - 2).wait()
        load_g(t).wait()
        o = blocks[t]

        def mul(i):
            act = dot_nt(gb[t % 2], w2v[span(i), :])
            grad = (act * slope[o, :, span(i)]).astype(BF16)
            hgb[t % 2, :, span(i)] = grad
            total = jnp.sum(grad.astype(F32), 0, keepdims=True)
            biaso[:, span(i)] = total if t == 0 else biaso[:, span(i)] + total

        loop(cols // wide, mul)
        store(5, t).start()

    def back_on(t):
        if t >= 2:
            store(4, t - 2).wait()

        def mul_back(i):
            nb[t % 2, :, span(i)] = dot_nt(hgb[t % 2], w1v[span(i), :]).astype(BF16)

        loop(width // wide, mul_back)
        store(4, t).start()
        mb[t] = dot_nt(gb[t % 2], wdv[...]).astype(BF16)
        store(6, t).start()

    greet(ways)
    for k in range(1, ways):
        labels(k).start()
    keeps = [
        pltpu.make_async_copy(g, go.at[me], own.at[0]),
        pltpu.make_async_copy(ids, ido.at[me], own.at[1]),
    ]
    for copy in keeps:
        copy.start()
    wa_out = pltpu.make_async_copy(wqv, wao, own.at[2])
    stores = [
        pltpu.make_async_copy(src, dst, keep_out.at[i])
        for i, (src, dst) in enumerate(
            ((cosb, coso), (sinb, sino), (qb, qo), (kb, ko), (vb, vo), (mixb, mixo), (lse, lseo))
        )
    ]
    table_stores, state_stores = stores[:2], stores[2:]
    steps = dict(
        X=lambda s: send_own(0, s),
        G=lambda s: send_own(1, s),
        S=send_share,
        W=wa_out.start,
        Z=lambda: [copy.start() for copy in state_stores],
        x=lambda k, s: pass_on(0, k, s),
        g=lambda k, s: pass_on(1, k, s),
        s=spread_on,
        c=corner_on,
        e=settle,
        l=tables,
        n=normalise,
        u=up,
        p=project,
        a=attend,
        d=down,
        b=back,
        r=back_on,
    )
    plan = (
        "S03", "S20", "X0", "S10", "l", "S01", "S00", "S02", "n0", "s01", "X1", "c10", "c20",
        "s03", "x10", "S21", "S23", "s02", "c00", "c01", "c03", "S22", "x11", "s21", "x20", "n1",
        "c02", "s23", "e0", "S11", "s22", "S13", "u0", "c21", "c23", "u1", "c22", "x21", "n2",
        "u2", "x30", "S12", "e2", "p0", "s13", "p1", "s11", "W", "p2", "x31", "G0", "G1", "n3",
        "p3", "a11", "s12", "a12", "a05", "a01", "c13", "a14", "a15", "u3", "c12", "c11", "g10",
        "a04", "a02", "a00", "a03", "a13", "g11", "e1", "b0", "a10", "r0", "b1", "g20", "Z", "d0",
        "d1", "d2", "g21", "r1", "g30", "b2", "r2", "g31", "d3", "b3", "r3",
    )
    for word in plan:
        steps[word[0]](*(int(digit) for digit in word[1:]))
    keeps[0].wait()

    for k in range(1, ways):
        labels(k).wait_send()
    for copy in table_stores + state_stores:
        copy.wait()
    wa_out.wait()
    for t in range(4):
        for which in (1, 2, 6):
            store(which, t).wait()
        if t >= 2:
            for which in (0, 3, 4, 5):
                store(which, t).wait()
    for a in range(2):
        for owner in range(ways):
            for s in range(PIECES):

                @pl.when(owner != me)
                def _():
                    across(a, owner, s, core).wait_send()

                @pl.when((me > 0) & (owner >= me))
                def _():
                    along(a, owner, s, 0).wait_send()

                @pl.when((me < ways - 1) & (owner <= me))
                def _():
                    along(a, owner, s, 1).wait_send()

    for grp in range(groups):
        for k in range(ways):
            if k:
                wait_send(share(grp, k))
            for axis in range(2):
                wait_send(spread(grp, k, axis))
            wait_send(corner(grp, k))


def forward(x, g, w1, w2, wq, wd, ids, gain, shift, fc1_shift, qkv_shift):
    ways = lax.axis_size("ctx")
    rows, width = x.shape
    groups, cols, head_cols = 3, w1.shape[1] // ways, wd.shape[0] // ways
    dma = pltpu.SemaphoreType.DMA
    vmem = pltpu.VMEM
    anywhere = pl.BlockSpec(memory_space=pl.ANY)
    inside = pl.BlockSpec(memory_space=pltpu.VMEM)
    seq = lambda n, dtype=BF16: jax.ShapeDtypeStruct((ways, rows, n), dtype)
    tokens = ways * rows
    line = lambda n, dtype: jax.ShapeDtypeStruct((tokens, n), dtype)
    outs = pl.pallas_call(
        functools.partial(forward_body, ways),
        in_specs=[anywhere] * 7 + [inside] * 5,
        out_specs=[anywhere] * 16 + [inside] * 2 + [anywhere],
        out_shape=[
            seq(width),
            seq(width),
            seq(width),
            seq(cols),
            seq(cols),
            seq(width),
            seq(width),
            seq(head_cols),
            jax.ShapeDtypeStruct((width, 3 * head_cols), BF16),
            line(head_cols, BF16),
            line(head_cols, BF16),
            line(head_cols, BF16),
            line(head_cols, BF16),
            line(128, F32),
            line(128, F32),
            line(128, F32),
            jax.ShapeDtypeStruct((ways, 8, rows), jnp.int32),
            jax.ShapeDtypeStruct((1, cols), F32),
            seq(width),
        ],
        scratch_shapes=[
            vmem((width, cols), BF16),
            vmem((cols, width), BF16),
            vmem((width, 3 * head_cols), BF16),
            vmem((head_cols, width), BF16),
            vmem((ways, rows, width), BF16),
            vmem((2, rows, width), BF16),
            vmem((2, rows, width), BF16),
            vmem((rows, cols), F32),
            vmem((ways, rows, cols), BF16),
            vmem((ways, rows, cols), F32),
            vmem((2, rows, cols), BF16),
            vmem((2, rows, width), BF16),
            vmem((2, rows, width), BF16),
            vmem((ways, rows, head_cols), BF16),
            vmem((tokens, head_cols), BF16),
            vmem((tokens, head_cols), BF16),
            vmem((tokens, head_cols), BF16),
            vmem((tokens, head_cols), BF16),
            vmem((tokens, 128), F32),
            vmem((tokens, 128), F32),
            vmem((tokens, 128), F32),
            vmem((8, tokens), F32),
            vmem((tokens, 8), F32),
            dma((2, 2, ways, PIECES)),
            dma((2, ways, PIECES)),
            dma((2, ways, PIECES)),
            dma((2, ways, PIECES)),
            dma((groups, ways, 4)),
            dma((groups, ways, 4)),
            dma((2, groups, ways, 2)),
            dma((2, groups, ways, 2)),
            dma((groups, ways, 2)),
            dma((groups, ways, 2)),
            dma((ways,)),
            dma((ways,)),
            dma((3,)),
            dma((2, ways)),
            dma((7, ways)),
            dma((7,)),
        ],
        compiler_params=pltpu.CompilerParams(
            collective_id=0, has_side_effects=True, vmem_limit_bytes=62 * MIB
        ),
    )(
        x, g, w1, w2, wq, wd, ids,
        gain.reshape(1, width), shift.reshape(1, width), fc1_shift.reshape(1, cols),
        qkv_shift.reshape(1, 3 * head_cols), frequencies(),
    )
    return outs


def backward_body(
    ways,
    p0, ngm, normed, xh, g, hg, hidden, q, k, v, mg, mix, lse, cos, sin, wa, labels, small,
    out, g1, g2, gq, gd, tin, smallo,
    lt, ra, rb, wp, qv, kv, vv, mgv, lsev, cosv, sinv, dkv, dvv, labr, labc,
    acc, zin, tst, ngi, xhi, ngs, gown, gsend, first_in, second_in, sums, sum_in, sum_out,
    tps, tpr, zs, zr, fs, fr, ss, sr, ws, wr, os, orr, loc, tloc, sms, smr, ins, lts, ngl,
):
    dp, me, core, dpx, dpy = place_of()
    rows, width = out.shape[1:]
    half = rows // 2
    piece = half // PIECES
    groups = first_in.shape[0]
    span_rows = gown.shape[3]
    lanes = gown.shape[4]
    depth = span_rows // ways
    cols, head_cols = hg.shape[1], q.shape[1]
    nxt = (dpx, dpy)
    far = dpx + dpy - dp
    scale = 1.0 / math.sqrt(HD)

    order = (0, 3, 1, 2)

    def part(which, s):
        return pl.ds(pl.multiple_of(which * half + s * piece, 16), piece)

    def loop(count, body):
        lax.fori_loop(0, count, lambda i, c: (body(i), c)[1], 0)

    def add(dst, src, height):
        step = 32

        def body(i):
            at = pl.ds(pl.multiple_of(i * step, step), step)
            dst[at, :] = dst[at, :] + src[at, :]

        loop(height // step, body)

    def swap(a, d, s):
        at = pl.ds(s * piece, piece)
        src = p0.at[d, part(1 - core, s), :] if a == 0 else ngs.at[order.index(d) % 2, at, :]
        return remote(
            src, tin.at[a, d, s], tps.at[a, d, s], tpr.at[a, d, s], (dp, me, 1 - core)
        )

    def load(d, s):
        return pltpu.make_async_copy(p0.at[d, part(core, s), :], acc.at[0, d, s], loc.at[d, s])

    def load_swapped(a, d, s):
        return pltpu.make_async_copy(tin.at[a, d, s], tst.at[s], tloc.at[a, d, s])

    def slot(d, side):
        if side:
            return d
        here = 1 - jnp.minimum(jnp.abs(me - 1 - d), 1)
        return d + here * (ways - d)

    def came(d, side):
        if side:
            return d
        here = 1 - jnp.minimum(jnp.abs(me - d), 1)
        return d + here * (ways - d)

    def stream(a, d, s, side):
        return remote(
            acc.at[a, d, s],
            zin.at[a, slot(d, side), s],
            zs.at[a, d, s],
            zr.at[a, slot(d, side), s],
            (dp, me - 1 + 2 * side, core),
        )

    def arrived(a, d, s, side):
        ref = zin.at[a, came(d, side), s]
        return remote(
            ref, ref, zs.at[a, d, s], zr.at[a, came(d, side), s], (dp, me - 1 + 2 * side, core)
        )

    def finish(a, s, which):
        ref = out.at[a, part(which, s), :]
        return remote(acc.at[a, me, s], ref, os.at[0, a, s], orr.at[a, s], (dp, me, 1 - core))

    def finish_here(a, s):
        return pltpu.make_async_copy(acc.at[a, me, s], out.at[a, part(core, s), :], os.at[1, a, s])

    def merge(a, d):
        for s in range(PIECES):
            swap(a, d, s).wait_recv()
            load_swapped(a, d, s).start()
        for s in range(PIECES):
            load_swapped(a, d, s).wait()
            if a == 0:
                load(d, s).wait()
            add(acc.at[a, d, s], tst.at[s], piece)
            pl.when((me == 0) & (d > 0))(lambda: stream(a, d, s, 1).start())
            pl.when((me == ways - 1) & (d < ways - 1))(lambda: stream(a, d, s, 0).start())

    def hop(a, far_by, j, s):
        d = ways - 1 - j

        @pl.when(me == far_by)
        def _():
            arrived(a, d, s, 1).wait_recv()
            add(acc.at[a, d, s], zin.at[a, came(d, 1), s], piece)
            if d > far_by:
                stream(a, d, s, 1).start()

        @pl.when(me == ways - 1 - far_by)
        def _():
            arrived(a, j, s, 0).wait_recv()
            add(acc.at[a, j, s], zin.at[a, came(j, 0), s], piece)
            if j < ways - 1 - far_by:
                stream(a, j, s, 0).start()

    def last(a):
        for s in range(PIECES):
            finish(a, s, core).start()
            finish_here(a, s).start()

    def lanes_of(path):
        return pl.ds(path * lanes, lanes)

    def first(grp, path, i):
        return remote(
            gsend.at[2 * i + path],
            first_in.at[grp, path, i],
            fs.at[grp, path, i],
            fr.at[grp, path, i],
            (nxt[path], me, core),
        )

    def second(grp, path):
        return remote(
            gown.at[grp % 2, path, 0],
            second_in.at[grp, path],
            ss.at[grp, path],
            sr.at[grp, path],
            (nxt[1 - path], me, core),
        )

    def pieces(grp, path, d):
        ref = gown.at[grp % 2, path, 1]
        across = pl.ds(pl.multiple_of(me * cols + path * lanes, 128), lanes)
        heads = pl.ds(pl.multiple_of(me * head_cols, 128), head_cols)
        rows_of_d = pl.ds(pl.multiple_of(d * depth, 128), depth)
        if grp == 0:
            return [(ref.at[rows_of_d, :], g1.at[:, across])]
        if grp == 1:
            return [(ref.at[:, rows_of_d], g2.at[across, :])]
        if path == 0:
            return [
                (ref.at[rows_of_d, pl.ds(c * head_cols, head_cols)], gq.at[c, :, heads])
                for c in range(2)
            ]
        per = head_cols // depth
        dense_rows = pl.ds(pl.multiple_of(d // per * head_cols, 128), head_cols)
        dense_lanes = pl.ds(pl.multiple_of(head_cols + d % per * depth, 128), depth)
        return [
            (ref.at[rows_of_d, pl.ds(0, head_cols)], gq.at[2, :, heads]),
            (ref.at[dense_rows, dense_lanes], gd.at[heads, :]),
        ]

    def share(grp, path, i):
        d = (me + i) % ways
        return [
            remote(src, dst, ws.at[grp, path, i, n], wr.at[grp, path, i, n], (dp, d, core))
            for n, (src, dst) in enumerate(pieces(grp, path, d))
        ]

    def keep(grp, path):
        return [
            pltpu.make_async_copy(src, dst, ws.at[grp, path, 0, n])
            for n, (src, dst) in enumerate(pieces(grp, path, me))
        ]

    def start(copies):
        for copy in copies:
            copy.start()

    def wait(copies):
        for copy in copies:
            copy.wait()

    def wait_recv(copies):
        for copy in copies:
            copy.wait_recv()

    def wait_send(copies):
        for copy in copies:
            copy.wait_send()

    quarters = (far, dpx, dpy, dp)

    def load_left(grp, r, which=0):
        at = pl.ds(pl.multiple_of(quarters[r] * span_rows, 128), span_rows)
        src = (normed, g, normed)[grp] if which == 0 else g
        into = (4 * grp + r) % 2 if grp < 2 else which
        return pltpu.make_async_copy(src.at[:, at], lt.at[into], lts.at[grp, r, which])

    def products(grp, r):
        load_left(grp, r).wait()
        if grp == 2:
            load_left(grp, r, 1).wait()
        elif 4 * grp + r < 7:
            after = 4 * grp + r + 1
            load_left(after // 4, after % 4).start()
        left = (4 * grp + r) % 2 if grp < 2 else 0
        for path in range(2):
            if r == 0:
                dst = gsend.at[path]
                i = 0
            elif r == 1 + path:
                dst = gsend.at[2 + path]
                i = 1
            else:
                dst = gown.at[grp % 2, path, 1 if r == 3 else 0]
                i = None
            if i is not None and grp:
                first(grp - 1, path, i).wait_send()
            if i is None and grp == 2:
                if r == 3:
                    wait(keep(0, path))
                    for n in range(1, ways):
                        wait_send(share(0, path, n))
                else:
                    second(0, path).wait_send()
            right = (ra, rb, ra)[grp]
            if grp == 1:
                dst[...] = dot_tn(right[:, lanes_of(path)], lt[left]).astype(BF16)
            elif grp == 2 and path == 1:
                dst[:, :head_cols] = dot_tn(lt[0], right[:, 2 * head_cols : 3 * head_cols]).astype(BF16)
                dense = dot_tn(right[:, 3 * head_cols :], lt[1]).astype(BF16)
                dst[:head_cols, head_cols:] = dense[:, :head_cols]
                dst[head_cols:, head_cols:] = dense[:, head_cols:]
            else:
                dst[...] = dot_tn(lt[left], right[:, lanes_of(path)]).astype(BF16)
            if i is not None:
                first(grp, path, i).start()
        if grp == 2 and r < 3:
            load_left(grp, r + 1).start()
            load_left(grp, r + 1, 1).start()

    def pass_sum(grp, path):
        first(grp, path, 0).wait_recv()
        add(gown.at[grp % 2, path, 0], first_in.at[grp, path, 0], span_rows)
        second(grp, path).start()

    def first_sum(grp, path):
        first(grp, path, 1).wait_recv()
        add(gown.at[grp % 2, path, 1], first_in.at[grp, path, 1], span_rows)

    def second_sum(grp, path):
        second(grp, path).wait_recv()
        add(gown.at[grp % 2, path, 1], second_in.at[grp, path], span_rows)
        for i in range(1, ways):
            start(share(grp, path, i))
        start(keep(grp, path))

    pairs = (
        (hg, ra), (hidden, rb), (wa, wp),
        (q, qv), (k, kv), (v, vv), (mg, mgv), (lse, lsev), (cos, cosv), (sin, sinv),
    )

    def copy_in(i):
        return pltpu.make_async_copy(*pairs[i], ins.at[i])

    mix_in = pltpu.make_async_copy(mix, ra.at[:, pl.ds(3 * head_cols, head_cols)], ins.at[10])

    def begin():
        for i in range(3, 10):
            copy_in(i).wait()
        mix_in.start()
        for o in range(ways):
            at = slice(o * rows, (o + 1) * rows)
            rows_here = labels[o].astype(F32)
            labr[:, at] = rows_here
            labc[at, :] = jnp.transpose(rows_here)

    def turned_back(value, at):
        return turn(value, cosv[at, :], -sinv[at, :]).astype(BF16)

    def attend_back(pair, i):
        at = pl.ds(pair * 128, 128)
        here, seen = pl.ds(i * QUERIES, QUERIES), pl.ds(0, (i + 1) * QUERIES)
        allowed = allowed_keys(labr, labc, i)
        head = lax.broadcasted_iota(jnp.int32, (QUERIES, 128), 1) < HD
        if i == 0:
            dkv[...] = jnp.zeros_like(dkv)
            dvv[...] = jnp.zeros_like(dvv)
        keys, values = kv[seen, at], vv[seen, at]
        parts = []
        for sub in range(2):
            mine = head if sub == 0 else ~head
            qi = jnp.where(mine, qv[here, at], 0)
            mi = jnp.where(mine, mgv[here, at], 0)
            log = lsev[here, pair * 2 + sub : pair * 2 + sub + 1]
            probs = jnp.where(allowed, jnp.exp(dot_nt(qi, keys) - log), 0.0)
            prob_grad = dot_nt(mi, values)
            delta = jnp.sum(probs * prob_grad, 1, keepdims=True)
            score_grad = (probs * (prob_grad - delta)).astype(BF16)
            parts.append(dot_nn(score_grad, keys))
            dkv[seen, :] += dot_tn(score_grad, qi)
            dvv[seen, :] += dot_tn(probs.astype(BF16), mi)
        ra[here, at] = turned_back(jnp.where(head, parts[0], parts[1]) * scale, here)
        if i == rows * ways // QUERIES - 1:
            ra[:, pl.ds(head_cols + pair * 128, 128)] = turned_back(dkv[...], slice(None))
            ra[:, pl.ds(2 * head_cols + pair * 128, 128)] = dvv[...].astype(BF16)

    def load_back(d, own):
        at = pl.ds(pl.multiple_of((core if own else 1 - core) * half, 16), half)
        return [
            pltpu.make_async_copy(ngm.at[d, at, :], ngi.at[own], ngl.at[0, d, own]),
            pltpu.make_async_copy(xh.at[d, at, :], xhi.at[own], ngl.at[1, d, own]),
        ]

    def normed_back(n):
        d = order[n]
        if n == 0:
            copy_in(2).wait()
            sums[...] = small[...]
        if n >= 2:
            for s in range(PIECES):
                swap(1, order[n - 2], s).wait_send()
        wide = 512
        for own in range(2):
            for copy in load_back(d, own):
                copy.wait()
            at = pl.ds(pl.multiple_of(d * rows + (core if own else 1 - core) * half, 16), half)

            def mul(i):
                cols = pl.ds(pl.multiple_of(i * wide, wide), wide)
                tile = dot_nt(ra[at, : 3 * head_cols], wp[cols, :]) + ngi[own, :, cols].astype(F32)
                sums[0:1, cols] += jnp.sum(tile * xhi[own, :, cols].astype(F32), 0, keepdims=True)
                sums[1:2, cols] += jnp.sum(tile, 0, keepdims=True)
                tile = tile.astype(BF16)
                for s in range(PIECES):
                    if own:
                        acc[1, d, s, :, cols] = tile[s * piece : (s + 1) * piece]
                    else:
                        ngs[n % 2, s * piece : (s + 1) * piece, cols] = tile[s * piece : (s + 1) * piece]

            loop(width // wide, mul)
            if not own:
                for s in range(PIECES):
                    swap(1, d, s).start()
            if n < ways - 1:
                for copy in load_back(order[n + 1], own):
                    copy.start()

    def small_send(i):
        src = sums if i == 0 else sum_out.at[i - 1]
        device = ((dp, me, 1 - core), (dpx, me, core), (dpy, me, core))[i]
        return remote(src, sum_in.at[i], sms.at[i], smr.at[i], device)

    def small_all(i):
        device = (dp, (me + i) % ways, core)
        return remote(sum_out.at[2], smallo.at[me], sms.at[2 + i], smr.at[2 + i], device)

    def small_begin():
        sums[4:5, : 3 * head_cols] = jnp.sum(ra[:, : 3 * head_cols].astype(F32), 0, keepdims=True)
        small_send(0).start()

    def small_step(i):
        small_send(i).wait_recv()
        before = sums[...] if i == 0 else sum_out[i - 1]
        after = before + sum_in[i]
        if i == 0:
            row = lax.broadcasted_iota(jnp.int32, after.shape, 0)
            after = jnp.where(row < 2, after, before)
        sum_out[i] = after
        if i < 2:
            small_send(i + 1).start()
        else:
            for n in range(1, ways):
                small_all(n).start()
            smallo[me] = after

    greet(ways)
    for d in order:
        for s in range(PIECES):
            swap(0, d, s).start()
            load(d, s).start()
    load_left(0, 0).start()
    for i in range(len(pairs)):
        copy_in(i).start()
    for own in range(2):
        for copy in load_back(order[0], own):
            copy.start()
    copy_in(0).wait()
    copy_in(1).wait()

    def last_left():
        mix_in.wait()
        load_left(2, 0).start()
        load_left(2, 0, 1).start()

    steps = dict(
        t=products,
        f=pass_sum,
        F=first_sum,
        h=second_sum,
        m=merge,
        z=hop,
        o=last,
        B=begin,
        a=attend_back,
        L=last_left,
        n=normed_back,
        Y=small_begin,
        y=small_step,
    )
    plan = (
        "t00", "m00", "m03", "t01", "t02", "m01", "t03", "f01", "z0100", "B", "a00", "a01", "a02",
        "z0101", "a03", "a04", "a05", "F01", "F00", "t10", "m02", "z0200", "a10", "h01", "a11",
        "t11", "a12", "t12", "z0110", "a13", "f00", "a14", "a15", "n0", "n1", "z0111", "m10",
        "m13", "h00", "n2", "f10", "z0300", "n3", "f11", "m12", "m11", "z0201", "t13", "F10",
        "z1100", "L", "Y", "z1101", "y0", "z0210", "z0120", "z0121", "F11", "h10", "z0211", "y1",
        "t20", "y2", "h11", "z1200", "z1110", "z0301", "t21", "t22", "f21", "z1120", "z1121",
        "f20", "z1201", "z1300", "z1301", "t23", "z1111", "F20", "h20", "z1210", "z1211", "o1",
        "o0", "F21", "h21",
    )
    for word in plan:
        steps[word[0]](*(int(digit) for digit in word[1:]))

    for i in range(3):
        small_send(i).wait_send()
    for i in range(1, ways):
        small_all(i).wait()
    for a in range(2):
        for s in range(PIECES):
            finish(a, s, core).wait_send()
            finish_here(a, s).wait()
            finish(a, s, 1 - core).wait_recv()
            for n, d in enumerate(order):
                if a == 0 or n >= 2:
                    swap(a, d, s).wait_send()
                pl.when(d > me)(lambda: stream(a, d, s, 1).wait_send())
                pl.when(d < me)(lambda: stream(a, d, s, 0).wait_send())
    for grp in range(groups):
        for path in range(2):
            if grp == 2:
                for i in range(2):
                    first(grp, path, i).wait_send()
            if grp:
                second(grp, path).wait_send()
                wait(keep(grp, path))
            for i in range(1, ways):
                wait_recv(share(grp, path, i))
                if grp:
                    wait_send(share(grp, path, i))


def backward(p0, ngm, normed, xh, g, hg, hidden, q, k, v, mg, mix, lse, cos, sin, wa, labels, small):
    ways, rows, width = p0.shape
    chips = lax.axis_size("dp")
    tokens = ways * rows
    groups, cols, head_cols = 3, hg.shape[-1], q.shape[-1]
    span = width // chips
    lanes = cols // 2
    piece = rows // 2 // PIECES
    half = rows // 2
    dma = pltpu.SemaphoreType.DMA
    vmem = pltpu.VMEM
    anywhere = pl.BlockSpec(memory_space=pl.ANY)
    inside = pl.BlockSpec(memory_space=pltpu.VMEM)
    flat = lambda t: t.reshape(tokens, t.shape[-1])
    depth = span // ways
    out, g1, g2, gq, gd, unused, smallo = pl.pallas_call(
        functools.partial(backward_body, ways),
        in_specs=[anywhere] * 16 + [inside] * 2,
        out_specs=[anywhere] * 6 + [inside],
        out_shape=[
            jax.ShapeDtypeStruct((2, rows, width), BF16),
            jax.ShapeDtypeStruct((depth, ways * cols), BF16),
            jax.ShapeDtypeStruct((ways * cols, depth), BF16),
            jax.ShapeDtypeStruct((3, depth, ways * head_cols), BF16),
            jax.ShapeDtypeStruct((ways * head_cols, depth), BF16),
            jax.ShapeDtypeStruct((2, ways, PIECES, piece, width), BF16),
            jax.ShapeDtypeStruct((ways,) + small.shape, F32),
        ],
        scratch_shapes=[
            vmem((2, tokens, span), BF16),
            vmem((tokens, cols), BF16),
            vmem((tokens, cols), BF16),
            vmem((width, 3 * head_cols), BF16),
            vmem((tokens, head_cols), BF16),
            vmem((tokens, head_cols), BF16),
            vmem((tokens, head_cols), BF16),
            vmem((tokens, head_cols), BF16),
            vmem((tokens, 128), F32),
            vmem((tokens, 128), F32),
            vmem((tokens, 128), F32),
            vmem((tokens, 128), F32),
            vmem((tokens, 128), F32),
            vmem((8, tokens), F32),
            vmem((tokens, 8), F32),
            vmem((2, ways, PIECES, piece, width), BF16),
            vmem((2, ways + 1, PIECES, piece, width), BF16),
            vmem((PIECES, piece, width), BF16),
            vmem((2, half, width), BF16),
            vmem((2, half, width), BF16),
            vmem((2, half, width), BF16),
            vmem((2, 2, 2, span, lanes), BF16),
            vmem((4, span, lanes), BF16),
            vmem((groups, 2, 2, span, lanes), BF16),
            vmem((groups, 2, span, lanes), BF16),
            vmem(small.shape, F32),
            vmem((3,) + small.shape, F32),
            vmem((3,) + small.shape, F32),
            dma((2, ways, PIECES)),
            dma((2, ways, PIECES)),
            dma((2, ways, PIECES)),
            dma((2, ways + 1, PIECES)),
            dma((groups, 2, 2)),
            dma((groups, 2, 2)),
            dma((groups, 2)),
            dma((groups, 2)),
            dma((groups, 2, ways, 2)),
            dma((groups, 2, ways, 2)),
            dma((2, 2, PIECES)),
            dma((2, PIECES)),
            dma((ways, PIECES)),
            dma((2, ways, PIECES)),
            dma((2 + ways,)),
            dma((2 + ways,)),
            dma((11,)),
            dma((groups, 4, 2)),
            dma((2, ways, 2)),
        ],
        compiler_params=pltpu.CompilerParams(
            collective_id=1, has_side_effects=True, vmem_limit_bytes=63 * MIB
        ),
    )(
        p0, ngm, flat(normed), xh, flat(g), flat(hg), flat(hidden), q, k, v, flat(mg), mix,
        lse, cos, sin, wa, labels, small,
    )
    grads = tuple(t.astype(F32) for t in (gq, gd, g1, g2))
    return out[0].astype(F32), out[1].astype(F32), grads, smallo


def layer_norm(x):
    xf = x.astype(F32)
    mean = jnp.mean(xf, -1, keepdims=True)
    centred = xf - mean
    inv_std = lax.rsqrt(jnp.mean(centred * centred, -1, keepdims=True) + EPS)
    return centred * inv_std, inv_std


def plain_work(
    x, g, w_qkv, w_dense, w_fc1, w_fc2, places, segments, gain, shift, fc1_shift, qkv_shift
):
    me, ways = lax.axis_index("ctx"), lax.axis_size("ctx")
    width = x.shape[1]
    depth = w_fc1.shape[0]
    cols, head_cols = w_fc1.shape[1] // ways, w_dense.shape[0] // ways
    fc1 = w_fc1.reshape(depth, ways, cols).transpose(1, 0, 2)
    fc2 = w_fc2.reshape(ways, cols, depth).transpose(0, 2, 1)
    qkv = w_qkv.reshape(3, depth, ways, head_cols).transpose(2, 1, 0, 3)
    dense = w_dense.reshape(ways, head_cols, depth).transpose(0, 2, 1)
    att = jnp.concatenate([qkv.reshape(ways, depth, 3 * head_cols), dense], -1)
    wsrc = jnp.stack([fc1, fc2, att])
    x_all, g_all, weights, places, segments = gather_plain(x, g, wsrc, places, segments)
    weights = weights.reshape(3, width, cols)
    w1, w2, wa = weights[0], weights[1], weights[2]
    wp, wd = wa[:, : 3 * head_cols], wa[:, 3 * head_cols :]
    x_hat, unused = layer_norm(x_all)
    normed = (x_hat * gain + shift).astype(BF16)
    projected = dot_nn(normed, wp) + qkv_shift.reshape(1, 3 * head_cols)
    mix_grad = dot_nn(g_all, wd).astype(BF16)
    mixture, gq, gk, gv = attention_plain(
        projected[:, :head_cols],
        projected[:, head_cols : 2 * head_cols],
        projected[:, 2 * head_cols :],
        mix_grad,
        places,
        segments,
    )
    proj_grad = jnp.concatenate([gq, gk, gv], 1)

    hidden_pre = dot_nn(normed, w1) + fc1_shift
    hidden, slope = gelu_and_slope(hidden_pre)
    hidden = hidden.astype(BF16)
    hidden_grad = (dot_nn(g_all, w2) * slope).astype(BF16)

    out_part = (dot_nt(mixture, wd) + dot_nt(hidden, w2)).astype(BF16)
    normed_part = dot_nt(proj_grad, wp) + dot_nt(hidden_grad, w1)
    weight_part = jnp.stack(
        [
            dot_tn(normed, hidden_grad).astype(BF16),
            dot_tn(g_all, hidden).astype(BF16),
            jnp.concatenate([dot_tn(normed, proj_grad), dot_tn(g_all, mixture)], 1).astype(BF16),
        ]
    )
    qkv_bias_part = jnp.sum(proj_grad.astype(F32), 0).reshape(3, head_cols)
    fc1_bias_part = jnp.sum(hidden_grad.astype(F32), 0)
    branches, normed_grad, weight_grads = scatter_plain(
        out_part, normed_part.astype(BF16), weight_part.reshape(3, -1, depth, cols)
    )
    place = lambda t, whole, axis: lax.dynamic_update_slice_in_dim(
        jnp.zeros(whole, F32), t, me * t.shape[axis], axis
    )
    small = lax.psum(
        (
            place(qkv_bias_part, (3, head_cols * ways), 1),
            place(fc1_bias_part, (cols * ways,), 0),
            jnp.sum(g.astype(F32), 0),
        ),
        ("dp", "ctx"),
    )
    norms = lax.psum(
        (jnp.sum(normed_part * x_hat, 0), jnp.sum(normed_part, 0)), ("dp", "ctx", "tp")
    )
    grad_fc1 = weight_grads[0].transpose(1, 0, 2).reshape(depth, ways * cols)
    grad_fc2 = weight_grads[1].transpose(0, 2, 1).reshape(ways * cols, depth)
    grad_att = weight_grads[2].reshape(ways, depth, 4, head_cols)
    grad_qkv = grad_att[:, :, :3].transpose(2, 1, 0, 3).reshape(3, depth, ways * head_cols)
    grad_dense = grad_att[:, :, 3].transpose(0, 2, 1).reshape(ways * head_cols, depth)
    weight_grads = (grad_qkv, grad_dense, grad_fc1, grad_fc2)
    return branches, normed_grad, weight_grads, norms + small


def fast_work(
    x, g, w_qkv, w_dense, w_fc1, w_fc2, places, segments, gain, shift, fc1_shift, qkv_shift
):
    ways = lax.axis_size("ctx")
    rows, width = x.shape
    cols, head_cols = w_fc1.shape[1] // ways, w_dense.shape[0] // ways
    ids = jnp.zeros((8, rows), jnp.int32).at[0].set(places).at[1].set(segments)
    (
        g_all, normed, x_hat, hidden, hidden_grad, out_part, back_mlp, mix_grad, wa,
        q, k, v, mixture, lse, cos, sin, labels, fc1_sum, unused,
    ) = forward(x, g, w_fc1, w_fc2, w_qkv, w_dense, ids, gain, shift, fc1_shift, qkv_shift)
    line = lambda t: jnp.pad(t.reshape(1, -1), ((0, 0), (0, width - t.size)))
    none = jnp.zeros((1, width), F32)
    small = jnp.concatenate(
        [none, none, jnp.sum(g.astype(F32), 0, keepdims=True), line(fc1_sum)] + [none] * 4
    )
    branches, normed_grad, weight_grads, sums = backward(
        out_part, back_mlp, normed, x_hat, g_all, hidden_grad, hidden,
        q, k, v, mix_grad, mixture, lse, cos, sin, wa, labels, small,
    )
    total = jnp.sum(sums[:, :3], 0)
    fc1_bias_sum = sums[:, 3, :cols].reshape(ways * cols)
    qkv_bias_sum = sums[:, 4, : 3 * head_cols].reshape(ways, 3, head_cols).transpose(1, 0, 2)
    return (
        branches,
        normed_grad,
        weight_grads,
        (total[0], total[1], qkv_bias_sum.reshape(3, ways * head_cols), fc1_bias_sum, total[2]),
    )


def per_device(
    block_input,
    cotangent,
    segment_ids,
    positions,
    norm_gain,
    norm_bias,
    w_qkv,
    qkv_bias,
    w_dense,
    w_fc1,
    fc1_bias,
    w_fc2,
    out_bias,
):
    ways = lax.axis_size("ctx")
    me = lax.axis_index("ctx")
    x, g = block_input[0], cotangent[0]
    rows, width = x.shape
    cols, head_cols = w_fc1.shape[1] // ways, w_dense.shape[0] // ways

    gain, shift = norm_gain.astype(F32), norm_bias.astype(F32)
    qkv_shift = lax.dynamic_slice_in_dim(qkv_bias, me * head_cols, head_cols, 1).astype(F32)
    fc1_shift = lax.dynamic_slice_in_dim(fc1_bias, me * cols, cols, 0).astype(F32)
    fast = ways == 4 and lax.axis_size("dp") == 4 and rows % 128 == 0
    fast = fast and head_cols == 256 and x.shape[1] == 8 * head_cols
    work = fast_work if fast else plain_work
    branches, normed_grad, weight_grads, sums = work(
        x, g, w_qkv, w_dense, w_fc1, w_fc2, positions[0], segment_ids[0], gain, shift, fc1_shift, qkv_shift
    )

    gf = g.astype(F32)
    output = (x.astype(F32) + branches + out_bias.astype(F32)).astype(BF16)
    own_hat, inv_std = layer_norm(x)
    scaled = normed_grad * gain
    grad_input = gf + inv_std * (
        scaled
        - jnp.mean(scaled, -1, keepdims=True)
        - own_hat * jnp.mean(scaled * own_hat, -1, keepdims=True)
    )
    gain_sum, shift_sum, qkv_bias_sum, fc1_bias_sum, out_bias_sum = sums

    grad_qkv, grad_dense, grad_fc1, grad_fc2 = weight_grads
    return (
        output[None],
        grad_input.astype(BF16)[None],
        gain_sum,
        shift_sum,
        grad_qkv,
        qkv_bias_sum,
        grad_dense,
        grad_fc1,
        fc1_bias_sum,
        grad_fc2,
        out_bias_sum,
    )


def solution(mesh):
    placed = (
        P("dp", "ctx", None),
        P("dp", "ctx", None),
        P("dp", "ctx"),
        P("dp", "ctx"),
        P(),
        P(),
        P(None, ("dp", "ctx"), "tp"),
        P(None, "tp"),
        P("tp", ("dp", "ctx")),
        P(("dp", "ctx"), "tp"),
        P("tp"),
        P("tp", ("dp", "ctx")),
        P(),
    )
    return jax.shard_map(
        per_device,
        mesh=mesh,
        in_specs=placed,
        out_specs=(
            P("dp", "ctx", None),
            P("dp", "ctx", None),
            P(),
            P(),
            P(None, ("dp", "ctx"), "tp"),
            P(None, "tp"),
            P("tp", ("dp", "ctx")),
            P(("dp", "ctx"), "tp"),
            P("tp"),
            P("tp", ("dp", "ctx")),
            P(),
        ),
        check_vma=False,
    )
```

```python
import functools
import math

import jax
import jax.numpy as jnp
import numpy as np
from jax import lax
from jax.experimental import pallas as pl
from jax.experimental.pallas import tpu as pltpu
from jax.sharding import PartitionSpec as P

HD = 64
ROT = 32
EPS = 1e-05
MIB = 1 << 20
F32 = jnp.float32
BF16 = jnp.bfloat16
MESH = pl.DeviceIdType.MESH


def dot_nn(a, b):
    return lax.dot_general(a, b, (((1,), (0,)), ((), ())), preferred_element_type=F32)


def dot_nt(a, b):
    return lax.dot_general(a, b, (((1,), (1,)), ((), ())), preferred_element_type=F32)


def dot_tn(a, b):
    return lax.dot_general(a, b, (((0,), (0,)), ((), ())), preferred_element_type=F32)


QUERIES = 256


def frequencies():
    half = ROT // 2
    some = 10000.0 ** (-(np.arange(half, dtype=np.float32) * np.float32(2.0 / ROT)))
    one = np.concatenate([some, some, np.zeros(HD - ROT)]).astype(np.float32)
    return np.concatenate([one, one])[None, :]


def turn(v, cos, sin):
    half = ROT // 2
    lane = lax.broadcasted_iota(jnp.int32, v.shape, 1) % HD
    left, right = pltpu.roll(v, 128 - half, 1), pltpu.roll(v, half, 1)
    return v * cos + jnp.where(lane < half, -left, right) * sin


def allowed_keys(labr, labc, i):
    shape = (QUERIES, (i + 1) * QUERIES)
    row = lax.broadcasted_iota(jnp.int32, shape, 0) + i * QUERIES
    col = lax.broadcasted_iota(jnp.int32, shape, 1)
    here = pl.ds(i * QUERIES, QUERIES)
    return (col <= row) & (labc[here, 1:2] == labr[1:2, 0 : (i + 1) * QUERIES])


def attention_plain(pq, pk, pv, mg, places, segments):
    rows, cols = pq.shape
    heads = cols // HD
    half = ROT // 2
    scale = 1.0 / math.sqrt(HD)
    frequency = 10000.0 ** (-(jnp.arange(half, dtype=F32) * 2.0 / ROT))
    angles = places.astype(F32)[:, None] * frequency[None, :]
    cos, sin = jnp.cos(angles)[:, None, :], jnp.sin(angles)[:, None, :]

    def rotate(t, s):
        t = t.reshape(rows, heads, HD)
        a, b = t[..., :half], t[..., half:ROT]
        return jnp.concatenate([a * cos - b * s, b * cos + a * s, t[..., ROT:]], -1)

    q = rotate(pq, sin).astype(BF16)
    k = rotate(pk, sin).astype(BF16)
    v = pv.astype(BF16).reshape(rows, heads, HD)
    m = mg.reshape(rows, heads, HD)
    span = 256
    index = jnp.arange(rows, dtype=jnp.int32)

    def step(carry, items):
        dk, dv = carry
        qi, mi, row_index, row_seg = items
        scores = jnp.einsum("qhd,khd->hqk", qi, k, preferred_element_type=F32) * scale
        allowed = (index[None, :] <= row_index[:, None]) & (segments[None, :] == row_seg[:, None])
        scores = jnp.where(allowed[None], scores, -1e30)
        expo = jnp.exp(scores - jnp.max(scores, -1, keepdims=True))
        probs = expo / jnp.sum(expo, -1, keepdims=True)
        low = probs.astype(BF16)
        out = jnp.einsum("hqk,khd->qhd", low, v, preferred_element_type=F32).astype(BF16)
        prob_grad = jnp.einsum("qhd,khd->hqk", mi, v, preferred_element_type=F32)
        delta = jnp.sum(probs * prob_grad, -1, keepdims=True)
        score_grad = (probs * (prob_grad - delta)).astype(BF16)
        dq = jnp.einsum("hqk,khd->qhd", score_grad, k, preferred_element_type=F32) * scale
        dk = dk + jnp.einsum("hqk,qhd->khd", score_grad, qi, preferred_element_type=F32) * scale
        dv = dv + jnp.einsum("hqk,qhd->khd", low, mi, preferred_element_type=F32)
        return (dk, dv), (out, dq)

    zero = jnp.zeros((rows, heads, HD), F32)
    cut = lambda t: t.reshape((rows // span, span) + t.shape[1:])
    (dk, dv), (out, dq) = lax.scan(step, (zero, zero), (cut(q), cut(m), cut(index), cut(segments)))
    flat = lambda t: t.reshape(rows, cols)
    return (
        flat(out),
        flat(rotate(dq.reshape(rows, cols), -sin)).astype(BF16),
        flat(rotate(dk.reshape(rows, cols), -sin)).astype(BF16),
        flat(dv).astype(BF16),
    )


def gather_plain(x, g, wsrc, places, segments):
    pieces = lax.all_to_all(wsrc, "ctx", split_axis=1, concat_axis=1, tiled=True)
    weights = lax.all_gather(pieces, "dp", axis=1, tiled=True)
    along = lambda t: lax.all_gather(t, "ctx", axis=0, tiled=True)
    return along(x), along(g), weights, along(places), along(segments)


def scatter_plain(out_part, normed_part, weight_part):
    summed = lambda t: lax.psum(
        lax.psum_scatter(t, "ctx", scatter_dimension=0, tiled=True), "tp"
    ).astype(F32)
    pieces = lax.psum_scatter(weight_part, "dp", scatter_dimension=1, tiled=True)
    pieces = lax.all_to_all(pieces, "ctx", split_axis=1, concat_axis=1, tiled=True)
    return summed(out_part), summed(normed_part), pieces.astype(F32)


def place_of():
    dp, me, core = lax.axis_index("dp"), lax.axis_index("ctx"), lax.axis_index("tp")
    return dp, me, core, dp + 1 - 2 * (dp % 2), dp + 2 - 4 * (dp // 2)


def greet(ways):
    dp, me, core, dpx, dpy = place_of()
    barrier = pltpu.get_barrier_semaphore()
    for device in [(dp, me, 1 - core), (dpx, me, core), (dpy, me, core)] + [
        (dp, (me + k) % ways, core) for k in range(1, ways)
    ]:
        pl.semaphore_signal(barrier, inc=1, device_id=device, device_id_type=MESH)
    pl.semaphore_wait(barrier, ways + 2)


def remote(src, dst, send, recv, device):
    return pltpu.make_async_remote_copy(
        src_ref=src, dst_ref=dst, send_sem=send, recv_sem=recv, device_id=device, device_id_type=MESH
    )


PIECES = 2


def gelu_and_slope(v):
    c = math.sqrt(2.0 / math.pi)
    square = v * v
    tanh = jnp.tanh(c * v * (1.0 + 0.044715 * square))
    half = 0.5 * (1.0 + tanh)
    slope = half + 0.5 * c * v * (1.0 - tanh * tanh) * (1.0 + 3.0 * 0.044715 * square)
    return v * half, slope


def forward_body(
    ways, x, g, w1, w2, wq, wd, ids, lines, freq,
    go, no, xho, ho, hgo, outo, ngo, mgo, wao, qo, ko, vo, mixo, lseo, coso, sino, ido, small,
    xo, w1v, w2v, wqv, wdv, norm, xb, gb, pre, hid, slope, hgb, ob, nb, mb, qb, kb, vb, mixb, lse, cosb, sinb, labr, labc,
    zs, zr, ts, tr, ws, wr, ls, lr, ds, dr, ids_s, ids_r, own, ls_in, ls_out, keep_out,
):
    dp, me, core, dpx, dpy = place_of()
    rows, width = x.shape
    piece = rows // 2 // PIECES
    groups, depth = ws.shape[0], w1.shape[0]
    cols, head_cols = w1v.shape[1], wdv.shape[0]
    gain, shift = lines.at[0:1, :], lines.at[1:2, :]
    fc1_shift, qkv_shift = lines.at[2:3, 0:cols], lines.at[3:4, 0 : 3 * head_cols]
    srcs, outs = (x, g), (xo, go)
    blocks = [me, 1 + me % 2, None, 3 * (1 - me // 2)]
    blocks[2] = 6 - me - blocks[1] - blocks[3]

    def part(which, s):
        return pl.ds(pl.multiple_of(which * (rows // 2) + s * piece, 16), piece)

    def along(a, owner, s, side, mine=False):
        at = part(core, s)
        src = srcs[a].at[at, :] if mine else outs[a].at[owner, at, :]
        return remote(
            src,
            outs[a].at[owner, at, :],
            zs.at[side, a, owner, s],
            zr.at[a, owner, s],
            (dp, me - 1 + 2 * side, core),
        )

    def across(a, owner, s, which):
        at = part(which, s)
        ref = outs[a].at[owner, at, :]
        return remote(ref, ref, ts.at[a, owner, s], tr.at[a, owner, s], (dp, me, 1 - core))

    def here(chip, j, height=None):
        return pl.ds(pl.multiple_of((chip * ways + j) * depth, depth), depth)

    def held(grp, chip, j):
        at = here(chip, j)
        return ([w1v.at[at, :]], [w2v.at[:, at]], [wqv.at[at, :], wdv.at[:, at]])[grp]

    def given(grp, d):
        at = here(dp, me)
        mine = pl.ds(pl.multiple_of(d * cols, 128), cols)
        if grp == 0:
            return [(w1.at[:, mine], w1v.at[at, :])]
        if grp == 1:
            return [(w2.at[mine, :], w2v.at[:, at])]
        mine = pl.ds(pl.multiple_of(d * head_cols, 128), head_cols)
        return [
            (wq.at[c, :, mine], wqv.at[at, pl.ds(c * head_cols, head_cols)]) for c in range(3)
        ] + [(wd.at[mine, :], wdv.at[:, at])]

    def share(grp, k):
        d = (me + k) % ways
        return [
            remote(src, dst, ws.at[grp, k, i], wr.at[grp, k, i], (dp, d, core))
            for i, (src, dst) in enumerate(given(grp, d))
        ]

    def keep(grp):
        return [
            pltpu.make_async_copy(src, dst, ws.at[grp, 0, i])
            for i, (src, dst) in enumerate(given(grp, me))
        ]

    def source(k):
        return (me - k + ways) % ways

    def spread(grp, k, axis):
        return [
            remote(ref, ref, ls.at[axis, grp, k, i], lr.at[axis, grp, k, i], ((dpx, dpy)[axis], me, core))
            for i, ref in enumerate(held(grp, dp, source(k)))
        ]

    def corner(grp, k):
        axis = (grp + k) % 2
        return [
            remote(ref, ref, ds.at[grp, k, i], dr.at[grp, k, i], ((dpy, dpx)[axis], me, core))
            for i, ref in enumerate(held(grp, (dpx, dpy)[axis], source(k)))
        ]

    def start(copies):
        for copy in copies:
            copy.start()

    def wait_recv(copies):
        for copy in copies:
            copy.wait_recv()

    def wait_send(copies):
        for copy in copies:
            copy.wait_send()

    def labels(k):
        return remote(ids, ido.at[me], ids_s.at[k], ids_r.at[k], (dp, (me + k) % ways, core))

    def send_own(a, s):
        pl.when(me > 0)(lambda: along(a, me, s, 0, True).start())
        pl.when(me < ways - 1)(lambda: along(a, me, s, 1, True).start())

    def send_share(grp, k):
        if k:
            start(share(grp, k))
            return
        start(keep(grp))
        for copy in keep(grp):
            copy.wait()
        for axis in range(2):
            start(spread(grp, 0, axis))

    def pass_on(a, k, s):
        @pl.when(me + k < ways)
        def _():
            along(a, me + k, s, 0).wait_recv()
            pl.when(me > 0)(lambda: along(a, me + k, s, 0).start())
            across(a, me + k, s, core).start()

        @pl.when(me - k >= 0)
        def _():
            along(a, me - k, s, 1).wait_recv()
            pl.when(me < ways - 1)(lambda: along(a, me - k, s, 1).start())
            across(a, me - k, s, core).start()

    def spread_on(grp, k):
        wait_recv(share(grp, k))
        for axis in range(2):
            start(spread(grp, k, axis))

    def corner_on(grp, k):
        wait_recv(spread(grp, k, (grp + k) % 2))
        start(corner(grp, k))

    def settle(grp):
        for k in range(ways):
            wait_recv(spread(grp, k, 1 - (grp + k) % 2))
            wait_recv(corner(grp, k))

    def arrive(a, t):
        if t:
            for s in range(PIECES):
                across(a, blocks[t], s, 1 - core).wait_recv()

    def loop(count, body):
        lax.fori_loop(0, count, lambda i, c: (body(i), c)[1], 0)

    def load_x(t):
        src = x if t == 0 else xo.at[blocks[t]]
        return pltpu.make_async_copy(src, xb.at[t % 2], ls_in.at[0, t])

    def load_g(t):
        src = g if t == 0 else go.at[blocks[t]]
        return pltpu.make_async_copy(src, gb.at[t % 2], ls_in.at[1, t])

    def store(which, t):
        o = blocks[t]
        src, dst = (
            (xb.at[t % 2], xho.at[o]),
            (norm.at[o], no.at[o]),
            (hid.at[o], ho.at[o]),
            (ob.at[t % 2], outo.at[o]),
            (nb.at[t % 2], ngo.at[o]),
            (hgb.at[t % 2], hgo.at[o]),
            (mb.at[t], mgo.at[o]),
        )[which]
        return pltpu.make_async_copy(src, dst, ls_out.at[which, t])

    def fetch_x(t):
        arrive(0, t)
        if t >= 2:
            store(0, t - 2).wait()
        load_x(t).start()

    def fetch_g(t):
        arrive(1, t)
        if t == 2:
            own_g.wait()
        load_g(t).start()

    own_g = pltpu.make_async_copy(gb.at[0], go.at[me], own.at[0])

    def normalise(t):
        load_x(t).wait()
        step = 192

        def body(i):
            at = pl.ds(pl.multiple_of(i * step, step), step)
            xf = xb[t % 2, at, :].astype(F32)
            centred = xf - jnp.mean(xf, -1, keepdims=True)
            inv_std = lax.rsqrt(jnp.mean(centred * centred, -1, keepdims=True) + EPS)
            x_hat = centred * inv_std
            norm[blocks[t], at, :] = (x_hat * gain[...] + shift[...]).astype(BF16)
            xb[t % 2, at, :] = x_hat.astype(BF16)

        loop(rows // step, body)
        store(0, t).start()
        store(1, t).start()

    wide = 512

    def span(i):
        return pl.ds(pl.multiple_of(i * wide, wide), wide)

    def up(t):
        o = blocks[t]

        def mul(i):
            pre[:, span(i)] = dot_nn(norm[o], w1v[:, span(i)]) + fc1_shift[:, span(i)]

        loop(cols // wide, mul)

        def act(i):
            at = pl.ds(pl.multiple_of(i * 16, 16), 16)
            value, grad = gelu_and_slope(pre[at, :])
            hid[o, at, :] = value.astype(BF16)
            slope[o, at, :] = grad

        loop(rows // 16, act)
        store(2, t).start()

    def tables():
        for k in range(1, ways):
            labels(k).wait_recv()
        keeps[0].wait()
        lse[...] = jnp.zeros_like(lse)
        for o in range(ways):
            at = slice(o * rows, (o + 1) * rows)
            rows_here = ido[o].astype(F32)
            labr[:, at] = rows_here
            columns = jnp.transpose(rows_here)
            labc[at, :] = columns
            angles = columns[:, 0:1] * freq[...]
            cosb[at, :] = jnp.cos(angles)
            sinb[at, :] = jnp.sin(angles)
        for copy in table_stores:
            copy.start()

    def project(t):
        o = blocks[t]
        at = pl.ds(pl.multiple_of(o * rows, 16), rows)
        cos, sin = cosb[at, :], sinb[at, :]
        for which, ref in enumerate((qb, kb, vb)):
            heads = pl.ds(which * head_cols, head_cols)
            v = dot_nn(norm[o], wqv[:, heads]) + qkv_shift[:, heads]
            for pair in range(head_cols // 128):
                part_of = v[:, pair * 128 : (pair + 1) * 128]
                if which < 2:
                    part_of = turn(part_of, cos, sin)
                part_of = part_of.astype(BF16)
                if which == 0:
                    part_of = part_of * BF16(1.0 / math.sqrt(HD))
                ref[at, pl.ds(pair * 128, 128)] = part_of

    def attend(pair, i):
        lanes = pl.ds(pair * 128, 128)
        here, seen = pl.ds(i * QUERIES, QUERIES), pl.ds(0, (i + 1) * QUERIES)
        allowed = allowed_keys(labr, labc, i)
        first = lax.broadcasted_iota(jnp.int32, (QUERIES, 128), 1) < HD
        lane = lax.broadcasted_iota(jnp.int32, (QUERIES, 128), 1)
        keys, values = kb[seen, lanes], vb[seen, lanes]
        outs_of, logs = [], lse[here, :]
        for sub in range(2):
            mine = first if sub == 0 else ~first
            scores = dot_nt(jnp.where(mine, qb[here, lanes], 0), keys)
            scores = jnp.where(allowed, scores, -1e30)
            top = jnp.max(scores, 1, keepdims=True)
            expo = jnp.exp(scores - top)
            total = jnp.sum(expo, 1, keepdims=True)
            outs_of.append(dot_nn((expo * (1.0 / total)).astype(BF16), values))
            logs = jnp.where(lane == pair * 2 + sub, top + jnp.log(total), logs)
        lse[here, :] = logs
        mixb[here, lanes] = jnp.where(first, outs_of[0], outs_of[1]).astype(BF16)

    def down(t):
        if t >= 2:
            store(3, t - 2).wait()
        o = blocks[t]
        at = pl.ds(pl.multiple_of(o * rows, 16), rows)

        def mul(i):
            total = dot_nn(hid[o], w2v[:, span(i)])
            total = total + dot_nn(mixb[at, :], wdv[:, span(i)])
            ob[t % 2, :, span(i)] = total.astype(BF16)

        loop(width // wide, mul)
        store(3, t).start()

    def back(t):
        if t >= 2:
            store(5, t - 2).wait()
        load_g(t).wait()
        if t == 0:
            own_g.start()
            small[...] = jnp.zeros_like(small)
            small[2:3, :] = jnp.sum(gb[0].astype(F32), 0, keepdims=True)
        o = blocks[t]

        def mul(i):
            act = dot_nt(gb[t % 2], w2v[span(i), :])
            grad = (act * slope[o, :, span(i)]).astype(BF16)
            hgb[t % 2, :, span(i)] = grad
            total = jnp.sum(grad.astype(F32), 0, keepdims=True)
            small[3:4, span(i)] += total

        loop(cols // wide, mul)
        store(5, t).start()

    def back_on(t):
        if t >= 2:
            store(4, t - 2).wait()

        def mul_back(i):
            nb[t % 2, :, span(i)] = dot_nt(hgb[t % 2], w1v[span(i), :]).astype(BF16)

        loop(width // wide, mul_back)
        store(4, t).start()
        mb[t] = dot_nt(gb[t % 2], wdv[...]).astype(BF16)
        store(6, t).start()

    greet(ways)
    for k in range(1, ways):
        labels(k).start()
    keeps = [
        pltpu.make_async_copy(ids, ido.at[me], own.at[1]),
    ]
    for copy in keeps:
        copy.start()
    wa_out = pltpu.make_async_copy(wqv, wao, own.at[2])
    stores = [
        pltpu.make_async_copy(src, dst, keep_out.at[i])
        for i, (src, dst) in enumerate(
            ((cosb, coso), (sinb, sino), (qb, qo), (kb, ko), (vb, vo), (mixb, mixo), (lse, lseo))
        )
    ]
    table_stores, state_stores = stores[:2], stores[2:]
    steps = dict(
        X=lambda s: send_own(0, s),
        G=lambda s: send_own(1, s),
        S=send_share,
        W=wa_out.start,
        Z=lambda: [copy.start() for copy in state_stores],
        x=lambda k, s: pass_on(0, k, s),
        g=lambda k, s: pass_on(1, k, s),
        s=spread_on,
        c=corner_on,
        e=settle,
        l=tables,
        i=fetch_x,
        j=fetch_g,
        n=normalise,
        u=up,
        p=project,
        a=attend,
        d=down,
        b=back,
        r=back_on,
    )
    plan = (
        "S22", "S21", "X0", "S10", "S20", "S23", "X1", "S01", "c10", "s22", "l", "S00", "c20",
        "x10", "s23", "i0", "S03", "s21", "c22", "S02", "x11", "S11", "c23", "c21", "s01", "c01",
        "i1", "S13", "s03", "e2", "j0", "n0", "c00", "x20", "s02", "W", "x21", "i2", "p0", "n1",
        "x30", "c02", "c03", "p1", "S12", "n2", "p2", "s13", "e0", "G0", "u0", "s11", "x31", "i3",
        "u1", "G1", "u2", "n3", "c13", "p3", "a12", "a05", "s12", "a14", "a00", "g10", "a04",
        "a11", "a03", "a10", "a01", "c11", "a02", "c12", "a15", "g11", "a13", "u3", "j1", "e1",
        "b0", "Z", "g20", "d0", "d1", "b1", "g21", "r1", "r0", "j2", "g30", "d2", "g31", "d3",
        "j3", "b2", "r2", "b3", "r3",
    )
    for word in plan:
        steps[word[0]](*(int(digit) for digit in word[1:]))
    for k in range(1, ways):
        labels(k).wait_send()
    for copy in table_stores + state_stores:
        copy.wait()
    wa_out.wait()
    for t in range(4):
        for which in (1, 2, 6):
            store(which, t).wait()
        if t >= 2:
            for which in (0, 3, 4, 5):
                store(which, t).wait()
    for a in range(2):
        for owner in range(ways):
            for s in range(PIECES):

                @pl.when(owner != me)
                def _():
                    across(a, owner, s, core).wait_send()

                @pl.when((me > 0) & (owner >= me))
                def _():
                    along(a, owner, s, 0).wait_send()

                @pl.when((me < ways - 1) & (owner <= me))
                def _():
                    along(a, owner, s, 1).wait_send()

    for grp in range(groups):
        for k in range(ways):
            if k:
                wait_send(share(grp, k))
            for axis in range(2):
                wait_send(spread(grp, k, axis))
            wait_send(corner(grp, k))


def forward(x, g, w1, w2, wq, wd, ids, lines):
    ways = lax.axis_size("ctx")
    rows, width = x.shape
    groups, cols, head_cols = 3, w1.shape[1] // ways, wd.shape[0] // ways
    dma = pltpu.SemaphoreType.DMA
    vmem = pltpu.VMEM
    anywhere = pl.BlockSpec(memory_space=pl.ANY)
    inside = pl.BlockSpec(memory_space=pltpu.VMEM)
    seq = lambda n, dtype=BF16: jax.ShapeDtypeStruct((ways, rows, n), dtype)
    tokens = ways * rows
    line = lambda n, dtype: jax.ShapeDtypeStruct((tokens, n), dtype)
    outs = pl.pallas_call(
        functools.partial(forward_body, ways),
        in_specs=[anywhere] * 7 + [inside] * 2,
        out_specs=[anywhere] * 16 + [inside] * 2 + [anywhere],
        out_shape=[
            seq(width),
            seq(width),
            seq(width),
            seq(cols),
            seq(cols),
            seq(width),
            seq(width),
            seq(head_cols),
            jax.ShapeDtypeStruct((width, 3 * head_cols), BF16),
            line(head_cols, BF16),
            line(head_cols, BF16),
            line(head_cols, BF16),
            line(head_cols, BF16),
            line(128, F32),
            line(128, F32),
            line(128, F32),
            jax.ShapeDtypeStruct((ways, 8, rows), jnp.int32),
            jax.ShapeDtypeStruct((8, width), F32),
            seq(width),
        ],
        scratch_shapes=[
            vmem((width, cols), BF16),
            vmem((cols, width), BF16),
            vmem((width, 3 * head_cols), BF16),
            vmem((head_cols, width), BF16),
            vmem((ways, rows, width), BF16),
            vmem((2, rows, width), BF16),
            vmem((2, rows, width), BF16),
            vmem((rows, cols), F32),
            vmem((ways, rows, cols), BF16),
            vmem((ways, rows, cols), F32),
            vmem((2, rows, cols), BF16),
            vmem((2, rows, width), BF16),
            vmem((2, rows, width), BF16),
            vmem((ways, rows, head_cols), BF16),
            vmem((tokens, head_cols), BF16),
            vmem((tokens, head_cols), BF16),
            vmem((tokens, head_cols), BF16),
            vmem((tokens, head_cols), BF16),
            vmem((tokens, 128), F32),
            vmem((tokens, 128), F32),
            vmem((tokens, 128), F32),
            vmem((8, tokens), F32),
            vmem((tokens, 8), F32),
            dma((2, 2, ways, PIECES)),
            dma((2, ways, PIECES)),
            dma((2, ways, PIECES)),
            dma((2, ways, PIECES)),
            dma((groups, ways, 4)),
            dma((groups, ways, 4)),
            dma((2, groups, ways, 2)),
            dma((2, groups, ways, 2)),
            dma((groups, ways, 2)),
            dma((groups, ways, 2)),
            dma((ways,)),
            dma((ways,)),
            dma((3,)),
            dma((2, ways)),
            dma((7, ways)),
            dma((7,)),
        ],
        compiler_params=pltpu.CompilerParams(
            collective_id=0, has_side_effects=True, vmem_limit_bytes=62 * MIB
        ),
    )(
        x, g, w1, w2, wq, wd, ids, lines, frequencies(),
    )
    return outs


def backward_body(
    ways,
    p0, ngm, normed, xh, g_flat, hg, hidden, q, k, v, mg, mix, lse, cos, sin, wa, labels, small,
    x, g, lines, out, gin, g1, g2, gq, gd, tin, smallo,
    lt, ra, rb, wp, qv, kv, vv, mgv, lsev, cosv, sinv, dkv, dvv, labr, labc,
    acc, zin, tst, ngi, xhi, ngs, gown, gsend, first_in, second_in, sums, sum_in, sum_out,
    tps, tpr, zs, zr, fs, fr, ss, sr, ws, wr, os, orr, loc, tloc, sms, smr, ins, lts, ngl,
):
    dp, me, core, dpx, dpy = place_of()
    rows, width = out.shape
    half = rows // 2
    piece = half // PIECES
    groups = first_in.shape[0]
    span_rows = gown.shape[3]
    lanes = gown.shape[4]
    depth = span_rows // ways
    cols, head_cols = hg.shape[1], q.shape[1]
    nxt = (dpx, dpy)
    far = dpx + dpy - dp
    scale = 1.0 / math.sqrt(HD)

    order = (0, 3, 1, 2)

    def part(which, s):
        return pl.ds(pl.multiple_of(which * half + s * piece, 16), piece)

    def loop(count, body):
        lax.fori_loop(0, count, lambda i, c: (body(i), c)[1], 0)

    def add(dst, src, height):
        step = 32

        def body(i):
            at = pl.ds(pl.multiple_of(i * step, step), step)
            dst[at, :] = dst[at, :] + src[at, :]

        loop(height // step, body)

    def swap(a, d, s):
        at = pl.ds(s * piece, piece)
        src = p0.at[d, part(1 - core, s), :] if a == 0 else ngs.at[order.index(d) % 2, at, :]
        return remote(
            src, tin.at[a, d, s], tps.at[a, d, s], tpr.at[a, d, s], (dp, me, 1 - core)
        )

    def load(d, s):
        return pltpu.make_async_copy(p0.at[d, part(core, s), :], acc.at[0, d, s], loc.at[d, s])

    def load_swapped(a, d, s):
        return pltpu.make_async_copy(tin.at[a, d, s], tst.at[s], tloc.at[a, d, s])

    def slot(d, side):
        if side:
            return d
        here = 1 - jnp.minimum(jnp.abs(me - 1 - d), 1)
        return d + here * (ways - d)

    def came(d, side):
        if side:
            return d
        here = 1 - jnp.minimum(jnp.abs(me - d), 1)
        return d + here * (ways - d)

    def stream(a, d, s, side):
        return remote(
            acc.at[a, d, s],
            zin.at[a, slot(d, side), s],
            zs.at[a, d, s],
            zr.at[a, slot(d, side), s],
            (dp, me - 1 + 2 * side, core),
        )

    def arrived(a, d, s, side):
        ref = zin.at[a, came(d, side), s]
        return remote(
            ref, ref, zs.at[a, d, s], zr.at[a, came(d, side), s], (dp, me - 1 + 2 * side, core)
        )

    results = (out, gin)

    def finish(a, s, which):
        ref = results[a].at[part(which, s), :]
        return remote(acc.at[a, me, s], ref, os.at[0, a, s], orr.at[a, s], (dp, me, 1 - core))

    def finish_here(a, s):
        return pltpu.make_async_copy(
            acc.at[a, me, s], results[a].at[part(core, s), :], os.at[1, a, s]
        )

    def load_own(i):
        at = pl.ds(pl.multiple_of(core * half, 16), half)
        src, dst = ((x.at[at, :], ngi.at[0]), (g.at[at, :], ngi.at[1]))[i]
        return pltpu.make_async_copy(src, dst, ins.at[11 + i])

    def merge(a, d):
        for s in range(PIECES):
            swap(a, d, s).wait_recv()
            load_swapped(a, d, s).start()
        for s in range(PIECES):
            load_swapped(a, d, s).wait()
            if a == 0:
                load(d, s).wait()
            add(acc.at[a, d, s], tst.at[s], piece)
            pl.when((me == 0) & (d > 0))(lambda: stream(a, d, s, 1).start())
            pl.when((me == ways - 1) & (d < ways - 1))(lambda: stream(a, d, s, 0).start())

    def hop(a, far_by, j, s):
        d = ways - 1 - j

        @pl.when(me == far_by)
        def _():
            arrived(a, d, s, 1).wait_recv()
            add(acc.at[a, d, s], zin.at[a, came(d, 1), s], piece)
            if d > far_by:
                stream(a, d, s, 1).start()

        @pl.when(me == ways - 1 - far_by)
        def _():
            arrived(a, j, s, 0).wait_recv()
            add(acc.at[a, j, s], zin.at[a, came(j, 0), s], piece)
            if j < ways - 1 - far_by:
                stream(a, j, s, 0).start()

    def last(a):
        if a == 0:
            for i in range(2):
                load_own(i).start()
            for i in range(2):
                load_own(i).wait()
        for s in range(PIECES):
            at = pl.ds(s * piece, piece)
            xf = ngi[0, at, :].astype(F32)
            total = acc[a, me, s].astype(F32)
            if a == 0:
                acc[a, me, s] = (xf + total + lines[4:5, :]).astype(BF16)
            else:
                centred = xf - jnp.mean(xf, -1, keepdims=True)
                inv_std = lax.rsqrt(jnp.mean(centred * centred, -1, keepdims=True) + EPS)
                x_hat = centred * inv_std
                scaled = total * lines[0:1, :]
                change = (
                    scaled
                    - jnp.mean(scaled, -1, keepdims=True)
                    - x_hat * jnp.mean(scaled * x_hat, -1, keepdims=True)
                )
                acc[a, me, s] = (ngi[1, at, :].astype(F32) + inv_std * change).astype(BF16)
            finish(a, s, core).start()
            finish_here(a, s).start()

    def lanes_of(path):
        return pl.ds(path * lanes, lanes)

    def first(grp, path, i):
        return remote(
            gsend.at[2 * i + path],
            first_in.at[grp, path, i],
            fs.at[grp, path, i],
            fr.at[grp, path, i],
            (nxt[path], me, core),
        )

    def second(grp, path):
        return remote(
            gown.at[grp % 2, path, 0],
            second_in.at[grp, path],
            ss.at[grp, path],
            sr.at[grp, path],
            (nxt[1 - path], me, core),
        )

    def pieces(grp, path, d):
        ref = gown.at[grp % 2, path, 1]
        across = pl.ds(pl.multiple_of(me * cols + path * lanes, 128), lanes)
        heads = pl.ds(pl.multiple_of(me * head_cols, 128), head_cols)
        rows_of_d = pl.ds(pl.multiple_of(d * depth, 128), depth)
        if grp == 0:
            return [(ref.at[rows_of_d, :], g1.at[:, across])]
        if grp == 1:
            return [(ref.at[:, rows_of_d], g2.at[across, :])]
        if path == 0:
            return [
                (ref.at[rows_of_d, pl.ds(c * head_cols, head_cols)], gq.at[c, :, heads])
                for c in range(2)
            ]
        per = head_cols // depth
        dense_rows = pl.ds(pl.multiple_of(d // per * head_cols, 128), head_cols)
        dense_lanes = pl.ds(pl.multiple_of(head_cols + d % per * depth, 128), depth)
        return [
            (ref.at[rows_of_d, pl.ds(0, head_cols)], gq.at[2, :, heads]),
            (ref.at[dense_rows, dense_lanes], gd.at[heads, :]),
        ]

    def share(grp, path, i):
        d = (me + i) % ways
        return [
            remote(src, dst, ws.at[grp, path, i, n], wr.at[grp, path, i, n], (dp, d, core))
            for n, (src, dst) in enumerate(pieces(grp, path, d))
        ]

    def keep(grp, path):
        return [
            pltpu.make_async_copy(src, dst, ws.at[grp, path, 0, n])
            for n, (src, dst) in enumerate(pieces(grp, path, me))
        ]

    def start(copies):
        for copy in copies:
            copy.start()

    def wait(copies):
        for copy in copies:
            copy.wait()

    def wait_recv(copies):
        for copy in copies:
            copy.wait_recv()

    def wait_send(copies):
        for copy in copies:
            copy.wait_send()

    quarters = (far, dpx, dpy, dp)

    def load_left(grp, r, which=0):
        at = pl.ds(pl.multiple_of(quarters[r] * span_rows, 128), span_rows)
        src = (normed, g_flat, normed)[grp] if which == 0 else g_flat
        into = (4 * grp + r) % 2 if grp < 2 else which
        return pltpu.make_async_copy(src.at[:, at], lt.at[into], lts.at[grp, r, which])

    def products(grp, r):
        load_left(grp, r).wait()
        if 4 * grp + r < 7:
            after = 4 * grp + r + 1
            load_left(after // 4, after % 4).start()
        left = (4 * grp + r) % 2 if grp < 2 else 0
        for path in range(2):
            if r == 0:
                dst = gsend.at[path]
                i = 0
            elif r == 1 + path:
                dst = gsend.at[2 + path]
                i = 1
            else:
                dst = gown.at[grp % 2, path, 1 if r == 3 else 0]
                i = None
            if i is not None and grp:
                first(grp - 1, path, i).wait_send()
            if i is None and grp == 2:
                if r == 3:
                    wait(keep(0, path))
                    for n in range(1, ways):
                        wait_send(share(0, path, n))
                else:
                    second(0, path).wait_send()
            right = (ra, rb, ra)[grp]
            if grp == 1:
                dst[...] = dot_tn(right[:, lanes_of(path)], lt[left]).astype(BF16)
            elif grp == 2 and path == 1:
                dst[:, :head_cols] = dot_tn(lt[0], right[:, 2 * head_cols : 3 * head_cols]).astype(BF16)
                if r < 3:
                    load_left(grp, r + 1).start()
                load_left(grp, r, 1).wait()
                dense = dot_tn(right[:, 3 * head_cols :], lt[1]).astype(BF16)
                dst[:head_cols, head_cols:] = dense[:, :head_cols]
                dst[head_cols:, head_cols:] = dense[:, head_cols:]
            else:
                dst[...] = dot_tn(lt[left], right[:, lanes_of(path)]).astype(BF16)
            if i is not None:
                first(grp, path, i).start()
        if grp == 2 and r < 3:
            load_left(grp, r + 1, 1).start()

    def pass_sum(grp, path):
        first(grp, path, 0).wait_recv()
        add(gown.at[grp % 2, path, 0], first_in.at[grp, path, 0], span_rows)
        second(grp, path).start()

    def first_sum(grp, path):
        first(grp, path, 1).wait_recv()
        add(gown.at[grp % 2, path, 1], first_in.at[grp, path, 1], span_rows)

    def second_sum(grp, path):
        second(grp, path).wait_recv()
        add(gown.at[grp % 2, path, 1], second_in.at[grp, path], span_rows)
        for i in range(1, ways):
            start(share(grp, path, i))
        start(keep(grp, path))

    pairs = (
        (hg, ra), (hidden, rb), (wa, wp),
        (q, qv), (k, kv), (v, vv), (mg, mgv), (lse, lsev), (cos, cosv), (sin, sinv),
    )

    def copy_in(i):
        return pltpu.make_async_copy(*pairs[i], ins.at[i])

    mix_in = pltpu.make_async_copy(mix, ra.at[:, pl.ds(3 * head_cols, head_cols)], ins.at[10])

    def begin():
        for i in range(3, 10):
            copy_in(i).wait()
        mix_in.start()
        for o in range(ways):
            at = slice(o * rows, (o + 1) * rows)
            rows_here = labels[o].astype(F32)
            labr[:, at] = rows_here
            labc[at, :] = jnp.transpose(rows_here)

    def turned_back(value, at):
        return turn(value, cosv[at, :], -sinv[at, :]).astype(BF16)

    def attend_back(pair, i):
        at = pl.ds(pair * 128, 128)
        here, seen = pl.ds(i * QUERIES, QUERIES), pl.ds(0, (i + 1) * QUERIES)
        allowed = allowed_keys(labr, labc, i)
        head = lax.broadcasted_iota(jnp.int32, (QUERIES, 128), 1) < HD
        if i == 0:
            dkv[...] = jnp.zeros_like(dkv)
            dvv[...] = jnp.zeros_like(dvv)
        keys, values = kv[seen, at], vv[seen, at]
        parts = []
        for sub in range(2):
            mine = head if sub == 0 else ~head
            qi = jnp.where(mine, qv[here, at], 0)
            mi = jnp.where(mine, mgv[here, at], 0)
            log = lsev[here, pair * 2 + sub : pair * 2 + sub + 1]
            probs = jnp.where(allowed, jnp.exp(dot_nt(qi, keys) - log), 0.0)
            prob_grad = dot_nt(mi, values)
            delta = jnp.sum(probs * prob_grad, 1, keepdims=True)
            score_grad = (probs * (prob_grad - delta)).astype(BF16)
            parts.append(dot_nn(score_grad, keys))
            dkv[seen, :] += dot_tn(score_grad, qi)
            dvv[seen, :] += dot_tn(probs.astype(BF16), mi)
        ra[here, at] = turned_back(jnp.where(head, parts[0], parts[1]) * scale, here)
        if i == rows * ways // QUERIES - 1:
            ra[:, pl.ds(head_cols + pair * 128, 128)] = turned_back(dkv[...], slice(None))
            ra[:, pl.ds(2 * head_cols + pair * 128, 128)] = dvv[...].astype(BF16)

    def load_back(d, own):
        at = pl.ds(pl.multiple_of((core if own else 1 - core) * half, 16), half)
        return [
            pltpu.make_async_copy(ngm.at[d, at, :], ngi.at[own], ngl.at[0, d, own]),
            pltpu.make_async_copy(xh.at[d, at, :], xhi.at[own], ngl.at[1, d, own]),
        ]

    def normed_back(n):
        d = order[n]
        if n == 0:
            copy_in(2).wait()
            sums[...] = small[...]
        if n >= 2:
            for s in range(PIECES):
                swap(1, order[n - 2], s).wait_send()
        wide = 512
        for own in range(2):
            for copy in load_back(d, own):
                copy.wait()
            at = pl.ds(pl.multiple_of(d * rows + (core if own else 1 - core) * half, 16), half)

            def mul(i):
                cols = pl.ds(pl.multiple_of(i * wide, wide), wide)
                tile = dot_nt(ra[at, : 3 * head_cols], wp[cols, :]) + ngi[own, :, cols].astype(F32)
                sums[0:1, cols] += jnp.sum(tile * xhi[own, :, cols].astype(F32), 0, keepdims=True)
                sums[1:2, cols] += jnp.sum(tile, 0, keepdims=True)
                tile = tile.astype(BF16)
                for s in range(PIECES):
                    if own:
                        acc[1, d, s, :, cols] = tile[s * piece : (s + 1) * piece]
                    else:
                        ngs[n % 2, s * piece : (s + 1) * piece, cols] = tile[s * piece : (s + 1) * piece]

            loop(width // wide, mul)
            if not own:
                for s in range(PIECES):
                    swap(1, d, s).start()
            if n < ways - 1:
                for copy in load_back(order[n + 1], own):
                    copy.start()

    def small_send(i):
        src = sums if i == 0 else sum_out.at[i - 1]
        device = ((dp, me, 1 - core), (dpx, me, core), (dpy, me, core))[i]
        return remote(src, sum_in.at[i], sms.at[i], smr.at[i], device)

    def small_all(i):
        device = (dp, (me + i) % ways, core)
        return remote(sum_out.at[2], smallo.at[me], sms.at[2 + i], smr.at[2 + i], device)

    def small_begin():
        sums[4:5, : 3 * head_cols] = jnp.sum(ra[:, : 3 * head_cols].astype(F32), 0, keepdims=True)
        small_send(0).start()

    def small_step(i):
        small_send(i).wait_recv()
        before = sums[...] if i == 0 else sum_out[i - 1]
        after = before + sum_in[i]
        if i == 0:
            row = lax.broadcasted_iota(jnp.int32, after.shape, 0)
            after = jnp.where(row < 2, after, before)
        sum_out[i] = after
        if i < 2:
            small_send(i + 1).start()
        else:
            for n in range(1, ways):
                small_all(n).start()
            smallo[me] = after

    greet(ways)
    for d in order:
        for s in range(PIECES):
            swap(0, d, s).start()
            load(d, s).start()
    load_left(0, 0).start()
    for i in range(len(pairs)):
        copy_in(i).start()
    for own in range(2):
        for copy in load_back(order[0], own):
            copy.start()
    copy_in(0).wait()
    copy_in(1).wait()

    def last_left():
        mix_in.wait()
        load_left(2, 0).start()
        load_left(2, 0, 1).start()

    steps = dict(
        t=products,
        f=pass_sum,
        F=first_sum,
        h=second_sum,
        m=merge,
        z=hop,
        o=last,
        B=begin,
        a=attend_back,
        L=last_left,
        n=normed_back,
        Y=small_begin,
        y=small_step,
    )
    plan = (
        "t00", "m00", "m03", "t01", "t02", "t03", "B", "m01", "z0100", "a00", "f00", "a01", "a02",
        "a03", "a04", "f01", "z0101", "F00", "a05", "m02", "z0200", "t10", "a10", "h00", "F01",
        "t11", "a11", "h01", "a12", "a13", "a14", "t12", "t13", "a15", "z0120", "n0", "z0300",
        "n1", "m10", "z0110", "F11", "n2", "z0111", "m13", "f11", "n3", "F10", "L", "Y", "t20",
        "m12", "z1100", "z0201", "t21", "y0", "m11", "f10", "z1101", "h11", "h10", "z1110",
        "z1200", "t22", "t23", "z0121", "z0210", "f20", "y1", "f21", "z1111", "z1120", "z1201",
        "z0211", "z1121", "z1210", "F20", "F21", "h20", "z1300", "y2", "z1211", "h21", "z0301",
        "z1301", "o0", "o1",
    )
    for word in plan:
        steps[word[0]](*(int(digit) for digit in word[1:]))

    for i in range(3):
        small_send(i).wait_send()
    for i in range(1, ways):
        small_all(i).wait()
    for a in range(2):
        for s in range(PIECES):
            finish(a, s, core).wait_send()
            finish_here(a, s).wait()
            finish(a, s, 1 - core).wait_recv()
            for n, d in enumerate(order):
                if a == 0 or n >= 2:
                    swap(a, d, s).wait_send()
                pl.when(d > me)(lambda: stream(a, d, s, 1).wait_send())
                pl.when(d < me)(lambda: stream(a, d, s, 0).wait_send())
    for grp in range(groups):
        for path in range(2):
            if grp == 2:
                for i in range(2):
                    first(grp, path, i).wait_send()
            if grp:
                second(grp, path).wait_send()
                wait(keep(grp, path))
            for i in range(1, ways):
                wait_recv(share(grp, path, i))
                if grp:
                    wait_send(share(grp, path, i))


def backward(
    p0, ngm, normed, xh, g_all, hg, hidden, q, k, v, mg, mix, lse, cos, sin, wa, labels, small,
    x, g, lines,
):
    ways, rows, width = p0.shape
    chips = lax.axis_size("dp")
    tokens = ways * rows
    groups, cols, head_cols = 3, hg.shape[-1], q.shape[-1]
    span = width // chips
    lanes = cols // 2
    piece = rows // 2 // PIECES
    half = rows // 2
    dma = pltpu.SemaphoreType.DMA
    vmem = pltpu.VMEM
    anywhere = pl.BlockSpec(memory_space=pl.ANY)
    inside = pl.BlockSpec(memory_space=pltpu.VMEM)
    flat = lambda t: t.reshape(tokens, t.shape[-1])
    depth = span // ways
    out, gin, g1, g2, gq, gd, unused, smallo = pl.pallas_call(
        functools.partial(backward_body, ways),
        in_specs=[anywhere] * 16 + [inside] * 2 + [anywhere] * 2 + [inside],
        out_specs=[anywhere] * 7 + [inside],
        out_shape=[
            jax.ShapeDtypeStruct((rows, width), BF16),
            jax.ShapeDtypeStruct((rows, width), BF16),
            jax.ShapeDtypeStruct((depth, ways * cols), BF16),
            jax.ShapeDtypeStruct((ways * cols, depth), BF16),
            jax.ShapeDtypeStruct((3, depth, ways * head_cols), BF16),
            jax.ShapeDtypeStruct((ways * head_cols, depth), BF16),
            jax.ShapeDtypeStruct((2, ways, PIECES, piece, width), BF16),
            jax.ShapeDtypeStruct((ways,) + small.shape, F32),
        ],
        scratch_shapes=[
            vmem((2, tokens, span), BF16),
            vmem((tokens, cols), BF16),
            vmem((tokens, cols), BF16),
            vmem((width, 3 * head_cols), BF16),
            vmem((tokens, head_cols), BF16),
            vmem((tokens, head_cols), BF16),
            vmem((tokens, head_cols), BF16),
            vmem((tokens, head_cols), BF16),
            vmem((tokens, 128), F32),
            vmem((tokens, 128), F32),
            vmem((tokens, 128), F32),
            vmem((tokens, 128), F32),
            vmem((tokens, 128), F32),
            vmem((8, tokens), F32),
            vmem((tokens, 8), F32),
            vmem((2, ways, PIECES, piece, width), BF16),
            vmem((2, ways + 1, PIECES, piece, width), BF16),
            vmem((PIECES, piece, width), BF16),
            vmem((2, half, width), BF16),
            vmem((2, half, width), BF16),
            vmem((2, half, width), BF16),
            vmem((2, 2, 2, span, lanes), BF16),
            vmem((4, span, lanes), BF16),
            vmem((groups, 2, 2, span, lanes), BF16),
            vmem((groups, 2, span, lanes), BF16),
            vmem(small.shape, F32),
            vmem((3,) + small.shape, F32),
            vmem((3,) + small.shape, F32),
            dma((2, ways, PIECES)),
            dma((2, ways, PIECES)),
            dma((2, ways, PIECES)),
            dma((2, ways + 1, PIECES)),
            dma((groups, 2, 2)),
            dma((groups, 2, 2)),
            dma((groups, 2)),
            dma((groups, 2)),
            dma((groups, 2, ways, 2)),
            dma((groups, 2, ways, 2)),
            dma((2, 2, PIECES)),
            dma((2, PIECES)),
            dma((ways, PIECES)),
            dma((2, ways, PIECES)),
            dma((2 + ways,)),
            dma((2 + ways,)),
            dma((13,)),
            dma((groups, 4, 2)),
            dma((2, ways, 2)),
        ],
        compiler_params=pltpu.CompilerParams(
            collective_id=1, has_side_effects=True, vmem_limit_bytes=63 * MIB
        ),
    )(
        p0, ngm, flat(normed), xh, flat(g_all), flat(hg), flat(hidden), q, k, v, flat(mg), mix,
        lse, cos, sin, wa, labels, small, x, g, lines,
    )
    grads = tuple(t.astype(F32) for t in (gq, gd, g1, g2))
    return out, gin, grads, smallo


def layer_norm(x):
    xf = x.astype(F32)
    mean = jnp.mean(xf, -1, keepdims=True)
    centred = xf - mean
    inv_std = lax.rsqrt(jnp.mean(centred * centred, -1, keepdims=True) + EPS)
    return centred * inv_std, inv_std


def plain_work(
    x, g, w_qkv, w_dense, w_fc1, w_fc2, places, segments, gain, shift, fc1_shift, qkv_shift, out_bias
):
    me, ways = lax.axis_index("ctx"), lax.axis_size("ctx")
    width = x.shape[1]
    depth = w_fc1.shape[0]
    cols, head_cols = w_fc1.shape[1] // ways, w_dense.shape[0] // ways
    fc1 = w_fc1.reshape(depth, ways, cols).transpose(1, 0, 2)
    fc2 = w_fc2.reshape(ways, cols, depth).transpose(0, 2, 1)
    qkv = w_qkv.reshape(3, depth, ways, head_cols).transpose(2, 1, 0, 3)
    dense = w_dense.reshape(ways, head_cols, depth).transpose(0, 2, 1)
    att = jnp.concatenate([qkv.reshape(ways, depth, 3 * head_cols), dense], -1)
    wsrc = jnp.stack([fc1, fc2, att])
    x_all, g_all, weights, places, segments = gather_plain(x, g, wsrc, places, segments)
    weights = weights.reshape(3, width, cols)
    w1, w2, wa = weights[0], weights[1], weights[2]
    wp, wd = wa[:, : 3 * head_cols], wa[:, 3 * head_cols :]
    x_hat, unused = layer_norm(x_all)
    normed = (x_hat * gain + shift).astype(BF16)
    projected = dot_nn(normed, wp) + qkv_shift.reshape(1, 3 * head_cols)
    mix_grad = dot_nn(g_all, wd).astype(BF16)
    mixture, gq, gk, gv = attention_plain(
        projected[:, :head_cols],
        projected[:, head_cols : 2 * head_cols],
        projected[:, 2 * head_cols :],
        mix_grad,
        places,
        segments,
    )
    proj_grad = jnp.concatenate([gq, gk, gv], 1)

    hidden_pre = dot_nn(normed, w1) + fc1_shift
    hidden, slope = gelu_and_slope(hidden_pre)
    hidden = hidden.astype(BF16)
    hidden_grad = (dot_nn(g_all, w2) * slope).astype(BF16)

    out_part = (dot_nt(mixture, wd) + dot_nt(hidden, w2)).astype(BF16)
    normed_part = dot_nt(proj_grad, wp) + dot_nt(hidden_grad, w1)
    weight_part = jnp.stack(
        [
            dot_tn(normed, hidden_grad).astype(BF16),
            dot_tn(g_all, hidden).astype(BF16),
            jnp.concatenate([dot_tn(normed, proj_grad), dot_tn(g_all, mixture)], 1).astype(BF16),
        ]
    )
    qkv_bias_part = jnp.sum(proj_grad.astype(F32), 0).reshape(3, head_cols)
    fc1_bias_part = jnp.sum(hidden_grad.astype(F32), 0)
    branches, normed_grad, weight_grads = scatter_plain(
        out_part, normed_part.astype(BF16), weight_part.reshape(3, -1, depth, cols)
    )
    place = lambda t, whole, axis: lax.dynamic_update_slice_in_dim(
        jnp.zeros(whole, F32), t, me * t.shape[axis], axis
    )
    small = lax.psum(
        (
            place(qkv_bias_part, (3, head_cols * ways), 1),
            place(fc1_bias_part, (cols * ways,), 0),
            jnp.sum(g.astype(F32), 0),
        ),
        ("dp", "ctx"),
    )
    norms = lax.psum(
        (jnp.sum(normed_part * x_hat, 0), jnp.sum(normed_part, 0)), ("dp", "ctx", "tp")
    )
    grad_fc1 = weight_grads[0].transpose(1, 0, 2).reshape(depth, ways * cols)
    grad_fc2 = weight_grads[1].transpose(0, 2, 1).reshape(ways * cols, depth)
    grad_att = weight_grads[2].reshape(ways, depth, 4, head_cols)
    grad_qkv = grad_att[:, :, :3].transpose(2, 1, 0, 3).reshape(3, depth, ways * head_cols)
    grad_dense = grad_att[:, :, 3].transpose(0, 2, 1).reshape(ways * head_cols, depth)
    weight_grads = (grad_qkv, grad_dense, grad_fc1, grad_fc2)
    gf = g.astype(F32)
    output = (x.astype(F32) + branches + out_bias).astype(BF16)
    own_hat, inv_std = layer_norm(x)
    scaled = normed_grad * gain
    grad_input = gf + inv_std * (
        scaled
        - jnp.mean(scaled, -1, keepdims=True)
        - own_hat * jnp.mean(scaled * own_hat, -1, keepdims=True)
    )
    return output, grad_input.astype(BF16), weight_grads, norms + small


def fast_work(
    x, g, w_qkv, w_dense, w_fc1, w_fc2, places, segments, gain, shift, fc1_shift, qkv_shift, out_bias
):
    ways = lax.axis_size("ctx")
    rows, width = x.shape
    cols, head_cols = w_fc1.shape[1] // ways, w_dense.shape[0] // ways
    ids = jnp.concatenate([places[None], segments[None], jnp.zeros((6, rows), jnp.int32)])
    line = lambda t: jnp.pad(t.reshape(1, -1), ((0, 0), (0, width - t.size)))
    lines = jnp.concatenate(
        [line(t) for t in (gain, shift, fc1_shift, qkv_shift, out_bias)]
        + [jnp.zeros((3, width), F32)]
    )
    (
        g_all, normed, x_hat, hidden, hidden_grad, out_part, back_mlp, mix_grad, wa,
        q, k, v, mixture, lse, cos, sin, labels, small, unused,
    ) = forward(x, g, w_fc1, w_fc2, w_qkv, w_dense, ids, lines)
    output, grad_input, weight_grads, sums = backward(
        out_part, back_mlp, normed, x_hat, g_all, hidden_grad, hidden,
        q, k, v, mix_grad, mixture, lse, cos, sin, wa, labels, small, x, g, lines,
    )
    total = jnp.sum(sums[:, :3], 0)
    fc1_bias_sum = sums[:, 3, :cols].reshape(ways * cols)
    qkv_bias_sum = sums[:, 4, : 3 * head_cols].reshape(ways, 3, head_cols).transpose(1, 0, 2)
    sums = (
        total[0], total[1], qkv_bias_sum.reshape(3, ways * head_cols), fc1_bias_sum, total[2]
    )
    return output, grad_input, weight_grads, sums


def per_device(
    block_input,
    cotangent,
    segment_ids,
    positions,
    norm_gain,
    norm_bias,
    w_qkv,
    qkv_bias,
    w_dense,
    w_fc1,
    fc1_bias,
    w_fc2,
    out_bias,
):
    ways = lax.axis_size("ctx")
    me = lax.axis_index("ctx")
    x, g = block_input[0], cotangent[0]
    rows, width = x.shape
    cols, head_cols = w_fc1.shape[1] // ways, w_dense.shape[0] // ways

    gain, shift = norm_gain.astype(F32), norm_bias.astype(F32)
    qkv_shift = lax.dynamic_slice_in_dim(qkv_bias, me * head_cols, head_cols, 1).astype(F32)
    fc1_shift = lax.dynamic_slice_in_dim(fc1_bias, me * cols, cols, 0).astype(F32)
    fast = ways == 4 and lax.axis_size("dp") == 4 and rows % 128 == 0
    fast = fast and head_cols == 256 and width == 8 * head_cols and 4 * cols == width * 2
    work = fast_work if fast else plain_work
    output, grad_input, weight_grads, sums = work(
        x, g, w_qkv, w_dense, w_fc1, w_fc2, positions[0], segment_ids[0],
        gain, shift, fc1_shift, qkv_shift, out_bias.astype(F32),
    )
    grad_qkv, grad_dense, grad_fc1, grad_fc2 = weight_grads
    gain_sum, shift_sum, qkv_bias_sum, fc1_bias_sum, out_bias_sum = sums

    return (
        output[None],
        grad_input[None],
        gain_sum,
        shift_sum,
        grad_qkv,
        qkv_bias_sum,
        grad_dense,
        grad_fc1,
        fc1_bias_sum,
        grad_fc2,
        out_bias_sum,
    )


def solution(mesh):
    placed = (
        P("dp", "ctx", None),
        P("dp", "ctx", None),
        P("dp", "ctx"),
        P("dp", "ctx"),
        P(),
        P(),
        P(None, ("dp", "ctx"), "tp"),
        P(None, "tp"),
        P("tp", ("dp", "ctx")),
        P(("dp", "ctx"), "tp"),
        P("tp"),
        P("tp", ("dp", "ctx")),
        P(),
    )
    return jax.shard_map(
        per_device,
        mesh=mesh,
        in_specs=placed,
        out_specs=(
            P("dp", "ctx", None),
            P("dp", "ctx", None),
            P(),
            P(),
            P(None, ("dp", "ctx"), "tp"),
            P(None, "tp"),
            P("tp", ("dp", "ctx")),
            P(("dp", "ctx"), "tp"),
            P("tp"),
            P("tp", ("dp", "ctx")),
            P(),
        ),
        check_vma=False,
    )
```

```python
import functools
import math

import jax
import jax.numpy as jnp
import numpy as np
from jax import lax
from jax.experimental import pallas as pl
from jax.experimental.pallas import tpu as pltpu
from jax.sharding import PartitionSpec as P

HD = 64
ROT = 32
EPS = 1e-05
MIB = 1 << 20
F32 = jnp.float32
BF16 = jnp.bfloat16
MESH = pl.DeviceIdType.MESH


def dot_nn(a, b):
    return lax.dot_general(a, b, (((1,), (0,)), ((), ())), preferred_element_type=F32)


def dot_nt(a, b):
    return lax.dot_general(a, b, (((1,), (1,)), ((), ())), preferred_element_type=F32)


def dot_tn(a, b):
    return lax.dot_general(a, b, (((0,), (0,)), ((), ())), preferred_element_type=F32)


QUERIES = 256


def frequencies():
    half = ROT // 2
    some = 10000.0 ** (-(np.arange(half, dtype=np.float32) * np.float32(2.0 / ROT)))
    one = np.concatenate([some, some, np.zeros(HD - ROT)]).astype(np.float32)
    return np.concatenate([one, one])[None, :]


def turn(v, cos, sin):
    half = ROT // 2
    lane = lax.broadcasted_iota(jnp.int32, v.shape, 1) % HD
    left, right = pltpu.roll(v, 128 - half, 1), pltpu.roll(v, half, 1)
    return v * cos + jnp.where(lane < half, -left, right) * sin


def allowed_keys(labr, labc, i):
    shape = (QUERIES, (i + 1) * QUERIES)
    row = lax.broadcasted_iota(jnp.int32, shape, 0) + i * QUERIES
    col = lax.broadcasted_iota(jnp.int32, shape, 1)
    here = pl.ds(i * QUERIES, QUERIES)
    return (col <= row) & (labc[here, 1:2] == labr[1:2, 0 : (i + 1) * QUERIES])


def attention_plain(pq, pk, pv, mg, places, segments):
    rows, cols = pq.shape
    heads = cols // HD
    half = ROT // 2
    scale = 1.0 / math.sqrt(HD)
    frequency = 10000.0 ** (-(jnp.arange(half, dtype=F32) * 2.0 / ROT))
    angles = places.astype(F32)[:, None] * frequency[None, :]
    cos, sin = jnp.cos(angles)[:, None, :], jnp.sin(angles)[:, None, :]

    def rotate(t, s):
        t = t.reshape(rows, heads, HD)
        a, b = t[..., :half], t[..., half:ROT]
        return jnp.concatenate([a * cos - b * s, b * cos + a * s, t[..., ROT:]], -1)

    q = rotate(pq, sin).astype(BF16)
    k = rotate(pk, sin).astype(BF16)
    v = pv.astype(BF16).reshape(rows, heads, HD)
    m = mg.reshape(rows, heads, HD)
    span = 256
    index = jnp.arange(rows, dtype=jnp.int32)

    def step(carry, items):
        dk, dv = carry
        qi, mi, row_index, row_seg = items
        scores = jnp.einsum("qhd,khd->hqk", qi, k, preferred_element_type=F32) * scale
        allowed = (index[None, :] <= row_index[:, None]) & (segments[None, :] == row_seg[:, None])
        scores = jnp.where(allowed[None], scores, -1e30)
        expo = jnp.exp(scores - jnp.max(scores, -1, keepdims=True))
        probs = expo / jnp.sum(expo, -1, keepdims=True)
        low = probs.astype(BF16)
        out = jnp.einsum("hqk,khd->qhd", low, v, preferred_element_type=F32).astype(BF16)
        prob_grad = jnp.einsum("qhd,khd->hqk", mi, v, preferred_element_type=F32)
        delta = jnp.sum(probs * prob_grad, -1, keepdims=True)
        score_grad = (probs * (prob_grad - delta)).astype(BF16)
        dq = jnp.einsum("hqk,khd->qhd", score_grad, k, preferred_element_type=F32) * scale
        dk = dk + jnp.einsum("hqk,qhd->khd", score_grad, qi, preferred_element_type=F32) * scale
        dv = dv + jnp.einsum("hqk,qhd->khd", low, mi, preferred_element_type=F32)
        return (dk, dv), (out, dq)

    zero = jnp.zeros((rows, heads, HD), F32)
    cut = lambda t: t.reshape((rows // span, span) + t.shape[1:])
    (dk, dv), (out, dq) = lax.scan(step, (zero, zero), (cut(q), cut(m), cut(index), cut(segments)))
    flat = lambda t: t.reshape(rows, cols)
    return (
        flat(out),
        flat(rotate(dq.reshape(rows, cols), -sin)).astype(BF16),
        flat(rotate(dk.reshape(rows, cols), -sin)).astype(BF16),
        flat(dv).astype(BF16),
    )


def gather_plain(x, g, wsrc, places, segments):
    pieces = lax.all_to_all(wsrc, "ctx", split_axis=1, concat_axis=1, tiled=True)
    weights = lax.all_gather(pieces, "dp", axis=1, tiled=True)
    along = lambda t: lax.all_gather(t, "ctx", axis=0, tiled=True)
    return along(x), along(g), weights, along(places), along(segments)


def scatter_plain(out_part, normed_part, weight_part):
    summed = lambda t: lax.psum(
        lax.psum_scatter(t, "ctx", scatter_dimension=0, tiled=True), "tp"
    ).astype(F32)
    pieces = lax.psum_scatter(weight_part, "dp", scatter_dimension=1, tiled=True)
    pieces = lax.all_to_all(pieces, "ctx", split_axis=1, concat_axis=1, tiled=True)
    return summed(out_part), summed(normed_part), pieces.astype(F32)


def place_of():
    dp, me, core = lax.axis_index("dp"), lax.axis_index("ctx"), lax.axis_index("tp")
    return dp, me, core, dp + 1 - 2 * (dp % 2), dp + 2 - 4 * (dp // 2)


def greet(ways):
    dp, me, core, dpx, dpy = place_of()
    barrier = pltpu.get_barrier_semaphore()
    for device in [(dp, me, 1 - core), (dpx, me, core), (dpy, me, core)] + [
        (dp, (me + k) % ways, core) for k in range(1, ways)
    ]:
        pl.semaphore_signal(barrier, inc=1, device_id=device, device_id_type=MESH)
    pl.semaphore_wait(barrier, ways + 2)


def remote(src, dst, send, recv, device):
    return pltpu.make_async_remote_copy(
        src_ref=src, dst_ref=dst, send_sem=send, recv_sem=recv, device_id=device, device_id_type=MESH
    )


PIECES = 2


def gelu_and_slope(v):
    c = math.sqrt(2.0 / math.pi)
    square = v * v
    tanh = jnp.tanh(c * v * (1.0 + 0.044715 * square))
    half = 0.5 * (1.0 + tanh)
    slope = half + 0.5 * c * v * (1.0 - tanh * tanh) * (1.0 + 3.0 * 0.044715 * square)
    return v * half, slope


def forward_body(
    ways, x, g, w1, w2, wq, wd, places, segments, lines, freq,
    go, no, xho, ho, hgo, outo, ngo, mgo, wao, qo, ko, vo, mixo, lseo, coso, sino, ido, small,
    xo, w1v, w2v, wqv, wdv, norm, xb, gb, pre, hid, slope, hgb, ob, nb, mb, qb, kb, vb, mixb, lse, cosb, sinb, labr, labc, ids,
    zs, zr, ts, tr, ws, wr, ls, lr, ds, dr, ids_s, ids_r, own, ls_in, ls_out, keep_out,
):
    dp, me, core, dpx, dpy = place_of()
    rows, width = x.shape
    piece = rows // 2 // PIECES
    groups, depth = ws.shape[0], w1.shape[0]
    cols, head_cols = w1v.shape[1], wdv.shape[0]
    gain, shift = lines.at[0:1, :], lines.at[1:2, :]
    fc1_shift, qkv_shift = lines.at[2:3, 0:cols], lines.at[3:4, 0 : 3 * head_cols]
    srcs, outs = (x, g), (xo, go)
    blocks = [me, 1 + me % 2, None, 3 * (1 - me // 2)]
    blocks[2] = 6 - me - blocks[1] - blocks[3]

    def part(which, s):
        return pl.ds(pl.multiple_of(which * (rows // 2) + s * piece, 16), piece)

    def along(a, owner, s, side, mine=False):
        at = part(core, s)
        src = srcs[a].at[at, :] if mine else outs[a].at[owner, at, :]
        return remote(
            src,
            outs[a].at[owner, at, :],
            zs.at[side, a, owner, s],
            zr.at[a, owner, s],
            (dp, me - 1 + 2 * side, core),
        )

    def across(a, owner, s, which):
        at = part(which, s)
        ref = outs[a].at[owner, at, :]
        return remote(ref, ref, ts.at[a, owner, s], tr.at[a, owner, s], (dp, me, 1 - core))

    def here(chip, j, height=None):
        return pl.ds(pl.multiple_of((chip * ways + j) * depth, depth), depth)

    def held(grp, chip, j):
        at = here(chip, j)
        return ([w1v.at[at, :]], [w2v.at[:, at]], [wqv.at[at, :], wdv.at[:, at]])[grp]

    def given(grp, d):
        at = here(dp, me)
        mine = pl.ds(pl.multiple_of(d * cols, 128), cols)
        if grp == 0:
            return [(w1.at[:, mine], w1v.at[at, :])]
        if grp == 1:
            return [(w2.at[mine, :], w2v.at[:, at])]
        mine = pl.ds(pl.multiple_of(d * head_cols, 128), head_cols)
        return [
            (wq.at[c, :, mine], wqv.at[at, pl.ds(c * head_cols, head_cols)]) for c in range(3)
        ] + [(wd.at[mine, :], wdv.at[:, at])]

    def share(grp, k):
        d = (me + k) % ways
        return [
            remote(src, dst, ws.at[grp, k, i], wr.at[grp, k, i], (dp, d, core))
            for i, (src, dst) in enumerate(given(grp, d))
        ]

    def keep(grp):
        return [
            pltpu.make_async_copy(src, dst, ws.at[grp, 0, i])
            for i, (src, dst) in enumerate(given(grp, me))
        ]

    def source(k):
        return (me - k + ways) % ways

    def spread(grp, k, axis):
        return [
            remote(ref, ref, ls.at[axis, grp, k, i], lr.at[axis, grp, k, i], ((dpx, dpy)[axis], me, core))
            for i, ref in enumerate(held(grp, dp, source(k)))
        ]

    def corner(grp, k):
        axis = (grp + k) % 2
        return [
            remote(ref, ref, ds.at[grp, k, i], dr.at[grp, k, i], ((dpy, dpx)[axis], me, core))
            for i, ref in enumerate(held(grp, (dpx, dpy)[axis], source(k)))
        ]

    def start(copies):
        for copy in copies:
            copy.start()

    def wait_recv(copies):
        for copy in copies:
            copy.wait_recv()

    def wait_send(copies):
        for copy in copies:
            copy.wait_send()

    def labels(k):
        return remote(ids, ido.at[me], ids_s.at[k], ids_r.at[k], (dp, (me + k) % ways, core))

    def send_own(a, s):
        pl.when(me > 0)(lambda: along(a, me, s, 0, True).start())
        pl.when(me < ways - 1)(lambda: along(a, me, s, 1, True).start())

    def send_share(grp, k):
        if k:
            start(share(grp, k))
            return
        start(keep(grp))
        for copy in keep(grp):
            copy.wait()
        for axis in range(2):
            start(spread(grp, 0, axis))

    def pass_on(a, k, s):
        @pl.when(me + k < ways)
        def _():
            along(a, me + k, s, 0).wait_recv()
            pl.when(me > 0)(lambda: along(a, me + k, s, 0).start())
            across(a, me + k, s, core).start()

        @pl.when(me - k >= 0)
        def _():
            along(a, me - k, s, 1).wait_recv()
            pl.when(me < ways - 1)(lambda: along(a, me - k, s, 1).start())
            across(a, me - k, s, core).start()

    def spread_on(grp, k):
        wait_recv(share(grp, k))
        for axis in range(2):
            start(spread(grp, k, axis))

    def corner_on(grp, k):
        wait_recv(spread(grp, k, (grp + k) % 2))
        start(corner(grp, k))

    def settle(grp):
        for k in range(ways):
            wait_recv(spread(grp, k, 1 - (grp + k) % 2))
            wait_recv(corner(grp, k))

    def arrive(a, t):
        if t:
            for s in range(PIECES):
                across(a, blocks[t], s, 1 - core).wait_recv()

    def loop(count, body):
        lax.fori_loop(0, count, lambda i, c: (body(i), c)[1], 0)

    def load_x(t):
        src = x if t == 0 else xo.at[blocks[t]]
        return pltpu.make_async_copy(src, xb.at[t % 2], ls_in.at[0, t])

    def load_g(t):
        src = g if t == 0 else go.at[blocks[t]]
        return pltpu.make_async_copy(src, gb.at[t % 2], ls_in.at[1, t])

    def store(which, t):
        o = blocks[t]
        src, dst = (
            (xb.at[t % 2], xho.at[o]),
            (norm.at[o], no.at[o]),
            (hid.at[o], ho.at[o]),
            (ob.at[t % 2], outo.at[o]),
            (nb.at[t % 2], ngo.at[o]),
            (hgb.at[t % 2], hgo.at[o]),
            (mb.at[t], mgo.at[o]),
        )[which]
        return pltpu.make_async_copy(src, dst, ls_out.at[which, t])

    def fetch_x(t):
        arrive(0, t)
        if t >= 2:
            store(0, t - 2).wait()
        load_x(t).start()

    def fetch_g(t):
        arrive(1, t)
        if t == 2:
            own_g.wait()
        load_g(t).start()

    own_g = pltpu.make_async_copy(gb.at[0], go.at[me], own.at[0])

    def normalise(t):
        load_x(t).wait()
        step = 192

        def body(i):
            at = pl.ds(pl.multiple_of(i * step, step), step)
            xf = xb[t % 2, at, :].astype(F32)
            centred = xf - jnp.mean(xf, -1, keepdims=True)
            inv_std = lax.rsqrt(jnp.mean(centred * centred, -1, keepdims=True) + EPS)
            x_hat = centred * inv_std
            norm[blocks[t], at, :] = (x_hat * gain[...] + shift[...]).astype(BF16)
            xb[t % 2, at, :] = x_hat.astype(BF16)

        loop(rows // step, body)
        store(0, t).start()
        store(1, t).start()

    wide = 512

    def span(i):
        return pl.ds(pl.multiple_of(i * wide, wide), wide)

    def up(t):
        o = blocks[t]

        def mul(i):
            pre[:, span(i)] = dot_nn(norm[o], w1v[:, span(i)]) + fc1_shift[:, span(i)]

        loop(cols // wide, mul)

        def act(i):
            at = pl.ds(pl.multiple_of(i * 16, 16), 16)
            value, grad = gelu_and_slope(pre[at, :])
            hid[o, at, :] = value.astype(BF16)
            slope[o, at, :] = grad

        loop(rows // 16, act)
        store(2, t).start()

    def tables():
        for k in range(1, ways):
            labels(k).wait_recv()
        keeps[0].wait()
        lse[...] = jnp.zeros_like(lse)
        for o in range(ways):
            at = slice(o * rows, (o + 1) * rows)
            rows_here = ido[o].astype(F32)
            labr[:, at] = rows_here
            columns = jnp.transpose(rows_here)
            labc[at, :] = columns
            angles = columns[:, 0:1] * freq[...]
            cosb[at, :] = jnp.cos(angles)
            sinb[at, :] = jnp.sin(angles)
        for copy in table_stores:
            copy.start()

    def project(t):
        o = blocks[t]
        at = pl.ds(pl.multiple_of(o * rows, 16), rows)
        cos, sin = cosb[at, :], sinb[at, :]
        for which, ref in enumerate((qb, kb, vb)):
            heads = pl.ds(which * head_cols, head_cols)
            v = dot_nn(norm[o], wqv[:, heads]) + qkv_shift[:, heads]
            for pair in range(head_cols // 128):
                part_of = v[:, pair * 128 : (pair + 1) * 128]
                if which < 2:
                    part_of = turn(part_of, cos, sin)
                part_of = part_of.astype(BF16)
                if which == 0:
                    part_of = part_of * BF16(1.0 / math.sqrt(HD))
                ref[at, pl.ds(pair * 128, 128)] = part_of

    def attend(pair, i):
        lanes = pl.ds(pair * 128, 128)
        here, seen = pl.ds(i * QUERIES, QUERIES), pl.ds(0, (i + 1) * QUERIES)
        allowed = allowed_keys(labr, labc, i)
        first = lax.broadcasted_iota(jnp.int32, (QUERIES, 128), 1) < HD
        lane = lax.broadcasted_iota(jnp.int32, (QUERIES, 128), 1)
        keys, values = kb[seen, lanes], vb[seen, lanes]
        queries, logs = qb[here, lanes], lse[here, :]
        both = jnp.concatenate([jnp.where(first, queries, 0), jnp.where(first, 0, queries)], 0)
        all_scores = dot_nt(both, keys)
        probs = []
        for sub in range(2):
            scores = jnp.where(allowed, all_scores[sub * QUERIES : (sub + 1) * QUERIES], -1e30)
            top = jnp.max(scores, 1, keepdims=True)
            expo = jnp.exp(scores - top)
            total = jnp.sum(expo, 1, keepdims=True)
            probs.append((expo * (1.0 / total)).astype(BF16))
            logs = jnp.where(lane == pair * 2 + sub, top + jnp.log(total), logs)
        mixed = dot_nn(jnp.concatenate(probs, 0), values)
        lse[here, :] = logs
        mixb[here, lanes] = jnp.where(first, mixed[:QUERIES], mixed[QUERIES:]).astype(BF16)

    def down(t):
        if t >= 2:
            store(3, t - 2).wait()
        o = blocks[t]
        at = pl.ds(pl.multiple_of(o * rows, 16), rows)

        def mul(i):
            total = dot_nn(hid[o], w2v[:, span(i)])
            total = total + dot_nn(mixb[at, :], wdv[:, span(i)])
            ob[t % 2, :, span(i)] = total.astype(BF16)

        loop(width // wide, mul)
        store(3, t).start()

    def back(t):
        if t >= 2:
            store(5, t - 2).wait()
        load_g(t).wait()
        if t == 0:
            own_g.start()
            small[...] = jnp.zeros_like(small)
            small[2:3, :] = jnp.sum(gb[0].astype(F32), 0, keepdims=True)
        o = blocks[t]

        def mul(i):
            act = dot_nt(gb[t % 2], w2v[span(i), :])
            grad = (act * slope[o, :, span(i)]).astype(BF16)
            hgb[t % 2, :, span(i)] = grad
            total = jnp.sum(grad.astype(F32), 0, keepdims=True)
            small[3:4, span(i)] += total

        loop(cols // wide, mul)
        store(5, t).start()

    def back_on(t):
        if t >= 2:
            store(4, t - 2).wait()

        def mul_back(i):
            nb[t % 2, :, span(i)] = dot_nt(hgb[t % 2], w1v[span(i), :]).astype(BF16)

        loop(width // wide, mul_back)
        store(4, t).start()
        mb[t] = dot_nt(gb[t % 2], wdv[...]).astype(BF16)
        store(6, t).start()

    ids[...] = jnp.zeros_like(ids)
    ids[0:1, :] = places[...]
    ids[1:2, :] = segments[...]
    greet(ways)
    for k in range(1, ways):
        labels(k).start()
    keeps = [
        pltpu.make_async_copy(ids, ido.at[me], own.at[1]),
    ]
    for copy in keeps:
        copy.start()
    wa_out = pltpu.make_async_copy(wqv, wao, own.at[2])
    stores = [
        pltpu.make_async_copy(src, dst, keep_out.at[i])
        for i, (src, dst) in enumerate(
            ((cosb, coso), (sinb, sino), (qb, qo), (kb, ko), (vb, vo), (mixb, mixo), (lse, lseo))
        )
    ]
    table_stores, state_stores = stores[:2], stores[2:]
    steps = dict(
        X=lambda s: send_own(0, s),
        G=lambda s: send_own(1, s),
        S=send_share,
        W=wa_out.start,
        Z=lambda: [copy.start() for copy in state_stores],
        x=lambda k, s: pass_on(0, k, s),
        g=lambda k, s: pass_on(1, k, s),
        s=spread_on,
        c=corner_on,
        e=settle,
        l=tables,
        i=fetch_x,
        j=fetch_g,
        n=normalise,
        u=up,
        p=project,
        a=attend,
        d=down,
        b=back,
        r=back_on,
    )
    plan = (
        "S22", "S21", "X0", "S10", "S20", "S23", "X1", "S01", "c10", "s22", "l", "S00", "c20",
        "x10", "s23", "i0", "S03", "s21", "c22", "S02", "x11", "S11", "c23", "c21", "s01", "c01",
        "i1", "S13", "s03", "e2", "j0", "n0", "c00", "x20", "s02", "W", "x21", "i2", "p0", "n1",
        "x30", "c02", "c03", "p1", "S12", "n2", "p2", "s13", "e0", "G0", "u0", "s11", "x31", "i3",
        "u1", "G1", "u2", "n3", "c13", "p3", "a12", "a05", "s12", "a14", "a00", "g10", "a04",
        "a11", "a03", "a10", "a01", "c11", "a02", "c12", "a15", "g11", "a13", "u3", "j1", "e1",
        "b0", "Z", "g20", "d0", "d1", "b1", "g21", "r1", "r0", "j2", "g30", "d2", "g31", "d3",
        "j3", "b2", "r2", "b3", "r3",
    )
    for word in plan:
        steps[word[0]](*(int(digit) for digit in word[1:]))
    for k in range(1, ways):
        labels(k).wait_send()
    for copy in table_stores + state_stores:
        copy.wait()
    wa_out.wait()
    for t in range(4):
        for which in (1, 2, 6):
            store(which, t).wait()
        if t >= 2:
            for which in (0, 3, 4, 5):
                store(which, t).wait()
    for a in range(2):
        for owner in range(ways):
            for s in range(PIECES):

                @pl.when(owner != me)
                def _():
                    across(a, owner, s, core).wait_send()

                @pl.when((me > 0) & (owner >= me))
                def _():
                    along(a, owner, s, 0).wait_send()

                @pl.when((me < ways - 1) & (owner <= me))
                def _():
                    along(a, owner, s, 1).wait_send()

    for grp in range(groups):
        for k in range(ways):
            if k:
                wait_send(share(grp, k))
            for axis in range(2):
                wait_send(spread(grp, k, axis))
            wait_send(corner(grp, k))


def forward(x, g, w1, w2, wq, wd, places, segments, lines):
    ways = lax.axis_size("ctx")
    rows, width = x.shape
    groups, cols, head_cols = 3, w1.shape[1] // ways, wd.shape[0] // ways
    dma = pltpu.SemaphoreType.DMA
    vmem = pltpu.VMEM
    anywhere = pl.BlockSpec(memory_space=pl.ANY)
    inside = pl.BlockSpec(memory_space=pltpu.VMEM)
    seq = lambda n, dtype=BF16: jax.ShapeDtypeStruct((ways, rows, n), dtype)
    tokens = ways * rows
    line = lambda n, dtype: jax.ShapeDtypeStruct((tokens, n), dtype)
    outs = pl.pallas_call(
        functools.partial(forward_body, ways),
        in_specs=[anywhere] * 6 + [inside] * 4,
        out_specs=[anywhere] * 16 + [inside] * 2 + [anywhere],
        out_shape=[
            seq(width),
            seq(width),
            seq(width),
            seq(cols),
            seq(cols),
            seq(width),
            seq(width),
            seq(head_cols),
            jax.ShapeDtypeStruct((width, 3 * head_cols), BF16),
            line(head_cols, BF16),
            line(head_cols, BF16),
            line(head_cols, BF16),
            line(head_cols, BF16),
            line(128, F32),
            line(128, F32),
            line(128, F32),
            jax.ShapeDtypeStruct((ways, 8, rows), jnp.int32),
            jax.ShapeDtypeStruct((8, width), F32),
            seq(width),
        ],
        scratch_shapes=[
            vmem((width, cols), BF16),
            vmem((cols, width), BF16),
            vmem((width, 3 * head_cols), BF16),
            vmem((head_cols, width), BF16),
            vmem((ways, rows, width), BF16),
            vmem((2, rows, width), BF16),
            vmem((2, rows, width), BF16),
            vmem((rows, cols), F32),
            vmem((ways, rows, cols), BF16),
            vmem((ways, rows, cols), F32),
            vmem((2, rows, cols), BF16),
            vmem((2, rows, width), BF16),
            vmem((2, rows, width), BF16),
            vmem((ways, rows, head_cols), BF16),
            vmem((tokens, head_cols), BF16),
            vmem((tokens, head_cols), BF16),
            vmem((tokens, head_cols), BF16),
            vmem((tokens, head_cols), BF16),
            vmem((tokens, 128), F32),
            vmem((tokens, 128), F32),
            vmem((tokens, 128), F32),
            vmem((8, tokens), F32),
            vmem((tokens, 8), F32),
            vmem((8, rows), jnp.int32),
            dma((2, 2, ways, PIECES)),
            dma((2, ways, PIECES)),
            dma((2, ways, PIECES)),
            dma((2, ways, PIECES)),
            dma((groups, ways, 4)),
            dma((groups, ways, 4)),
            dma((2, groups, ways, 2)),
            dma((2, groups, ways, 2)),
            dma((groups, ways, 2)),
            dma((groups, ways, 2)),
            dma((ways,)),
            dma((ways,)),
            dma((3,)),
            dma((2, ways)),
            dma((7, ways)),
            dma((7,)),
        ],
        compiler_params=pltpu.CompilerParams(
            collective_id=0, has_side_effects=True, vmem_limit_bytes=62 * MIB
        ),
    )(
        x, g, w1, w2, wq, wd, places, segments, lines, frequencies(),
    )
    return outs


def backward_body(
    ways,
    p0, ngm, normed, xh, g_flat, hg, hidden, q, k, v, mg, mix, lse, cos, sin, wa, labels, small,
    x, g, lines, out, gin, g1, g2, gq, gd, tin, sg, ss_, sb, sf, sq,
    lt, ra, rb, wp, qv, kv, vv, mgv, lsev, cosv, sinv, dkv, dvv, labr, labc,
    acc, zin, tst, ngi, xhi, ngs, gown, gsend, first_in, second_in, sums, sum_in, sum_out,
    smallo, tps, tpr, zs, zr, fs, fr, ss, sr, ws, wr, os, orr, loc, tloc, sms, smr, ins, lts, ngl,
):
    dp, me, core, dpx, dpy = place_of()
    rows, width = out.shape
    half = rows // 2
    piece = half // PIECES
    groups = first_in.shape[0]
    span_rows = gown.shape[3]
    lanes = gown.shape[4]
    depth = span_rows // ways
    cols, head_cols = hg.shape[1], q.shape[1]
    nxt = (dpx, dpy)
    far = dpx + dpy - dp
    scale = 1.0 / math.sqrt(HD)

    order = (0, 3, 1, 2)

    def part(which, s):
        return pl.ds(pl.multiple_of(which * half + s * piece, 16), piece)

    def loop(count, body):
        lax.fori_loop(0, count, lambda i, c: (body(i), c)[1], 0)

    def add(dst, src, height):
        step = 32

        def body(i):
            at = pl.ds(pl.multiple_of(i * step, step), step)
            dst[at, :] = dst[at, :] + src[at, :]

        loop(height // step, body)

    def swap(a, d, s):
        at = pl.ds(s * piece, piece)
        src = p0.at[d, part(1 - core, s), :] if a == 0 else ngs.at[order.index(d) % 2, at, :]
        return remote(
            src, tin.at[a, d, s], tps.at[a, d, s], tpr.at[a, d, s], (dp, me, 1 - core)
        )

    def load(d, s):
        return pltpu.make_async_copy(p0.at[d, part(core, s), :], acc.at[0, d, s], loc.at[d, s])

    def load_swapped(a, d, s):
        return pltpu.make_async_copy(tin.at[a, d, s], tst.at[s], tloc.at[a, d, s])

    def slot(d, side):
        if side:
            return d
        here = 1 - jnp.minimum(jnp.abs(me - 1 - d), 1)
        return d + here * (ways - d)

    def came(d, side):
        if side:
            return d
        here = 1 - jnp.minimum(jnp.abs(me - d), 1)
        return d + here * (ways - d)

    def stream(a, d, s, side):
        return remote(
            acc.at[a, d, s],
            zin.at[a, slot(d, side), s],
            zs.at[a, d, s],
            zr.at[a, slot(d, side), s],
            (dp, me - 1 + 2 * side, core),
        )

    def arrived(a, d, s, side):
        ref = zin.at[a, came(d, side), s]
        return remote(
            ref, ref, zs.at[a, d, s], zr.at[a, came(d, side), s], (dp, me - 1 + 2 * side, core)
        )

    results = (out, gin)

    def finish(a, s, which):
        ref = results[a].at[part(which, s), :]
        return remote(acc.at[a, me, s], ref, os.at[0, a, s], orr.at[a, s], (dp, me, 1 - core))

    def finish_here(a, s):
        return pltpu.make_async_copy(
            acc.at[a, me, s], results[a].at[part(core, s), :], os.at[1, a, s]
        )

    def load_own(i):
        at = pl.ds(pl.multiple_of(core * half, 16), half)
        src, dst = ((x.at[at, :], ngi.at[0]), (g.at[at, :], ngi.at[1]))[i]
        return pltpu.make_async_copy(src, dst, ins.at[11 + i])

    def merge(a, d):
        for s in range(PIECES):
            swap(a, d, s).wait_recv()
            load_swapped(a, d, s).start()
        for s in range(PIECES):
            load_swapped(a, d, s).wait()
            if a == 0:
                load(d, s).wait()
            add(acc.at[a, d, s], tst.at[s], piece)
            pl.when((me == 0) & (d > 0))(lambda: stream(a, d, s, 1).start())
            pl.when((me == ways - 1) & (d < ways - 1))(lambda: stream(a, d, s, 0).start())

    def hop(a, far_by, j, s):
        d = ways - 1 - j

        @pl.when(me == far_by)
        def _():
            arrived(a, d, s, 1).wait_recv()
            add(acc.at[a, d, s], zin.at[a, came(d, 1), s], piece)
            if d > far_by:
                stream(a, d, s, 1).start()

        @pl.when(me == ways - 1 - far_by)
        def _():
            arrived(a, j, s, 0).wait_recv()
            add(acc.at[a, j, s], zin.at[a, came(j, 0), s], piece)
            if j < ways - 1 - far_by:
                stream(a, j, s, 0).start()

    def last(a):
        if a == 0:
            for i in range(2):
                load_own(i).start()
            for i in range(2):
                load_own(i).wait()
        for s in range(PIECES):
            at = pl.ds(s * piece, piece)
            xf = ngi[0, at, :].astype(F32)
            total = acc[a, me, s].astype(F32)
            if a == 0:
                acc[a, me, s] = (xf + total + lines[4:5, :]).astype(BF16)
            else:
                centred = xf - jnp.mean(xf, -1, keepdims=True)
                inv_std = lax.rsqrt(jnp.mean(centred * centred, -1, keepdims=True) + EPS)
                x_hat = centred * inv_std
                scaled = total * lines[0:1, :]
                change = (
                    scaled
                    - jnp.mean(scaled, -1, keepdims=True)
                    - x_hat * jnp.mean(scaled * x_hat, -1, keepdims=True)
                )
                acc[a, me, s] = (ngi[1, at, :].astype(F32) + inv_std * change).astype(BF16)
            finish(a, s, core).start()
            finish_here(a, s).start()

    def lanes_of(path):
        return pl.ds(path * lanes, lanes)

    def first(grp, path, i):
        return remote(
            gsend.at[2 * i + path],
            first_in.at[grp, path, i],
            fs.at[grp, path, i],
            fr.at[grp, path, i],
            (nxt[path], me, core),
        )

    def second(grp, path):
        return remote(
            gown.at[grp % 2, path, 0],
            second_in.at[grp, path],
            ss.at[grp, path],
            sr.at[grp, path],
            (nxt[1 - path], me, core),
        )

    def pieces(grp, path, d):
        ref = gown.at[grp % 2, path, 1]
        across = pl.ds(pl.multiple_of(me * cols + path * lanes, 128), lanes)
        heads = pl.ds(pl.multiple_of(me * head_cols, 128), head_cols)
        rows_of_d = pl.ds(pl.multiple_of(d * depth, 128), depth)
        if grp == 0:
            return [(ref.at[rows_of_d, :], g1.at[:, across])]
        if grp == 1:
            return [(ref.at[:, rows_of_d], g2.at[across, :])]
        if path == 0:
            return [
                (ref.at[rows_of_d, pl.ds(c * head_cols, head_cols)], gq.at[c, :, heads])
                for c in range(2)
            ]
        per = head_cols // depth
        dense_rows = pl.ds(pl.multiple_of(d // per * head_cols, 128), head_cols)
        dense_lanes = pl.ds(pl.multiple_of(head_cols + d % per * depth, 128), depth)
        return [
            (ref.at[rows_of_d, pl.ds(0, head_cols)], gq.at[2, :, heads]),
            (ref.at[dense_rows, dense_lanes], gd.at[heads, :]),
        ]

    def share(grp, path, i):
        d = (me + i) % ways
        return [
            remote(src, dst, ws.at[grp, path, i, n], wr.at[grp, path, i, n], (dp, d, core))
            for n, (src, dst) in enumerate(pieces(grp, path, d))
        ]

    def keep(grp, path):
        return [
            pltpu.make_async_copy(src, dst, ws.at[grp, path, 0, n])
            for n, (src, dst) in enumerate(pieces(grp, path, me))
        ]

    def start(copies):
        for copy in copies:
            copy.start()

    def wait(copies):
        for copy in copies:
            copy.wait()

    def wait_recv(copies):
        for copy in copies:
            copy.wait_recv()

    def wait_send(copies):
        for copy in copies:
            copy.wait_send()

    quarters = (far, dpx, dpy, dp)

    def load_left(grp, r, which=0):
        at = pl.ds(pl.multiple_of(quarters[r] * span_rows, 128), span_rows)
        src = (normed, g_flat, normed)[grp] if which == 0 else g_flat
        into = (4 * grp + r) % 2 if grp < 2 else which
        return pltpu.make_async_copy(src.at[:, at], lt.at[into], lts.at[grp, r, which])

    def products(grp, r):
        load_left(grp, r).wait()
        if 4 * grp + r < 7:
            after = 4 * grp + r + 1
            load_left(after // 4, after % 4).start()
        left = (4 * grp + r) % 2 if grp < 2 else 0
        if grp == 0:
            tile = dot_tn(lt[left], ra[...]).astype(BF16)
        elif grp == 1:
            tile = dot_tn(rb[...], lt[left]).astype(BF16)
        else:
            tile = dot_tn(lt[0], ra[:, : 3 * head_cols]).astype(BF16)
            if r < 3:
                load_left(grp, r + 1).start()
            load_left(grp, r, 1).wait()
            dense = dot_tn(ra[:, 3 * head_cols :], lt[1]).astype(BF16)
            if r < 3:
                load_left(grp, r + 1, 1).start()
        for path in range(2):
            if r == 0:
                dst = gsend.at[path]
                i = 0
            elif r == 1 + path:
                dst = gsend.at[2 + path]
                i = 1
            else:
                dst = gown.at[grp % 2, path, 1 if r == 3 else 0]
                i = None
            if i is not None and grp:
                first(grp - 1, path, i).wait_send()
            if i is None and grp == 2:
                if r == 3:
                    wait(keep(0, path))
                    for n in range(1, ways):
                        wait_send(share(0, path, n))
                else:
                    second(0, path).wait_send()
            half_of = slice(path * lanes, (path + 1) * lanes)
            if grp == 1:
                dst[...] = tile[half_of]
            elif grp == 2 and path == 1:
                dst[:, :head_cols] = tile[:, 2 * head_cols :]
                dst[:head_cols, head_cols:] = dense[:, :head_cols]
                dst[head_cols:, head_cols:] = dense[:, head_cols:]
            else:
                dst[...] = tile[:, half_of]
            if i is not None:
                first(grp, path, i).start()

    def pass_sum(grp, path):
        first(grp, path, 0).wait_recv()
        add(gown.at[grp % 2, path, 0], first_in.at[grp, path, 0], span_rows)
        second(grp, path).start()

    def first_sum(grp, path):
        first(grp, path, 1).wait_recv()
        add(gown.at[grp % 2, path, 1], first_in.at[grp, path, 1], span_rows)

    def second_sum(grp, path):
        second(grp, path).wait_recv()
        add(gown.at[grp % 2, path, 1], second_in.at[grp, path], span_rows)
        for i in range(1, ways):
            start(share(grp, path, i))
        start(keep(grp, path))

    pairs = (
        (hg, ra), (hidden, rb), (wa, wp),
        (q, qv), (k, kv), (v, vv), (mg, mgv), (lse, lsev), (cos, cosv), (sin, sinv),
    )

    def copy_in(i):
        return pltpu.make_async_copy(*pairs[i], ins.at[i])

    mix_in = pltpu.make_async_copy(mix, ra.at[:, pl.ds(3 * head_cols, head_cols)], ins.at[10])

    def begin():
        for i in range(3, 10):
            copy_in(i).wait()
        mix_in.start()
        mix_in.wait()
        for o in range(ways):
            at = slice(o * rows, (o + 1) * rows)
            rows_here = labels[o].astype(F32)
            labr[:, at] = rows_here
            labc[at, :] = jnp.transpose(rows_here)

    def turned_back(value, at):
        return turn(value, cosv[at, :], -sinv[at, :]).astype(BF16)

    def attend_back(pair, i):
        at = pl.ds(pair * 128, 128)
        here, seen = pl.ds(i * QUERIES, QUERIES), pl.ds(0, (i + 1) * QUERIES)
        allowed = allowed_keys(labr, labc, i)
        head = lax.broadcasted_iota(jnp.int32, (QUERIES, 128), 1) < HD
        if i == 0:
            dkv[...] = jnp.zeros_like(dkv)
            dvv[...] = jnp.zeros_like(dvv)
        keys, values = kv[seen, at], vv[seen, at]
        mixed = ra[here, pl.ds(3 * head_cols + pair * 128, 128)].astype(F32)
        parts, kept = [], []
        for sub in range(2):
            mine = head if sub == 0 else ~head
            qi = jnp.where(mine, qv[here, at], 0)
            mi = jnp.where(mine, mgv[here, at], 0)
            log = lsev[here, pair * 2 + sub : pair * 2 + sub + 1]
            probs = jnp.where(allowed, jnp.exp(dot_nt(qi, keys) - log), 0.0)
            prob_grad = dot_nt(mi, values)
            delta = jnp.sum(mi.astype(F32) * mixed, 1, keepdims=True)
            score_grad = (probs * (prob_grad - delta)).astype(BF16)
            parts.append(dot_nn(score_grad, keys))
            kept.append((score_grad, qi, probs.astype(BF16), mi))
        stacked = [jnp.concatenate(both, 0) for both in zip(*kept)]
        dkv[seen, :] += dot_tn(stacked[0], stacked[1])
        dvv[seen, :] += dot_tn(stacked[2], stacked[3])
        ra[here, at] = turned_back(jnp.where(head, parts[0], parts[1]) * scale, here)
        if i == rows * ways // QUERIES - 1:
            ra[:, pl.ds(head_cols + pair * 128, 128)] = turned_back(dkv[...], slice(None))
            ra[:, pl.ds(2 * head_cols + pair * 128, 128)] = dvv[...].astype(BF16)

    def load_back(d, own):
        at = pl.ds(pl.multiple_of((core if own else 1 - core) * half, 16), half)
        return [
            pltpu.make_async_copy(ngm.at[d, at, :], ngi.at[own], ngl.at[0, d, own]),
            pltpu.make_async_copy(xh.at[d, at, :], xhi.at[own], ngl.at[1, d, own]),
        ]

    def normed_back(n):
        d = order[n]
        if n == 0:
            copy_in(2).wait()
            sums[...] = small[...]
        if n >= 2:
            for s in range(PIECES):
                swap(1, order[n - 2], s).wait_send()
        wide = 512
        for own in range(2):
            for copy in load_back(d, own):
                copy.wait()
            at = pl.ds(pl.multiple_of(d * rows + (core if own else 1 - core) * half, 16), half)

            def mul(i):
                cols = pl.ds(pl.multiple_of(i * wide, wide), wide)
                tile = dot_nt(ra[at, : 3 * head_cols], wp[cols, :]) + ngi[own, :, cols].astype(F32)
                sums[0:1, cols] += jnp.sum(tile * xhi[own, :, cols].astype(F32), 0, keepdims=True)
                sums[1:2, cols] += jnp.sum(tile, 0, keepdims=True)
                tile = tile.astype(BF16)
                for s in range(PIECES):
                    if own:
                        acc[1, d, s, :, cols] = tile[s * piece : (s + 1) * piece]
                    else:
                        ngs[n % 2, s * piece : (s + 1) * piece, cols] = tile[s * piece : (s + 1) * piece]

            loop(width // wide, mul)
            if not own:
                for s in range(PIECES):
                    swap(1, d, s).start()
            if n < ways - 1:
                for copy in load_back(order[n + 1], own):
                    copy.start()

    def small_send(i):
        src = sums if i == 0 else sum_out.at[i - 1]
        device = ((dp, me, 1 - core), (dpx, me, core), (dpy, me, core))[i]
        return remote(src, sum_in.at[i], sms.at[i], smr.at[i], device)

    def small_all(i):
        device = (dp, (me + i) % ways, core)
        return remote(sum_out.at[2], smallo.at[me], sms.at[2 + i], smr.at[2 + i], device)

    def small_begin():
        sums[4:5, : 3 * head_cols] = jnp.sum(ra[:, : 3 * head_cols].astype(F32), 0, keepdims=True)
        small_send(0).start()

    def small_step(i):
        small_send(i).wait_recv()
        before = sums[...] if i == 0 else sum_out[i - 1]
        after = before + sum_in[i]
        if i == 0:
            row = lax.broadcasted_iota(jnp.int32, after.shape, 0)
            after = jnp.where(row < 2, after, before)
        sum_out[i] = after
        if i < 2:
            small_send(i + 1).start()
        else:
            for n in range(1, ways):
                small_all(n).start()
            smallo[me] = after

    greet(ways)
    for d in order:
        for s in range(PIECES):
            swap(0, d, s).start()
            load(d, s).start()
    load_left(0, 0).start()
    for i in range(len(pairs)):
        copy_in(i).start()
    for own in range(2):
        for copy in load_back(order[0], own):
            copy.start()
    copy_in(0).wait()
    copy_in(1).wait()

    def last_left():
        load_left(2, 0).start()
        load_left(2, 0, 1).start()

    steps = dict(
        t=products,
        f=pass_sum,
        F=first_sum,
        h=second_sum,
        m=merge,
        z=hop,
        o=last,
        B=begin,
        a=attend_back,
        L=last_left,
        n=normed_back,
        Y=small_begin,
        y=small_step,
    )
    plan = (
        "t00", "m00", "m03", "t01", "m02", "t02", "t03", "B", "a00", "a01", "a02", "a03", "z0100",
        "f01", "a04", "a05", "m01", "t10", "a10", "F01", "a11", "z0101", "a12", "a13", "a14",
        "f00", "h01", "t11", "t12", "F00", "a15", "z0110", "z0200", "t13", "L", "z0201", "f10",
        "n0", "n1", "m10", "z0111", "m13", "h00", "t20", "n2", "n3", "z1100", "t21", "z0210",
        "f11", "F11", "z0211", "Y", "t22", "m11", "z0300", "z0120", "m12", "F10", "h10", "z1101",
        "z0301", "z0121", "f20", "t23", "z1200", "h11", "o0", "y0", "F21", "F20", "z1300", "h20",
        "z1110", "z1210", "z1111", "z1120", "y1", "f21", "z1201", "h21", "z1121", "y2", "z1301",
        "z1211", "o1",
    )
    for word in plan:
        steps[word[0]](*(int(digit) for digit in word[1:]))

    for i in range(3):
        small_send(i).wait_send()
    for i in range(1, ways):
        small_all(i).wait()
    for row, ref in enumerate((sg, ss_, sb)):
        total = smallo[0, row : row + 1, :]
        for o in range(1, ways):
            total = total + smallo[o, row : row + 1, :]
        ref[...] = total
    for o in range(ways):
        sf[:, o * cols : (o + 1) * cols] = smallo[o, 3:4, :cols]
        for c in range(3):
            sq[c : c + 1, o * head_cols : (o + 1) * head_cols] = smallo[
                o, 4:5, c * head_cols : (c + 1) * head_cols
            ]
    for a in range(2):
        for s in range(PIECES):
            finish(a, s, core).wait_send()
            finish_here(a, s).wait()
            finish(a, s, 1 - core).wait_recv()
            for n, d in enumerate(order):
                if a == 0 or n >= 2:
                    swap(a, d, s).wait_send()
                pl.when(d > me)(lambda: stream(a, d, s, 1).wait_send())
                pl.when(d < me)(lambda: stream(a, d, s, 0).wait_send())
    for grp in range(groups):
        for path in range(2):
            if grp == 2:
                for i in range(2):
                    first(grp, path, i).wait_send()
            if grp:
                second(grp, path).wait_send()
                wait(keep(grp, path))
            for i in range(1, ways):
                wait_recv(share(grp, path, i))
                if grp:
                    wait_send(share(grp, path, i))


def backward(
    p0, ngm, normed, xh, g_all, hg, hidden, q, k, v, mg, mix, lse, cos, sin, wa, labels, small,
    x, g, lines,
):
    ways, rows, width = p0.shape
    chips = lax.axis_size("dp")
    tokens = ways * rows
    groups, cols, head_cols = 3, hg.shape[-1], q.shape[-1]
    span = width // chips
    lanes = cols // 2
    piece = rows // 2 // PIECES
    half = rows // 2
    dma = pltpu.SemaphoreType.DMA
    vmem = pltpu.VMEM
    anywhere = pl.BlockSpec(memory_space=pl.ANY)
    inside = pl.BlockSpec(memory_space=pltpu.VMEM)
    flat = lambda t: t.reshape(tokens, t.shape[-1])
    depth = span // ways
    out, gin, g1, g2, gq, gd, unused, *sums = pl.pallas_call(
        functools.partial(backward_body, ways),
        in_specs=[anywhere] * 16 + [inside] * 2 + [anywhere] * 2 + [inside],
        out_specs=[anywhere] * 7 + [inside] * 5,
        out_shape=[
            jax.ShapeDtypeStruct((rows, width), BF16),
            jax.ShapeDtypeStruct((rows, width), BF16),
            jax.ShapeDtypeStruct((depth, ways * cols), BF16),
            jax.ShapeDtypeStruct((ways * cols, depth), BF16),
            jax.ShapeDtypeStruct((3, depth, ways * head_cols), BF16),
            jax.ShapeDtypeStruct((ways * head_cols, depth), BF16),
            jax.ShapeDtypeStruct((2, ways, PIECES, piece, width), BF16),
            jax.ShapeDtypeStruct((1, width), F32),
            jax.ShapeDtypeStruct((1, width), F32),
            jax.ShapeDtypeStruct((1, width), F32),
            jax.ShapeDtypeStruct((1, ways * cols), F32),
            jax.ShapeDtypeStruct((3, ways * head_cols), F32),
        ],
        scratch_shapes=[
            vmem((2, tokens, span), BF16),
            vmem((tokens, cols), BF16),
            vmem((tokens, cols), BF16),
            vmem((width, 3 * head_cols), BF16),
            vmem((tokens, head_cols), BF16),
            vmem((tokens, head_cols), BF16),
            vmem((tokens, head_cols), BF16),
            vmem((tokens, head_cols), BF16),
            vmem((tokens, 128), F32),
            vmem((tokens, 128), F32),
            vmem((tokens, 128), F32),
            vmem((tokens, 128), F32),
            vmem((tokens, 128), F32),
            vmem((8, tokens), F32),
            vmem((tokens, 8), F32),
            vmem((2, ways, PIECES, piece, width), BF16),
            vmem((2, ways + 1, PIECES, piece, width), BF16),
            vmem((PIECES, piece, width), BF16),
            vmem((2, half, width), BF16),
            vmem((2, half, width), BF16),
            vmem((2, half, width), BF16),
            vmem((2, 2, 2, span, lanes), BF16),
            vmem((4, span, lanes), BF16),
            vmem((groups, 2, 2, span, lanes), BF16),
            vmem((groups, 2, span, lanes), BF16),
            vmem(small.shape, F32),
            vmem((3,) + small.shape, F32),
            vmem((3,) + small.shape, F32),
            vmem((ways,) + small.shape, F32),
            dma((2, ways, PIECES)),
            dma((2, ways, PIECES)),
            dma((2, ways, PIECES)),
            dma((2, ways + 1, PIECES)),
            dma((groups, 2, 2)),
            dma((groups, 2, 2)),
            dma((groups, 2)),
            dma((groups, 2)),
            dma((groups, 2, ways, 2)),
            dma((groups, 2, ways, 2)),
            dma((2, 2, PIECES)),
            dma((2, PIECES)),
            dma((ways, PIECES)),
            dma((2, ways, PIECES)),
            dma((2 + ways,)),
            dma((2 + ways,)),
            dma((13,)),
            dma((groups, 4, 2)),
            dma((2, ways, 2)),
        ],
        compiler_params=pltpu.CompilerParams(
            collective_id=1, has_side_effects=True, vmem_limit_bytes=63 * MIB
        ),
    )(
        p0, ngm, flat(normed), xh, flat(g_all), flat(hg), flat(hidden), q, k, v, flat(mg), mix,
        lse, cos, sin, wa, labels, small, x, g, lines,
    )
    grads = tuple(t.astype(F32) for t in (gq, gd, g1, g2))
    return out, gin, grads, sums


def layer_norm(x):
    xf = x.astype(F32)
    mean = jnp.mean(xf, -1, keepdims=True)
    centred = xf - mean
    inv_std = lax.rsqrt(jnp.mean(centred * centred, -1, keepdims=True) + EPS)
    return centred * inv_std, inv_std


def plain_work(
    x, g, w_qkv, w_dense, w_fc1, w_fc2, places, segments, gain, shift, fc1_shift, qkv_shift, out_bias
):
    me, ways = lax.axis_index("ctx"), lax.axis_size("ctx")
    width = x.shape[1]
    depth = w_fc1.shape[0]
    cols, head_cols = w_fc1.shape[1] // ways, w_dense.shape[0] // ways
    fc1 = w_fc1.reshape(depth, ways, cols).transpose(1, 0, 2)
    fc2 = w_fc2.reshape(ways, cols, depth).transpose(0, 2, 1)
    qkv = w_qkv.reshape(3, depth, ways, head_cols).transpose(2, 1, 0, 3)
    dense = w_dense.reshape(ways, head_cols, depth).transpose(0, 2, 1)
    att = jnp.concatenate([qkv.reshape(ways, depth, 3 * head_cols), dense], -1)
    wsrc = jnp.stack([fc1, fc2, att])
    x_all, g_all, weights, places, segments = gather_plain(x, g, wsrc, places, segments)
    weights = weights.reshape(3, width, cols)
    w1, w2, wa = weights[0], weights[1], weights[2]
    wp, wd = wa[:, : 3 * head_cols], wa[:, 3 * head_cols :]
    x_hat, unused = layer_norm(x_all)
    normed = (x_hat * gain + shift).astype(BF16)
    projected = dot_nn(normed, wp) + qkv_shift.reshape(1, 3 * head_cols)
    mix_grad = dot_nn(g_all, wd).astype(BF16)
    mixture, gq, gk, gv = attention_plain(
        projected[:, :head_cols],
        projected[:, head_cols : 2 * head_cols],
        projected[:, 2 * head_cols :],
        mix_grad,
        places,
        segments,
    )
    proj_grad = jnp.concatenate([gq, gk, gv], 1)

    hidden_pre = dot_nn(normed, w1) + fc1_shift
    hidden, slope = gelu_and_slope(hidden_pre)
    hidden = hidden.astype(BF16)
    hidden_grad = (dot_nn(g_all, w2) * slope).astype(BF16)

    out_part = (dot_nt(mixture, wd) + dot_nt(hidden, w2)).astype(BF16)
    normed_part = dot_nt(proj_grad, wp) + dot_nt(hidden_grad, w1)
    weight_part = jnp.stack(
        [
            dot_tn(normed, hidden_grad).astype(BF16),
            dot_tn(g_all, hidden).astype(BF16),
            jnp.concatenate([dot_tn(normed, proj_grad), dot_tn(g_all, mixture)], 1).astype(BF16),
        ]
    )
    qkv_bias_part = jnp.sum(proj_grad.astype(F32), 0).reshape(3, head_cols)
    fc1_bias_part = jnp.sum(hidden_grad.astype(F32), 0)
    branches, normed_grad, weight_grads = scatter_plain(
        out_part, normed_part.astype(BF16), weight_part.reshape(3, -1, depth, cols)
    )
    place = lambda t, whole, axis: lax.dynamic_update_slice_in_dim(
        jnp.zeros(whole, F32), t, me * t.shape[axis], axis
    )
    small = lax.psum(
        (
            place(qkv_bias_part, (3, head_cols * ways), 1),
            place(fc1_bias_part, (cols * ways,), 0),
            jnp.sum(g.astype(F32), 0),
        ),
        ("dp", "ctx"),
    )
    norms = lax.psum(
        (jnp.sum(normed_part * x_hat, 0), jnp.sum(normed_part, 0)), ("dp", "ctx", "tp")
    )
    grad_fc1 = weight_grads[0].transpose(1, 0, 2).reshape(depth, ways * cols)
    grad_fc2 = weight_grads[1].transpose(0, 2, 1).reshape(ways * cols, depth)
    grad_att = weight_grads[2].reshape(ways, depth, 4, head_cols)
    grad_qkv = grad_att[:, :, :3].transpose(2, 1, 0, 3).reshape(3, depth, ways * head_cols)
    grad_dense = grad_att[:, :, 3].transpose(0, 2, 1).reshape(ways * head_cols, depth)
    weight_grads = (grad_qkv, grad_dense, grad_fc1, grad_fc2)
    gf = g.astype(F32)
    output = (x.astype(F32) + branches + out_bias).astype(BF16)
    own_hat, inv_std = layer_norm(x)
    scaled = normed_grad * gain
    grad_input = gf + inv_std * (
        scaled
        - jnp.mean(scaled, -1, keepdims=True)
        - own_hat * jnp.mean(scaled * own_hat, -1, keepdims=True)
    )
    return output, grad_input.astype(BF16), weight_grads, norms + small


def fast_work(
    x, g, w_qkv, w_dense, w_fc1, w_fc2, places, segments, gain, shift, fc1_shift, qkv_shift, out_bias
):
    ways = lax.axis_size("ctx")
    rows, width = x.shape
    cols, head_cols = w_fc1.shape[1] // ways, w_dense.shape[0] // ways
    line = lambda t: jnp.pad(t.reshape(1, -1), ((0, 0), (0, width - t.size)))
    lines = jnp.concatenate(
        [line(t) for t in (gain, shift, fc1_shift, qkv_shift, out_bias)]
        + [jnp.zeros((3, width), F32)]
    )
    (
        g_all, normed, x_hat, hidden, hidden_grad, out_part, back_mlp, mix_grad, wa,
        q, k, v, mixture, lse, cos, sin, labels, small, unused,
    ) = forward(x, g, w_fc1, w_fc2, w_qkv, w_dense, places[None], segments[None], lines)
    output, grad_input, weight_grads, sums = backward(
        out_part, back_mlp, normed, x_hat, g_all, hidden_grad, hidden,
        q, k, v, mix_grad, mixture, lse, cos, sin, wa, labels, small, x, g, lines,
    )
    gain_sum, shift_sum, out_sum, fc1_sum, qkv_sum = sums
    sums = (
        gain_sum.reshape(width), shift_sum.reshape(width), qkv_sum, fc1_sum.reshape(-1),
        out_sum.reshape(width),
    )
    return output, grad_input, weight_grads, sums


def per_device(
    block_input,
    cotangent,
    segment_ids,
    positions,
    norm_gain,
    norm_bias,
    w_qkv,
    qkv_bias,
    w_dense,
    w_fc1,
    fc1_bias,
    w_fc2,
    out_bias,
):
    ways = lax.axis_size("ctx")
    me = lax.axis_index("ctx")
    x, g = block_input[0], cotangent[0]
    rows, width = x.shape
    cols, head_cols = w_fc1.shape[1] // ways, w_dense.shape[0] // ways

    gain, shift = norm_gain.astype(F32), norm_bias.astype(F32)
    qkv_shift = lax.dynamic_slice_in_dim(qkv_bias, me * head_cols, head_cols, 1).astype(F32)
    fc1_shift = lax.dynamic_slice_in_dim(fc1_bias, me * cols, cols, 0).astype(F32)
    fast = ways == 4 and lax.axis_size("dp") == 4 and rows % 128 == 0
    fast = fast and head_cols == 256 and width == 8 * head_cols and 4 * cols == width * 2
    work = fast_work if fast else plain_work
    output, grad_input, weight_grads, sums = work(
        x, g, w_qkv, w_dense, w_fc1, w_fc2, positions[0], segment_ids[0],
        gain, shift, fc1_shift, qkv_shift, out_bias.astype(F32),
    )
    grad_qkv, grad_dense, grad_fc1, grad_fc2 = weight_grads
    gain_sum, shift_sum, qkv_bias_sum, fc1_bias_sum, out_bias_sum = sums

    return (
        output[None],
        grad_input[None],
        gain_sum,
        shift_sum,
        grad_qkv,
        qkv_bias_sum,
        grad_dense,
        grad_fc1,
        fc1_bias_sum,
        grad_fc2,
        out_bias_sum,
    )


def solution(mesh):
    placed = (
        P("dp", "ctx", None),
        P("dp", "ctx", None),
        P("dp", "ctx"),
        P("dp", "ctx"),
        P(),
        P(),
        P(None, ("dp", "ctx"), "tp"),
        P(None, "tp"),
        P("tp", ("dp", "ctx")),
        P(("dp", "ctx"), "tp"),
        P("tp"),
        P("tp", ("dp", "ctx")),
        P(),
    )
    return jax.shard_map(
        per_device,
        mesh=mesh,
        in_specs=placed,
        out_specs=(
            P("dp", "ctx", None),
            P("dp", "ctx", None),
            P(),
            P(),
            P(None, ("dp", "ctx"), "tp"),
            P(None, "tp"),
            P("tp", ("dp", "ctx")),
            P(("dp", "ctx"), "tp"),
            P("tp"),
            P("tp", ("dp", "ctx")),
            P(),
        ),
        check_vma=False,
    )
```
